512 devices in a mesh: tile: 64 (over z, x, core), lev: 8 (over y).
Axes of the slice: x: 4, y: 8, z: 8, core: 2. Of those that a mesh axis runs over, the one named last changes fastest.
Arguments:
- adj_in: bfloat16 [4, 32, 524288], P(None, 'lev', 'tile'), may hold values from -6 to 6
- helm_coef: float32 [32, 524288], P('lev', 'tile'), may hold values from 0.25 to 4
- geo_coef: float32 [32], P('lev'), may hold values from 0.03 to 0.3
- dest_tile: int32 [4096, 1], P('tile'), may hold values from 0 to 63, as said below
- src_window: int32 [4096], P('tile'), may hold values from 0 to 31
- src_cell: int32 [12, 524288], P(None, 'tile'), may hold values from 0 to 255
- interp_w: bfloat16 [12, 524288], P(None, 'tile'), may hold values from 0.019897461 to 0.5
Outputs:
- adj_out: float32 [4, 32, 524288], P(None, 'lev', 'tile')
The draws below stay inside these ranges and needn't reach their ends.
Inputs may be any that keep to these rules, and one draw needn't show every extreme that they name: `dest_tile`: block b of tile t names t or a tile at most 3 away on either side. Exactly 32 of the 64 blocks of every tile name the tile itself; of the others, at most 16 name any one tile, and in every tile exactly 16 name some one other tile.
All inputs are finite; a program needn't handle non-finite values.
Results may differ from the reference program's by a relative error of at most 0.002.
Values may be sent and summed in bfloat16 or wider, within the bound.
No kernel may reach another device: no remote copies, remote signals or barrier semaphores. Data moves between devices by JAX's collectives and lax.ppermute only.
A program may use at most 64 MiB of HBM per device.

```python
import math
import jax
import jax.numpy as jnp
from jax import lax

F = 4
NLON = 4096
BLK = 128
WIN = 256
STEN = 12
SWEEPS = 4
REACH = 3
LEVELS = 32
CELLS = 8192
NBLK = 64
NCELLS = 524288
NBLOCKS = 4096
N_TILE = 64


def draw_dest_tile(key, part):
    offsets = jnp.concatenate([jnp.arange(-REACH, 0, dtype=jnp.int32), jnp.arange(1, REACH + 1, dtype=jnp.int32)])
    width_count = 2 * REACH
    tiles = jnp.arange(N_TILE, dtype=jnp.int32)
    target = tiles[:, None] + offsets[None, :]
    valid = (target >= 0) & (target < N_TILE)
    key_main = jax.random.fold_in(key, 11)
    key_other = jax.random.fold_in(key, 12)
    key_order = jax.random.fold_in(key, 13)
    column_ids = jnp.arange(width_count, dtype=jnp.int32)
    main_score = jax.random.randint(key_main, (N_TILE, width_count), 0, 1 << 20) * width_count + column_ids[None, :]
    main_score = jnp.where(valid, main_score, -1)
    main_pick = jnp.argmax(main_score, axis=1).astype(jnp.int32)
    other_count = NBLK - NBLK // 2 - NBLK // 4
    other_score = jax.random.randint(key_other, (N_TILE, other_count, width_count), 0, 1 << 20) * width_count + column_ids[None, None, :]
    allowed = valid[:, None, :] & (column_ids[None, None, :] != main_pick[:, None, None])
    other_score = jnp.where(allowed, other_score, -1)
    other_pick = jnp.argmax(other_score, axis=2).astype(jnp.int32)
    home_part = jnp.zeros((N_TILE, NBLK // 2), jnp.int32)
    main_part = jnp.broadcast_to(offsets[main_pick][:, None], (N_TILE, NBLK // 4))
    other_part = offsets[other_pick]
    offset_of = jnp.concatenate([home_part, main_part, other_part], axis=1)
    order_keys = jax.random.split(key_order, N_TILE)
    orders = jax.vmap(lambda one_key: jax.random.permutation(one_key, NBLK))(order_keys)
    shuffled = jnp.take_along_axis(offset_of, orders.astype(jnp.int32), axis=1)
    return (tiles[:, None] + shuffled).reshape(N_TILE * NBLK, 1).astype(jnp.int32)


def plant(drawn, rng, least, largest):
    shape = drawn.shape
    index_at = [jax.random.randint(jax.random.fold_in(rng, axis), (), 0, shape[axis]) for axis in range(len(shape))]
    drawn = drawn.at[tuple(index_at)].set(least)
    longest = shape.index(max(shape))
    index_at[longest] = (index_at[longest] + 1) % shape[longest]
    return drawn.at[tuple(index_at)].set(largest)


def block_scale(key, dims, cuts, smallest, high):
    def one(dim, parts):
        draws = jax.random.uniform(jax.random.fold_in(jax.random.fold_in(key, 6), dim), (parts,), jnp.float32, smallest / len(cuts), high / len(cuts))
        return jnp.repeat(jnp.exp(draws), dims[dim] // parts).reshape((-1,) + (1,) * (len(dims) - dim - 1))

    factor_of = one(*cuts[0])
    for cut in cuts[1:]:
        factor_of = factor_of * one(*cut)
    return factor_of


def noise(own_key, dims, spread, bound, cuts=(), kind=jnp.bfloat16):
    result = jax.random.normal(own_key, dims, jnp.float32) * spread
    if len(cuts) > 0:
        result = block_scale(own_key, dims, cuts, -0.22, 0.18) * result
    return jnp.clip(result, min=-bound, max=bound).astype(kind)


def setup_inputs(seed: int = 0) -> dict:
    seeds = jax.random.split(jax.random.key(seed), 8)
    return {
        "adj_in": noise(seeds[0], (F, LEVELS, NCELLS), 1.0, 6.0, ((1, 8), (2, 64))),
        "helm_coef": jnp.clip(jnp.exp(math.log(4.0) - 2.7725887 * jax.random.uniform(seeds[1], (LEVELS, NCELLS), jnp.float32) ** block_scale(seeds[1], (LEVELS, NCELLS), ((0, 8), (1, 64)), -0.2, 0.2)), 0.25, 4.0),
        "geo_coef": jnp.clip(jnp.exp(math.log(0.3) - 2.3025852 * jax.random.uniform(seeds[2], (LEVELS,), jnp.float32) ** block_scale(seeds[2], (LEVELS,), ((0, 8),), -0.2, 0.2)), 0.03, 0.3),
        "dest_tile": draw_dest_tile(jax.random.fold_in(seeds[7], 71), 0),
        "src_window": plant(jax.random.randint(seeds[4], (NBLOCKS,), 0, CELLS // WIN), jax.random.fold_in(seeds[4], 1), 0, (CELLS // WIN) - 1).astype(jnp.int32),
        "src_cell": plant(jax.random.randint(seeds[5], (STEN, NCELLS), 0, WIN), jax.random.fold_in(seeds[5], 1), 0, WIN - 1).astype(jnp.int32),
        "interp_w": jnp.clip(0.019897461 + 0.48010254 * jax.random.uniform(seeds[6], (STEN, NCELLS), jnp.float32) ** block_scale(seeds[6], (STEN, NCELLS), ((1, 64),), -0.2, 0.2), 0.019897461, 0.5).astype(jnp.bfloat16),
    }


def reference(adj_in, helm_coef, geo_coef, dest_tile, src_window, src_cell, interp_w):
    field_count, level_count, cell_count = adj_in.shape
    row_total = cell_count // NLON
    right_side = adj_in[0].astype(jnp.float32)
    diagonal = 1.0 + 4.0 * helm_coef
    solved = right_side / diagonal
    for sweep in range(SWEEPS):
        shifted = (helm_coef * solved).reshape(level_count, row_total, NLON)
        padded = jnp.pad(shifted, ((0, 0), (1, 1), (0, 0)))
        summed = padded[:, :-2] + padded[:, 2:] + jnp.roll(shifted, 1, axis=2) + jnp.roll(shifted, -1, axis=2)
        solved = (right_side + summed.reshape(level_count, cell_count)) / diagonal
    level_sums = jnp.cumsum(solved, axis=0)
    outgoing = jnp.concatenate([solved.astype(jnp.bfloat16)[None], adj_in[1:]], axis=0)
    cell_ids = jnp.arange(cell_count, dtype=jnp.int32)
    block_of = cell_ids // BLK
    base_cell = dest_tile[:, 0].astype(jnp.int32)[block_of] * CELLS + src_window.astype(jnp.int32)[block_of] * WIN
    targets = base_cell[None, :] + src_cell.astype(jnp.int32)
    weights = interp_w.astype(jnp.float32)

    def one_field(values):
        scaled = values.astype(jnp.float32)
        accum = jnp.zeros((level_count, cell_count), jnp.float32)
        for point in range(STEN):
            accum = accum.at[:, targets[point]].add(scaled * weights[point][None, :])
        return accum

    transported = lax.map(one_field, outgoing)
    return transported.at[2].add(geo_coef[:, None] * level_sums)
```

```python
import jax
import jax.numpy as jnp
from jax import lax
from jax.experimental import pallas as pl
from jax.experimental.pallas import tpu as pltpu
from jax.sharding import PartitionSpec as P

NLON = 4096
BLK = 128
WIN = 256
SWEEPS = 4
REACH = 3
HOME = 32
OFFCAP = 16

F32 = jnp.float32
BF16 = jnp.bfloat16
STEN = 12
NBLK = 64
CELLS = 8192
NWIN = CELLS // WIN
OFFSETS = (1, -1, 2, -2, 3, -3)
SLOTS = HOME + OFFCAP * len(OFFSETS)
BASES = {0: 0, **{by: HOME + OFFCAP * i for i, by in enumerate(OFFSETS)}}
HALO = NLON // BLK
ROUTE = 2 * STEN + 1
ENTRIES = 2 * SLOTS
UNROLL = 4
REMAINDER = 1e-6


def vmem():
    return pl.BlockSpec(memory_space=pltpu.VMEM)


def smem():
    return pl.BlockSpec(memory_space=pltpu.SMEM)


def hbm():
    return pl.BlockSpec(memory_space=pl.ANY)


def lanes(i):
    return slice(i * BLK, (i + 1) * BLK)


def call(kernel, outs, ins, scratch, cost, limit):
    return pl.pallas_call(
        kernel,
        out_shape=[jax.ShapeDtypeStruct(shape, dtype) for shape, dtype, _ in outs],
        out_specs=[spec for _, _, spec in outs],
        in_specs=ins,
        scratch_shapes=scratch,
        compiler_params=pltpu.CompilerParams(vmem_limit_bytes=limit << 20),
        cost_estimate=pl.CostEstimate(flops=cost * 1000000, bytes_accessed=cost * 3000000, transcendentals=0),
    )


def pack_kernel(me, dest, win, adj, helm, cell, weight, slots, a_home, b_home, *rest):
    parcels, (count, a_all, b_all) = rest[: len(OFFSETS)], rest[len(OFFSETS) :]
    for by in range(-REACH, REACH + 1):
        count[by + REACH] = BASES[by]
    a_all[...] = jnp.zeros_like(a_all)
    b_all[...] = jnp.zeros_like(b_all)
    for b in range(NBLK):
        route = dest[b] - me[0] + REACH
        slot = count[route]
        count[route] = slot + 1
        slots[b] = slot
        a_all[pl.ds(slot, STEN, stride=SLOTS), :] = weight[:, lanes(b)].astype(F32)
        a_all[pl.ds(STEN * SLOTS + slot, STEN, stride=SLOTS), :] = cell[:, lanes(b)].astype(F32)
        a_all[pl.ds(2 * STEN * SLOTS + slot, 1), :] = jnp.full((1, BLK), win[b] + 1, jnp.int32).astype(F32)
        b_all[slot] = jnp.concatenate([adj[f, :, lanes(b)].astype(F32) for f in range(4)], axis=0).astype(BF16)
    for r in range(ROUTE):
        a_home[r] = a_all[r * SLOTS : r * SLOTS + HOME, :].astype(BF16)
    b_home[...] = b_all[:HOME]
    for by, parcel in zip(OFFSETS, parcels):
        at = HALO if abs(by) < 3 else 0
        base = BASES[by]
        for r in range(ROUTE):
            parcel[at + r] = a_all[r * SLOTS + base : r * SLOTS + base + OFFCAP, :].astype(BF16)
        parcel[at + ROUTE : at + ROUTE + OFFCAP] = b_all[base : base + OFFCAP]
    for i in range(HALO):
        piece = jnp.concatenate(
            [
                adj[0, :, lanes(i)].astype(F32),
                adj[0, :, lanes(HALO + i)].astype(F32),
                helm[:, lanes(i)],
                helm[:, lanes(HALO + i)],
            ],
            axis=0,
        ).astype(BF16)
        for by, parcel in zip(OFFSETS, parcels):
            if abs(by) < 3:
                parcel[i] = piece


def solve_kernel(slots, adj, helm, n2, n1, s1, s2, local, totals, f_home, *rest):
    f_out, (halo, f_all, t_all, sems) = rest[: len(OFFSETS)], rest[len(OFFSETS) :]
    copies = []
    for i, parcel in enumerate((n2, n1, s1, s2)):
        copy = pltpu.make_async_copy(parcel.at[pl.ds(0, HALO)], halo.at[i], sems.at[i])
        copy.start()
        copies.append(copy)
    f_all[...] = jnp.zeros_like(f_all)
    for copy in copies:
        copy.wait()
    rhs, coef = [], []
    for band in range(5):
        if band == 2:
            rhs.append(jnp.concatenate([adj[0, :, :NLON].astype(F32), adj[0, :, NLON:].astype(F32)], axis=0))
            coef.append(jnp.concatenate([helm[:, :NLON], helm[:, NLON:]], axis=0))
        else:
            at = band - (band > 2)
            tiles = [halo[at, i].astype(F32) for i in range(HALO)]
            rhs.append(jnp.concatenate([t[:8] for t in tiles], axis=1))
            coef.append(jnp.concatenate([t[8:] for t in tiles], axis=1))
    scale = [1.0 / (1.0 + 4.0 * c) for c in coef]
    solved = [r * s for r, s in zip(rhs, scale)]
    upper = lax.broadcasted_iota(jnp.int32, (8, NLON), 0) < 4
    for wanted in ((0, 1, 2, 3, 4), (1, 2, 3), (1, 2, 3), (2,)):
        shifted = [c * s for c, s in zip(coef, solved)]
        turned = [pltpu.roll(p, 4, 0) for p in shifted]
        fresh = list(solved)
        for band in wanted:
            p = shifted[band]
            north = turned[max(band - 1, 0)]
            south = turned[min(band + 1, 4)]
            total = turned[band] + jnp.where(upper, north, south)
            total = total + pltpu.roll(p, 1, 1) + pltpu.roll(p, NLON - 1, 1)
            fresh[band] = (rhs[band] + total) * scale[band]
        solved = fresh
    mine = solved[2]
    for r in range(2):
        sums = mine[4 * r : 4 * r + 1]
        local[4 * r : 4 * r + 1, :] = sums
        for level in range(1, 4):
            sums = sums + mine[4 * r + level : 4 * r + level + 1]
            local[4 * r + level : 4 * r + level + 1, :] = sums
        for i in range(HALO):
            t_all[HALO * r + i : HALO * r + i + 1, :] = sums[:, lanes(i)]
            f_all[pl.ds(slots[HALO * r + i] * 4, 4), :] = mine[4 * r : 4 * r + 4, lanes(i)]
    totals_here = t_all[...].astype(BF16)
    for i in range(totals.shape[0]):
        totals[i] = totals_here
    f_home[...] = f_all[: HOME * 4].astype(BF16)
    for by, out in zip(OFFSETS, f_out):
        out[...] = f_all[BASES[by] * 4 : (BASES[by] + OFFCAP) * 4].astype(BF16)


def matrix_kernel(a_home, *rest):
    parcels = rest[: len(OFFSETS)]
    mats, entry_slot, entry_win, entry_count, a_in, cells, merged, meta, meta_s, sems, meta_sem = rest[len(OFFSETS) :]
    copies = []
    for i, (by, parcel) in enumerate(zip(OFFSETS, parcels)):
        at = HALO if abs(by) < 3 else 0
        copy = pltpu.make_async_copy(parcel.at[pl.ds(at, ROUTE)], a_in.at[i], sems.at[i])
        copy.start()
        copies.append(copy)

    lane = lax.broadcasted_iota(jnp.int32, (8, BLK), 1)
    row = lax.broadcasted_iota(jnp.int32, (8, BLK), 0)

    def merge(base, load):
        w = [load(k) for k in range(STEN)]
        c = [load(STEN + k) for k in range(STEN)]
        total = list(w)
        for k in range(STEN):
            for m in range(k):
                same = c[k] == c[m]
                total[k] = total[k] + jnp.where(same, w[m], 0.0)
                total[m] = total[m] + jnp.where(same, w[k], 0.0)
        lost = jnp.zeros((8, BLK), F32)
        held = jnp.zeros((8, BLK), F32)
        for k in range(STEN):
            high = total[k].astype(BF16).astype(F32)
            low = total[k] - high
            cells[k, base : base + 8, :] = c[k]
            merged[k, base : base + 8, :] = high
            merged[k, SLOTS + base : SLOTS + base + 8, :] = low
            lost = lost + low * low
            held = held + w[k] * w[k]
        more = jnp.sum(lost, axis=1, keepdims=True) > REMAINDER * jnp.sum(held, axis=1, keepdims=True)
        mark = load(2 * STEN)
        mark = jnp.where(mark > 0.0, mark + jnp.where(more, 64.0, 0.0), 0.0)
        return jnp.where(lane == row + base, mark, 0.0)

    marks = jnp.zeros((8, BLK), F32)
    for half in range(0, HOME, 16):
        pair = [a_home[r, half : half + 16, :].astype(F32) for r in range(ROUTE)]
        for part in (0, 8):
            marks = marks + merge(half + part, lambda r: pair[r][part : part + 8])
    for i, by in enumerate(OFFSETS):
        copies[i].wait()
        pair = [a_in[i, r].astype(F32) for r in range(ROUTE)]
        for part in (0, 8):
            marks = marks + merge(BASES[by] + part, lambda r: pair[r][part : part + 8])
    meta[...] = jnp.sum(marks, axis=0, keepdims=True).astype(jnp.int32)
    copy = pltpu.make_async_copy(meta, meta_s, meta_sem)
    copy.start()
    copy.wait()

    def enlist(i, n):
        for j in range(8):
            slot = i * 8 + j
            mark = meta_s[0, slot]
            window = (mark & 63) - 1
            entry_slot[n] = slot
            entry_win[n] = window
            n = n + (mark > 0).astype(jnp.int32)
            entry_slot[n] = slot + SLOTS
            entry_win[n] = window
            n = n + (mark >= 64).astype(jnp.int32)
        return n

    n = lax.fori_loop(0, SLOTS // 8, enlist, jnp.int32(0))
    entry_count[0] = n
    for j in range(UNROLL):
        entry_slot[n + j] = 0
        entry_win[n + j] = NWIN

    iota = lax.broadcasted_iota(jnp.int32, (16, BLK), 0).astype(F32)

    def build(i, carry):
        entry = entry_slot[i]
        slot = lax.rem(entry, SLOTS)
        c = [jnp.broadcast_to(cells[k, pl.ds(slot, 1), :], (16, BLK)).astype(BF16) for k in range(STEN)]
        w = [jnp.broadcast_to(merged[k, pl.ds(entry, 1), :], (16, BLK)).astype(BF16) for k in range(STEN)]
        for j in range(WIN // 16):
            here = (iota + 16.0 * j).astype(BF16)
            m = jnp.zeros((16, BLK), BF16)
            for k in range(STEN):
                m = jnp.where(c[k] == here, w[k], m)
            mats[i, 16 * j : 16 * j + 16, :] = m
        return carry

    lax.fori_loop(0, n, build, 0)


def spread_kernel(entry_slot, entry_win, entry_count, lev, geo, mats, b_home, f_home, local, above, *rest):
    parcels, f_in = rest[: len(OFFSETS)], rest[len(OFFSETS) : 2 * len(OFFSETS)]
    out, values, firsts, total, sems = rest[2 * len(OFFSETS) :]
    copies = []
    for i, (by, parcel) in enumerate(zip(OFFSETS, parcels)):
        at = (HALO if abs(by) < 3 else 0) + ROUTE
        copy = pltpu.make_async_copy(parcel.at[pl.ds(at, OFFCAP)], values.at[pl.ds(BASES[by], OFFCAP)], sems.at[i])
        copy.start()
        copies.append(copy)
    values[:HOME] = b_home[...]
    total[...] = jnp.zeros_like(total)
    firsts[: HOME * 4, :] = f_home[...].astype(F32)
    for by, part in zip(OFFSETS, f_in):
        firsts[BASES[by] * 4 : (BASES[by] + OFFCAP) * 4, :] = part[...].astype(F32)
    firsts[SLOTS * 4 :, :] = jnp.zeros((8, BLK), F32)
    for copy in copies:
        copy.wait()
    first_rows = lax.broadcasted_iota(jnp.int32, (8, BLK), 0) < 4

    def step(i, carry):
        parts = []
        for j in range(UNROLL):
            at = i * UNROLL + j
            slot = lax.rem(entry_slot[at], SLOTS)
            tile = values[slot].astype(F32)
            head = jnp.where(first_rows, firsts[pl.ds(slot * 4, 8), :], tile[:8])
            left = jnp.concatenate([head, tile[8:]], axis=0).astype(BF16)
            parts.append(
                lax.dot_general(left, mats[at], (((1,), (1,)), ((), ())), preferred_element_type=F32)
            )
        for j in range(UNROLL):
            start = pl.multiple_of(entry_win[i * UNROLL + j] * WIN, WIN)
            total[:, pl.ds(start, WIN)] += parts[j]
        return carry

    lax.fori_loop(0, (entry_count[0] + UNROLL - 1) // UNROLL, step, 0)

    sums = jnp.zeros((NBLK, BLK), F32)
    for peer in range(above.shape[0]):
        sums = sums + jnp.where(peer < lev[0], above[peer].astype(F32), 0.0)
    level = lax.broadcasted_iota(jnp.int32, (4, BLK), 0)
    factor = jnp.zeros((4, BLK), F32)
    for l in range(4):
        factor = jnp.where(level == l, geo[l], factor)
    for f in (0, 1, 3):
        out[f] = total[4 * f : 4 * f + 4, :CELLS]
    for b in range(NBLK):
        r = b // HALO
        term = factor * (local[4 * r : 4 * r + 4, lanes(b % HALO)] + sums[b : b + 1])
        out[2, :, lanes(b)] = total[8:12, lanes(b)] + term


def moved(parcel, by):
    peers = lax.axis_size("tile")
    return lax.ppermute(parcel, "tile", [(i, i + by) for i in range(peers) if 0 <= i + by < peers])


def body(adj_in, helm_coef, geo_coef, dest_tile, src_window, src_cell, interp_w):
    me = lax.axis_index("tile").astype(jnp.int32)[None]
    lev = lax.axis_index("lev").astype(jnp.int32)[None]
    peers = lax.axis_size("lev")
    directions = len(OFFSETS)

    def parcel_of(by):
        return (ROUTE + OFFCAP + (HALO if abs(by) < 3 else 0), 16, BLK)

    slots, a_home, b_home, *parcels = call(
        pack_kernel,
        [
            ((NBLK,), jnp.int32, smem()),
            ((ROUTE, HOME, BLK), BF16, vmem()),
            ((HOME, 16, BLK), BF16, vmem()),
        ]
        + [(parcel_of(by), BF16, vmem()) for by in OFFSETS],
        [smem()] * 3 + [vmem()] * 4,
        [
            pltpu.SMEM((2 * REACH + 1,), jnp.int32),
            pltpu.VMEM((ROUTE * SLOTS, BLK), F32),
            pltpu.VMEM((SLOTS, 16, BLK), BF16),
        ],
        1,
        32,
    )(me, dest_tile[:, 0], src_window, adj_in, helm_coef, src_cell, interp_w)
    arrived = [moved(parcel, by) for by, parcel in zip(OFFSETS, parcels)]
    arrived_from = dict(zip(OFFSETS, arrived))

    local, totals, f_home, *f_out = call(
        solve_kernel,
        [
            ((8, NLON), F32, vmem()),
            ((peers, NBLK, BLK), BF16, vmem()),
            ((HOME * 4, BLK), BF16, vmem()),
        ]
        + [((OFFCAP * 4, BLK), BF16, vmem())] * directions,
        [smem()] + [vmem()] * 2 + [hbm()] * 4,
        [
            pltpu.VMEM((4, HALO, 16, BLK), BF16),
            pltpu.VMEM((SLOTS * 4, BLK), F32),
            pltpu.VMEM((NBLK, BLK), F32),
            pltpu.SemaphoreType.DMA((4,)),
        ],
        2,
        32,
    )(slots, adj_in, helm_coef, *(arrived_from[by] for by in (2, 1, -1, -2)))
    above = lax.all_to_all(totals, "lev", 0, 0)
    f_in = [moved(part, by) for by, part in zip(OFFSETS, f_out)]

    mats, entry_slot, entry_win, entry_count = call(
        matrix_kernel,
        [
            ((ENTRIES, WIN, BLK), BF16, vmem()),
            ((ENTRIES + 8,), jnp.int32, smem()),
            ((ENTRIES + 8,), jnp.int32, smem()),
            ((1,), jnp.int32, smem()),
        ],
        [vmem()] + [hbm()] * directions,
        [
            pltpu.VMEM((directions, ROUTE, 16, BLK), BF16),
            pltpu.VMEM((STEN, SLOTS, BLK), F32),
            pltpu.VMEM((STEN, 2 * SLOTS, BLK), F32),
            pltpu.VMEM((1, BLK), jnp.int32),
            pltpu.SMEM((1, BLK), jnp.int32),
            pltpu.SemaphoreType.DMA((directions,)),
            pltpu.SemaphoreType.DMA,
        ],
        8,
        40,
    )(a_home, *arrived)

    return call(
        spread_kernel,
        [((4, 4, CELLS), F32, vmem())],
        [smem()] * 5 + [vmem()] * 5 + [hbm()] * directions + [vmem()] * directions,
        [
            pltpu.VMEM((SLOTS, 16, BLK), BF16),
            pltpu.VMEM((SLOTS * 4 + 8, BLK), F32),
            pltpu.VMEM((16, CELLS + WIN), F32),
            pltpu.SemaphoreType.DMA((directions,)),
        ],
        5,
        40,
    )(entry_slot, entry_win, entry_count, lev, geo_coef, mats, b_home, f_home, local, above, *arrived, *f_in)[0]


def solution(mesh):
    placed = (
        P(None, "lev", "tile"),
        P("lev", "tile"),
        P("lev"),
        P("tile", None),
        P("tile"),
        P(None, "tile"),
        P(None, "tile"),
    )
    return jax.shard_map(
        body, mesh=mesh, in_specs=placed, out_specs=P(None, "lev", "tile"), check_vma=False
    )
```

```python
import jax
import jax.numpy as jnp
from jax import lax
from jax.experimental import pallas as pl
from jax.experimental.pallas import tpu as pltpu
from jax.sharding import PartitionSpec as P

NLON = 4096
BLK = 128
WIN = 256
SWEEPS = 4
REACH = 3
HOME = 32
OFFCAP = 16

F32 = jnp.float32
BF16 = jnp.bfloat16
STEN = 12
NBLK = 64
CELLS = 8192
NWIN = CELLS // WIN
OFFSETS = (-3, -2, -1, 1, 2, 3)
GROUPS = len(OFFSETS)
SLOTS = HOME + OFFCAP * GROUPS
HALO = NLON // BLK
ROUTE = 2 * STEN + 1
LOAD = ROUTE + OFFCAP
RELAY = HALO + LOAD
LOWS = HALO // 2
OWN = HALO + LOWS + 1 + LOAD
EARLY = HOME + 3 * OFFCAP
LATE = 3 * OFFCAP
PACK = 4
RING = 4
REMAINDER = 1e-6


def vmem():
    return pl.BlockSpec(memory_space=pltpu.VMEM)


def smem():
    return pl.BlockSpec(memory_space=pltpu.SMEM)


def hbm():
    return pl.BlockSpec(memory_space=pl.ANY)


def lanes(i):
    return slice(i * BLK, (i + 1) * BLK)


def base_of(by):
    return 0 if by == 0 else HOME + OFFCAP * OFFSETS.index(by)


def either(core, first, second):
    return pl.multiple_of(jnp.where(core == 0, base_of(first), base_of(second)), OFFCAP)


def launch(copies):
    copies = [pltpu.make_async_copy(*copy) for copy in copies]
    for copy in copies:
        copy.start()
    return copies


def finish(copies):
    for copy in copies:
        copy.wait()


def call(kernel, outs, ins, scratch, cost, limit):
    return pl.pallas_call(
        kernel,
        out_shape=[jax.ShapeDtypeStruct(shape, dtype) for shape, dtype, _ in outs],
        out_specs=[spec for _, _, spec in outs],
        in_specs=ins,
        scratch_shapes=scratch,
        compiler_params=pltpu.CompilerParams(vmem_limit_bytes=limit << 20),
        cost_estimate=pl.CostEstimate(flops=cost * 1000000, bytes_accessed=cost * 3000000, transcendentals=0),
    )


def pack_kernel(
    me, dest_in, win_in, adj_in, helm_in, cell_in, weight_in,
    slots, a_home, b_home, own, plus, minus, cross,
    dest, win, adj, helm, cell, weight, count, a_all, b_all, sems,
):
    pairs = ((dest_in, dest), (win_in, win), (adj_in, adj), (helm_in, helm), (cell_in, cell), (weight_in, weight))
    copies = launch([(a, b, sems.at[i]) for i, (a, b) in enumerate(pairs)])
    core = lax.rem(me[0], 2)
    for by in range(-REACH, REACH + 1):
        count[by + REACH] = base_of(by)
    a_all[...] = jnp.zeros_like(a_all)
    b_all[...] = jnp.zeros_like(b_all)
    finish(copies)
    lane = lax.broadcasted_iota(jnp.int32, (16, BLK), 1)
    table = jnp.zeros((16, BLK), jnp.int32)
    for b in range(NBLK):
        route = dest[b] - me[0] + REACH
        slot = count[route]
        count[route] = slot + 1
        slots[b] = slot
        table = jnp.where(lane == b, slot, table)
        a_all[pl.ds(slot, STEN, stride=SLOTS), :] = weight[:, lanes(b)].astype(F32)
        a_all[pl.ds(STEN * SLOTS + slot, STEN, stride=SLOTS), :] = cell[:, lanes(b)].astype(F32)
        a_all[pl.ds(2 * STEN * SLOTS + slot, 1), :] = jnp.full((1, BLK), win[b] + 1, jnp.int32).astype(F32)
        b_all[slot] = jnp.concatenate([adj[f, :, lanes(b)].astype(F32) for f in range(4)], axis=0).astype(BF16)
    for r in range(ROUTE):
        a_home[r] = a_all[r * SLOTS : r * SLOTS + HOME, :].astype(BF16)
    b_home[...] = b_all[:HOME]
    loads = (
        (own, HALO + LOWS + 1, either(core, 1, -1)),
        (plus, HALO, either(core, 3, 1)),
        (plus, RELAY, either(core, 2, 2)),
        (minus, HALO, either(core, -1, -3)),
        (minus, RELAY, either(core, -2, -2)),
        (cross, 0, either(core, -3, 3)),
    )
    for parcel, at, base in loads:
        for r in range(ROUTE):
            parcel[at + r] = a_all[pl.ds(r * SLOTS + base, OFFCAP), :].astype(BF16)
        parcel[at + ROUTE : at + LOAD] = b_all[pl.ds(base, OFFCAP)]
    rest = []
    for i in range(HALO):
        coef = jnp.concatenate([helm[:, lanes(i)], helm[:, lanes(HALO + i)]], axis=0)
        rest.append(coef - coef.astype(BF16).astype(F32))
        first = [adj[0, :, lanes(i)].astype(F32), adj[0, :, lanes(HALO + i)].astype(F32)]
        piece = jnp.concatenate(first + [coef], axis=0).astype(BF16)
        for parcel in (own, plus, minus):
            parcel[i] = piece
    for i in range(LOWS):
        own[HALO + i] = jnp.concatenate(rest[2 * i : 2 * i + 2], axis=0).astype(BF16)
    own[HALO + LOWS] = table.astype(F32).astype(BF16)


def relay_kernel(own, plus, minus, out, sems):
    finish(
        launch(
            [
                (own, out.at[pl.ds(0, OWN)], sems.at[0]),
                (plus.at[pl.ds(0, RELAY)], out.at[pl.ds(OWN, RELAY)], sems.at[1]),
                (minus.at[pl.ds(0, RELAY)], out.at[pl.ds(OWN + RELAY, RELAY)], sems.at[2]),
            ]
        )
    )


def solve_kernel(
    me, slots, adj_in, helm_in, own, plus, minus, mate,
    local, totals, f_home, f_mate, f_plus, f_minus, f_cross,
    adj, helm, halo, lows, rhs, coef, result, table, table_s, mine_all, mate_all, t_all, sems, table_sem,
):
    core = lax.rem(me[0], 2)
    tables = launch([(mate.at[pl.ds(HALO, LOWS + 1)], lows, sems.at[8])])
    pairs = (
        (adj_in.at[0], adj),
        (helm_in, helm),
        (plus.at[pl.ds(0, HALO)], halo.at[core]),
        (mate.at[pl.ds(OWN, HALO)], halo.at[1 - core]),
        (own.at[pl.ds(0, HALO)], halo.at[2 + core]),
        (mate.at[pl.ds(0, HALO)], halo.at[3 - core]),
        (minus.at[pl.ds(0, HALO)], halo.at[4 + core]),
        (mate.at[pl.ds(OWN + RELAY, HALO)], halo.at[5 - core]),
    )
    copies = launch([(a, b, sems.at[i]) for i, (a, b) in enumerate(pairs)])
    mine_all[...] = jnp.zeros_like(mine_all)
    mate_all[...] = jnp.zeros_like(mate_all)
    finish(tables)
    table[...] = lows[LOWS].astype(F32)[:1].astype(jnp.int32)
    tables = launch([(table, table_s, table_sem)])
    finish(copies)
    for band in range(6):
        for i in range(HALO):
            tile = halo[band, i].astype(F32)
            rhs[band, :, lanes(i)] = tile[:8]
            coef[band, :, lanes(i)] = tile[8:]
    for i in range(LOWS):
        tile = lows[i].astype(F32)
        coef[3 - core, :, lanes(2 * i)] += tile[:8]
        coef[3 - core, :, lanes(2 * i + 1)] += tile[8:]
    coef[2 + core] = jnp.concatenate([helm[:, :NLON], helm[:, NLON:]], axis=0)
    right = [rhs[band] for band in range(6)]
    factor = [coef[band] for band in range(6)]
    scale = [1.0 / (1.0 + 4.0 * c) for c in factor]
    solved = [r * s for r, s in zip(right, scale)]
    upper = lax.broadcasted_iota(jnp.int32, (8, NLON), 0) < 4
    for wanted in ((0, 1, 2, 3, 4, 5), (1, 2, 3, 4), (1, 2, 3, 4), (2, 3)):
        shifted = [c * s for c, s in zip(factor, solved)]
        turned = [pltpu.roll(p, 4, 0) for p in shifted]
        fresh = list(solved)
        for band in wanted:
            p = shifted[band]
            north = turned[max(band - 1, 0)]
            south = turned[min(band + 1, 5)]
            total = turned[band] + jnp.where(upper, north, south)
            total = total + pltpu.roll(p, 1, 1) + pltpu.roll(p, NLON - 1, 1)
            fresh[band] = (right[band] + total) * scale[band]
        solved = fresh
    result[0] = solved[2]
    result[1] = solved[3]
    mine = result[core]
    other = result[1 - core]
    finish(tables)
    for r in range(2):
        sums = mine[4 * r : 4 * r + 1]
        local[4 * r : 4 * r + 1, :] = sums
        for level in range(1, 4):
            sums = sums + mine[4 * r + level : 4 * r + level + 1]
            local[4 * r + level : 4 * r + level + 1, :] = sums
        for i in range(HALO):
            b = HALO * r + i
            t_all[b : b + 1, :] = sums[:, lanes(i)]
            mine_all[pl.ds(slots[b] * 4, 4), :] = mine[4 * r : 4 * r + 4, lanes(i)]
            mate_all[pl.ds(table_s[0, b] * 4, 4), :] = other[4 * r : 4 * r + 4, lanes(i)]
    totals_here = t_all[...].astype(BF16)
    for i in range(totals.shape[0]):
        totals[i] = totals_here

    def part(source, first, second):
        return source[pl.ds(either(core, first, second) * 4, OFFCAP * 4), :].astype(BF16)

    f_home[...] = mine_all[: HOME * 4].astype(BF16)
    f_mate[...] = part(mate_all, -1, 1)
    f_plus[: OFFCAP * 4] = part(mine_all, 2, 2)
    f_plus[OFFCAP * 4 :] = part(mate_all, 1, 3)
    f_minus[: OFFCAP * 4] = part(mine_all, -2, -2)
    f_minus[OFFCAP * 4 :] = part(mate_all, -3, -1)
    f_cross[...] = part(mine_all, -3, 3)


def matrix_kernel(count, home, offsets, *refs):
    a_home = refs[0] if home else None
    parcels, refs = refs[home : home + len(offsets)], refs[home + len(offsets) :]
    mats, entry_slot, entry_win, entry_count, a_in, cells, merged, ring, meta, meta_s, sems, ring_sems, meta_sem = refs
    copies = launch([(p.at[pl.ds(at, ROUTE)], a_in.at[i], sems.at[i]) for i, (p, at) in enumerate(zip(parcels, offsets))])

    lane = lax.broadcasted_iota(jnp.int32, (8, BLK), 1)
    row = lax.broadcasted_iota(jnp.int32, (8, BLK), 0)

    def merge(base, load):
        w = [load(k) for k in range(STEN)]
        c = [load(STEN + k) for k in range(STEN)]
        total = list(w)
        for k in range(STEN):
            for m in range(k):
                same = c[k] == c[m]
                total[k] = total[k] + jnp.where(same, w[m], 0.0)
                total[m] = total[m] + jnp.where(same, w[k], 0.0)
        lost = jnp.zeros((8, BLK), F32)
        held = jnp.zeros((8, BLK), F32)
        for k in range(STEN):
            high = total[k].astype(BF16).astype(F32)
            low = total[k] - high
            cells[k, base : base + 8, :] = c[k]
            merged[k, base : base + 8, :] = high
            merged[k, count + base : count + base + 8, :] = low
            lost = lost + low * low
            held = held + w[k] * w[k]
        more = jnp.sum(lost, axis=1, keepdims=True) > REMAINDER * jnp.sum(held, axis=1, keepdims=True)
        mark = load(2 * STEN)
        mark = jnp.where(mark > 0.0, mark + jnp.where(more, 64.0, 0.0), 0.0)
        return jnp.where(lane == row + base, mark, 0.0)

    marks = jnp.zeros((8, BLK), F32)
    for at in range(0, HOME if home else 0, 16):
        pair = [a_home[r, at : at + 16, :].astype(F32) for r in range(ROUTE)]
        for half in (0, 8):
            marks = marks + merge(at + half, lambda r: pair[r][half : half + 8])
    for i in range(len(offsets)):
        copies[i].wait()
        pair = [a_in[i, r].astype(F32) for r in range(ROUTE)]
        at = (HOME if home else 0) + OFFCAP * i
        for half in (0, 8):
            marks = marks + merge(at + half, lambda r: pair[r][half : half + 8])
    meta[...] = jnp.sum(marks, axis=0, keepdims=True).astype(jnp.int32)
    finish(launch([(meta, meta_s, meta_sem)]))

    def enlist(i, n):
        for j in range(8):
            slot = i * 8 + j
            mark = meta_s[0, slot]
            window = (mark & 63) - 1
            entry_slot[n] = slot
            entry_win[n] = window
            n = n + (mark > 0).astype(jnp.int32)
            entry_slot[n] = slot + count
            entry_win[n] = window
            n = n + (mark >= 64).astype(jnp.int32)
        return n

    n = lax.fori_loop(0, count // 8, enlist, jnp.int32(0))
    entry_count[0] = n
    for j in range(PACK):
        entry_slot[n + j] = 0
        entry_win[n + j] = NWIN

    iota = lax.broadcasted_iota(jnp.int32, (16, BLK), 0).astype(F32)

    def stored(group):
        at = lax.rem(group, 2)
        return pltpu.make_async_copy(ring.at[at], mats.at[pl.ds(group * PACK, PACK)], ring_sems.at[at])

    def build(group, carry):
        @pl.when(group >= 2)
        def _():
            stored(group - 2).wait()

        for j in range(PACK):
            entry = entry_slot[group * PACK + j]
            slot = lax.rem(entry, count)
            c = [jnp.broadcast_to(cells[k, pl.ds(slot, 1), :], (16, BLK)).astype(BF16) for k in range(STEN)]
            w = [jnp.broadcast_to(merged[k, pl.ds(entry, 1), :], (16, BLK)).astype(BF16) for k in range(STEN)]
            for i in range(WIN // 16):
                here = (iota + 16.0 * i).astype(BF16)
                m = jnp.zeros((16, BLK), BF16)
                for k in range(STEN):
                    m = jnp.where(c[k] == here, w[k], m)
                ring[lax.rem(group, 2), j, 16 * i : 16 * i + 16, :] = m
        stored(group).start()
        return carry

    groups = (n + PACK - 1) // PACK
    lax.fori_loop(0, groups, build, 0)

    @pl.when(groups >= 2)
    def _():
        stored(groups - 2).wait()

    @pl.when(groups >= 1)
    def _():
        stored(groups - 1).wait()


def spread_kernel(
    me, lev, geo_in, slot1, win1, count1, mats1, slot2, win2, count2, mats2,
    b_home, plus, minus, cross, mate, f_home, f_mate, f_plus, f_minus, f_cross, local, above,
    out, geo, values, firsts, total, ring, sems, ring_sems,
):
    core = lax.rem(me[0], 2)
    parts = (
        (plus, RELAY + ROUTE),
        (minus, RELAY + ROUTE),
        (cross, ROUTE),
        (mate, HALO + LOWS + 1 + ROUTE),
        (mate, OWN + HALO + ROUTE),
        (mate, OWN + RELAY + HALO + ROUTE),
    )
    pairs = [(b_home, values.at[pl.ds(0, HOME)])]
    pairs += [
        (p.at[pl.ds(at, OFFCAP)], values.at[pl.ds(HOME + OFFCAP * i, OFFCAP)]) for i, (p, at) in enumerate(parts)
    ]
    pairs += [(geo_in, geo)]
    copies = launch([(a, b, sems.at[i]) for i, (a, b) in enumerate(pairs)])
    loops = ((slot1, win1, count1, mats1, 0, EARLY), (slot2, win2, count2, mats2, EARLY, LATE))

    def fetched(mats, lane, group):
        at = lax.rem(group, RING)
        return pltpu.make_async_copy(mats.at[pl.ds(group * PACK, PACK)], ring.at[lane, at], ring_sems.at[lane, at])

    for lane, (_, _, count, mats, _, _) in enumerate(loops):
        groups = (count[0] + PACK - 1) // PACK
        for g in range(RING):

            @pl.when(g < groups)
            def _():
                fetched(mats, lane, g).start()

    total[...] = jnp.zeros_like(total)
    half = OFFCAP * 4
    pieces = (
        f_plus[:half], f_minus[:half], f_cross[...], f_mate[...], f_plus[half:], f_minus[half:],
    )
    firsts[: HOME * 4, :] = f_home[...].astype(F32)
    for i, piece in enumerate(pieces):
        firsts[HOME * 4 + half * i : HOME * 4 + half * (i + 1), :] = piece.astype(F32)
    firsts[SLOTS * 4 :, :] = jnp.zeros((8, BLK), F32)
    finish(copies)
    first_rows = lax.broadcasted_iota(jnp.int32, (8, BLK), 0) < 4

    for lane, (slots, wins, count, mats, base, size) in enumerate(loops):
        groups = (count[0] + PACK - 1) // PACK

        def step(group, carry):
            fetched(mats, lane, group).wait()
            products = []
            for j in range(PACK):
                slot = base + lax.rem(slots[group * PACK + j], size)
                tile = values[slot].astype(F32)
                head = jnp.where(first_rows, firsts[pl.ds(slot * 4, 8), :], tile[:8])
                left = jnp.concatenate([head, tile[8:]], axis=0).astype(BF16)
                mat = ring[lane, lax.rem(group, RING), j]
                products.append(lax.dot_general(left, mat, (((1,), (1,)), ((), ())), preferred_element_type=F32))

            for j in range(PACK):
                start = pl.multiple_of(wins[group * PACK + j] * WIN, WIN)
                total[:, pl.ds(start, WIN)] += products[j]

            @pl.when(group + RING < groups)
            def _():
                fetched(mats, lane, group + RING).start()

            return carry

        lax.fori_loop(0, groups, step, 0)

    sums = jnp.zeros((NBLK, BLK), F32)
    for peer in range(above.shape[0]):
        sums = sums + jnp.where(peer < lev[0], above[peer].astype(F32), 0.0)
    level = lax.broadcasted_iota(jnp.int32, (4, BLK), 0)
    factor = jnp.zeros((4, BLK), F32)
    for i in range(4):
        factor = jnp.where(level == i, geo[i], factor)
    for f in (0, 1, 3):
        out[f] = total[4 * f : 4 * f + 4, :CELLS]
    for b in range(NBLK):
        r = b // HALO
        term = factor * (local[4 * r : 4 * r + 4, lanes(b % HALO)] + sums[b : b + 1])
        out[2, :, lanes(b)] = total[8:12, lanes(b)] + term


def moved(parcel, by):
    peers = lax.axis_size("tile")
    return lax.ppermute(parcel, "tile", [(i, i + by) for i in range(peers) if 0 <= i + by < peers])


def swapped(parcel):
    return lax.ppermute(parcel, "tile", [(i, i ^ 1) for i in range(lax.axis_size("tile"))])


def crossed(parcel):
    peers = lax.axis_size("tile")
    pairs = [(i, i + (3 if i % 2 else -3)) for i in range(peers)]
    return lax.ppermute(parcel, "tile", [(i, j) for i, j in pairs if 0 <= j < peers])


def matrices(home, parts):
    count = (HOME if home else 0) + OFFCAP * len(parts)
    entries = 2 * count
    return call(
        lambda *refs: matrix_kernel(count, len(home), [at for _, at in parts], *refs),
        [
            ((entries, WIN, BLK), BF16, hbm()),
            ((entries + 8,), jnp.int32, smem()),
            ((entries + 8,), jnp.int32, smem()),
            ((1,), jnp.int32, smem()),
        ],
        [vmem()] * len(home) + [hbm()] * len(parts),
        [
            pltpu.VMEM((len(parts), ROUTE, 16, BLK), BF16),
            pltpu.VMEM((STEN, count, BLK), F32),
            pltpu.VMEM((STEN, 2 * count, BLK), F32),
            pltpu.VMEM((2, PACK, WIN, BLK), BF16),
            pltpu.VMEM((1, BLK), jnp.int32),
            pltpu.SMEM((1, BLK), jnp.int32),
            pltpu.SemaphoreType.DMA((len(parts),)),
            pltpu.SemaphoreType.DMA((2,)),
            pltpu.SemaphoreType.DMA,
        ],
        4,
        16,
    )(*home, *[parcel for parcel, _ in parts])


def body(adj_in, helm_coef, geo_coef, dest_tile, src_window, src_cell, interp_w):
    me = lax.axis_index("tile").astype(jnp.int32)[None]
    lev = lax.axis_index("lev").astype(jnp.int32)[None]
    peers = lax.axis_size("lev")

    def parcel(entries):
        return ((entries, 16, BLK), BF16, vmem())

    def strip(blocks):
        return ((blocks * 4, BLK), BF16, vmem())

    slots, a_home, b_home, own, plus, minus, cross = call(
        pack_kernel,
        [
            ((NBLK,), jnp.int32, smem()),
            ((ROUTE, HOME, BLK), BF16, vmem()),
            parcel(HOME),
            parcel(OWN),
            parcel(RELAY + LOAD),
            parcel(RELAY + LOAD),
            parcel(LOAD),
        ],
        [smem()] + [hbm()] * 6,
        [
            pltpu.SMEM((NBLK,), jnp.int32),
            pltpu.SMEM((NBLK,), jnp.int32),
            pltpu.VMEM(adj_in.shape, BF16),
            pltpu.VMEM(helm_coef.shape, F32),
            pltpu.VMEM(src_cell.shape, jnp.int32),
            pltpu.VMEM(interp_w.shape, BF16),
            pltpu.SMEM((2 * REACH + 1,), jnp.int32),
            pltpu.VMEM((ROUTE * SLOTS, BLK), F32),
            pltpu.VMEM((SLOTS, 16, BLK), BF16),
            pltpu.SemaphoreType.DMA((6,)),
        ],
        1,
        24,
    )(me, dest_tile[:, 0], src_window, adj_in, helm_coef, src_cell, interp_w)
    plus = moved(plus, 2)
    minus = moved(minus, -2)
    cross = crossed(cross)

    relayed = call(
        relay_kernel,
        [((OWN + 2 * RELAY, 16, BLK), BF16, hbm())],
        [hbm()] * 3,
        [pltpu.SemaphoreType.DMA((3,))],
        1,
        16,
    )(own, plus, minus)[0]
    mate = swapped(relayed)

    early = matrices([a_home], [(plus, RELAY), (minus, RELAY), (cross, 0)])

    local, totals, f_home, f_mate, f_plus, f_minus, f_cross = call(
        solve_kernel,
        [
            ((8, NLON), F32, vmem()),
            ((peers, NBLK, BLK), BF16, vmem()),
            strip(HOME),
            strip(OFFCAP),
            strip(2 * OFFCAP),
            strip(2 * OFFCAP),
            strip(OFFCAP),
        ],
        [smem()] * 2 + [hbm()] * 6,
        [
            pltpu.VMEM(adj_in.shape[1:], BF16),
            pltpu.VMEM(helm_coef.shape, F32),
            pltpu.VMEM((6, HALO, 16, BLK), BF16),
            pltpu.VMEM((LOWS + 1, 16, BLK), BF16),
            pltpu.VMEM((6, 8, NLON), F32),
            pltpu.VMEM((6, 8, NLON), F32),
            pltpu.VMEM((2, 8, NLON), F32),
            pltpu.VMEM((1, BLK), jnp.int32),
            pltpu.SMEM((1, BLK), jnp.int32),
            pltpu.VMEM((SLOTS * 4, BLK), F32),
            pltpu.VMEM((SLOTS * 4, BLK), F32),
            pltpu.VMEM((NBLK, BLK), F32),
            pltpu.SemaphoreType.DMA((9,)),
            pltpu.SemaphoreType.DMA,
        ],
        2,
        24,
    )(me, slots, adj_in, helm_coef, own, plus, minus, mate)
    above = lax.all_to_all(totals, "lev", 0, 0)
    f_plus = moved(f_plus, 2)
    f_minus = moved(f_minus, -2)
    f_cross = crossed(f_cross)

    late = matrices(
        [],
        [(mate, HALO + LOWS + 1), (mate, OWN + HALO), (mate, OWN + RELAY + HALO)],
    )

    def lists(found):
        mats, entry_slot, entry_win, entry_count = found
        return entry_slot, entry_win, entry_count, mats

    listed = [smem()] * 3 + [hbm()]
    return call(
        spread_kernel,
        [((4, 4, CELLS), F32, vmem())],
        [smem()] * 2 + [hbm()] + listed * 2 + [hbm()] * 5 + [vmem()] * 7,
        [
            pltpu.SMEM((4,), F32),
            pltpu.VMEM((SLOTS, 16, BLK), BF16),
            pltpu.VMEM((SLOTS * 4 + 8, BLK), F32),
            pltpu.VMEM((16, CELLS + WIN), F32),
            pltpu.VMEM((2, RING, PACK, WIN, BLK), BF16),
            pltpu.SemaphoreType.DMA((GROUPS + 2,)),
            pltpu.SemaphoreType.DMA((2, RING)),
        ],
        4,
        24,
    )(
        me, lev, geo_coef, *lists(early), *lists(late),
        b_home, plus, minus, cross, mate, f_home, f_mate, f_plus, f_minus, f_cross, local, above,
    )[0]


def solution(mesh):
    placed = (
        P(None, "lev", "tile"),
        P("lev", "tile"),
        P("lev"),
        P("tile", None),
        P("tile"),
        P(None, "tile"),
        P(None, "tile"),
    )
    return jax.shard_map(
        body, mesh=mesh, in_specs=placed, out_specs=P(None, "lev", "tile"), check_vma=False
    )
```

```python
import jax
import jax.numpy as jnp
from jax import lax
from jax.experimental import pallas as pl
from jax.experimental.pallas import tpu as pltpu
from jax.sharding import PartitionSpec as P

NLON = 4096
BLK = 128
WIN = 256
SWEEPS = 4
REACH = 3
HOME = 32
OFFCAP = 16

F32 = jnp.float32
BF16 = jnp.bfloat16
STEN = 12
NBLK = 64
CELLS = 8192
NWIN = CELLS // WIN
OFFSETS = (-3, -2, -1, 1, 2, 3)
GROUPS = len(OFFSETS)
SLOTS = HOME + OFFCAP * GROUPS
HALO = NLON // BLK
ROUTE = 2 * STEN + 1
LOAD = ROUTE + OFFCAP
RELAY = HALO + LOAD
LOWS = HALO // 2
OWN = HALO + LOWS + 1 + LOAD
EARLY = HOME + 3 * OFFCAP
LATE = 3 * OFFCAP
PACK = 4
RING = 4
REMAINDER = 1e-6


def vmem():
    return pl.BlockSpec(memory_space=pltpu.VMEM)


def smem():
    return pl.BlockSpec(memory_space=pltpu.SMEM)


def free():
    return pl.BlockSpec(memory_space=pl.ANY)


def hbm():
    return pl.BlockSpec(memory_space=pltpu.HBM)


def kept(array):
    return pltpu.with_memory_space_constraint(array, pltpu.HBM)


def lanes(i):
    return slice(i * BLK, (i + 1) * BLK)


def base_of(by):
    return 0 if by == 0 else HOME + OFFCAP * OFFSETS.index(by)


def either(core, first, second):
    return pl.multiple_of(jnp.where(core == 0, base_of(first), base_of(second)), OFFCAP)


def launch(copies):
    copies = [pltpu.make_async_copy(*copy) for copy in copies]
    for copy in copies:
        copy.start()
    return copies


def finish(copies):
    for copy in copies:
        copy.wait()


def call(kernel, outs, ins, scratch, cost, limit):
    return pl.pallas_call(
        kernel,
        out_shape=[(out[3] if out[3:] else jax.ShapeDtypeStruct)(out[0], out[1]) for out in outs],
        out_specs=[out[2] for out in outs],
        in_specs=ins,
        scratch_shapes=scratch,
        compiler_params=pltpu.CompilerParams(vmem_limit_bytes=limit << 20),
        cost_estimate=pl.CostEstimate(flops=cost * 1000000, bytes_accessed=cost * 3000000, transcendentals=0),
    )


def pack_kernel(
    me, dest_in, win_in, adj_in, helm_in, cell_in, weight_in,
    slots, a_home, b_home, own, plus, minus, cross,
    dest, win, adj, helm, cell, weight, count, a_all, b_all, sems,
):
    pairs = ((dest_in, dest), (win_in, win), (adj_in, adj), (helm_in, helm), (cell_in, cell), (weight_in, weight))
    copies = launch([(a, b, sems.at[i]) for i, (a, b) in enumerate(pairs)])
    core = lax.rem(me[0], 2)
    for by in range(-REACH, REACH + 1):
        count[by + REACH] = base_of(by)
    a_all[...] = jnp.zeros_like(a_all)
    b_all[...] = jnp.zeros_like(b_all)
    finish(copies)
    lane = lax.broadcasted_iota(jnp.int32, (16, BLK), 1)
    table = jnp.zeros((16, BLK), jnp.int32)
    for b in range(NBLK):
        route = dest[b] - me[0] + REACH
        slot = count[route]
        count[route] = slot + 1
        slots[b] = slot
        table = jnp.where(lane == b, slot, table)
        a_all[pl.ds(slot, STEN, stride=SLOTS), :] = weight[:, lanes(b)].astype(F32)
        a_all[pl.ds(STEN * SLOTS + slot, STEN, stride=SLOTS), :] = cell[:, lanes(b)].astype(F32)
        a_all[pl.ds(2 * STEN * SLOTS + slot, 1), :] = jnp.full((1, BLK), win[b] + 1, jnp.int32).astype(F32)
        b_all[slot] = jnp.concatenate([adj[f, :, lanes(b)].astype(F32) for f in range(4)], axis=0).astype(BF16)
    for r in range(ROUTE):
        a_home[r] = a_all[r * SLOTS : r * SLOTS + HOME, :].astype(BF16)
    b_home[...] = b_all[:HOME]
    loads = (
        (own, HALO + LOWS + 1, either(core, 1, -1)),
        (plus, HALO, either(core, 3, 1)),
        (plus, RELAY, either(core, 2, 2)),
        (minus, HALO, either(core, -1, -3)),
        (minus, RELAY, either(core, -2, -2)),
        (cross, 0, either(core, -3, 3)),
    )
    for parcel, at, base in loads:
        for r in range(ROUTE):
            parcel[at + r] = a_all[pl.ds(r * SLOTS + base, OFFCAP), :].astype(BF16)
        parcel[at + ROUTE : at + LOAD] = b_all[pl.ds(base, OFFCAP)]
    rest = []
    for i in range(HALO):
        coef = jnp.concatenate([helm[:, lanes(i)], helm[:, lanes(HALO + i)]], axis=0)
        rest.append(coef - coef.astype(BF16).astype(F32))
        first = [adj[0, :, lanes(i)].astype(F32), adj[0, :, lanes(HALO + i)].astype(F32)]
        piece = jnp.concatenate(first + [coef], axis=0).astype(BF16)
        for parcel in (own, plus, minus):
            parcel[i] = piece
    for i in range(LOWS):
        own[HALO + i] = jnp.concatenate(rest[2 * i : 2 * i + 2], axis=0).astype(BF16)
    own[HALO + LOWS] = table.astype(F32).astype(BF16)


def relay_kernel(own, plus, minus, out, sems):
    finish(
        launch(
            [
                (own, out.at[pl.ds(0, OWN)], sems.at[0]),
                (plus.at[pl.ds(0, RELAY)], out.at[pl.ds(OWN, RELAY)], sems.at[1]),
                (minus.at[pl.ds(0, RELAY)], out.at[pl.ds(OWN + RELAY, RELAY)], sems.at[2]),
            ]
        )
    )


def solve_kernel(
    me, slots, _, helm_in, own, plus, minus, mate,
    local, totals, f_home, f_mate, f_plus, f_minus, f_cross,
    helm, halo, lows, rhs, coef, result, table, table_s, mine_all, mate_all, t_all, sems, table_sem,
):
    core = lax.rem(me[0], 2)
    tables = launch([(mate.at[pl.ds(HALO, LOWS + 1)], lows, sems.at[7])])
    pairs = (
        (helm_in, helm),
        (plus.at[pl.ds(0, HALO)], halo.at[core]),
        (mate.at[pl.ds(OWN, HALO)], halo.at[1 - core]),
        (own.at[pl.ds(0, HALO)], halo.at[2 + core]),
        (mate.at[pl.ds(0, HALO)], halo.at[3 - core]),
        (minus.at[pl.ds(0, HALO)], halo.at[4 + core]),
        (mate.at[pl.ds(OWN + RELAY, HALO)], halo.at[5 - core]),
    )
    copies = launch([(a, b, sems.at[i]) for i, (a, b) in enumerate(pairs)])
    mine_all[...] = jnp.zeros_like(mine_all)
    mate_all[...] = jnp.zeros_like(mate_all)
    finish(tables)
    table[...] = lows[LOWS].astype(F32)[:1].astype(jnp.int32)
    tables = launch([(table, table_s, table_sem)])
    finish(copies)
    for band in range(6):
        for i in range(HALO):
            tile = halo[band, i].astype(F32)
            rhs[band, :, lanes(i)] = tile[:8]
            coef[band, :, lanes(i)] = tile[8:]
    for i in range(LOWS):
        tile = lows[i].astype(F32)
        coef[3 - core, :, lanes(2 * i)] += tile[:8]
        coef[3 - core, :, lanes(2 * i + 1)] += tile[8:]
    coef[2 + core] = jnp.concatenate([helm[:, :NLON], helm[:, NLON:]], axis=0)
    right = [rhs[band] for band in range(6)]
    factor = [coef[band] for band in range(6)]
    scale = [1.0 / (1.0 + 4.0 * c) for c in factor]
    solved = [r * s for r, s in zip(right, scale)]
    upper = lax.broadcasted_iota(jnp.int32, (8, NLON), 0) < 4
    for wanted in ((0, 1, 2, 3, 4, 5), (1, 2, 3, 4), (1, 2, 3, 4), (2, 3)):
        shifted = [c * s for c, s in zip(factor, solved)]
        turned = [pltpu.roll(p, 4, 0) for p in shifted]
        fresh = list(solved)
        for band in wanted:
            p = shifted[band]
            north = turned[max(band - 1, 0)]
            south = turned[min(band + 1, 5)]
            total = turned[band] + jnp.where(upper, north, south)
            total = total + pltpu.roll(p, 1, 1) + pltpu.roll(p, NLON - 1, 1)
            fresh[band] = (right[band] + total) * scale[band]
        solved = fresh
    result[0] = solved[2]
    result[1] = solved[3]
    mine = result[core]
    other = result[1 - core]
    finish(tables)
    for r in range(2):
        sums = mine[4 * r : 4 * r + 1]
        local[4 * r : 4 * r + 1, :] = sums
        for level in range(1, 4):
            sums = sums + mine[4 * r + level : 4 * r + level + 1]
            local[4 * r + level : 4 * r + level + 1, :] = sums
        for i in range(HALO):
            b = HALO * r + i
            t_all[b : b + 1, :] = sums[:, lanes(i)]
            mine_all[pl.ds(slots[b] * 4, 4), :] = mine[4 * r : 4 * r + 4, lanes(i)]
            mate_all[pl.ds(table_s[0, b] * 4, 4), :] = other[4 * r : 4 * r + 4, lanes(i)]
    totals_here = t_all[...].astype(BF16)
    for i in range(totals.shape[0]):
        totals[i] = totals_here

    def part(source, first, second):
        return source[pl.ds(either(core, first, second) * 4, OFFCAP * 4), :].astype(BF16)

    f_home[...] = mine_all[: HOME * 4].astype(BF16)
    f_mate[...] = part(mate_all, -1, 1)
    f_plus[: OFFCAP * 4] = part(mine_all, 2, 2)
    f_plus[OFFCAP * 4 :] = part(mate_all, 1, 3)
    f_minus[: OFFCAP * 4] = part(mine_all, -2, -2)
    f_minus[OFFCAP * 4 :] = part(mate_all, -3, -1)
    f_cross[...] = part(mine_all, -3, 3)


def matrix_kernel(count, home, offsets, *refs):
    a_home = refs[0] if home else None
    parcels, refs = refs[home : home + len(offsets)], refs[home + len(offsets) :]
    mats, entry_slot, entry_win, entry_count, a_in, cells, merged, ring, meta, meta_s, sems, ring_sems, meta_sem = refs
    copies = launch([(p.at[pl.ds(at, ROUTE)], a_in.at[i], sems.at[i]) for i, (p, at) in enumerate(zip(parcels, offsets))])

    lane = lax.broadcasted_iota(jnp.int32, (8, BLK), 1)
    row = lax.broadcasted_iota(jnp.int32, (8, BLK), 0)

    def merge(base, load):
        w = [load(k) for k in range(STEN)]
        c = [load(STEN + k) for k in range(STEN)]
        total = list(w)
        for k in range(STEN):
            for m in range(k):
                same = c[k] == c[m]
                total[k] = total[k] + jnp.where(same, w[m], 0.0)
                total[m] = total[m] + jnp.where(same, w[k], 0.0)
        lost = jnp.zeros((8, BLK), F32)
        held = jnp.zeros((8, BLK), F32)
        for k in range(STEN):
            high = total[k].astype(BF16).astype(F32)
            low = total[k] - high
            cells[k, base : base + 8, :] = c[k]
            merged[k, base : base + 8, :] = high
            merged[k, count + base : count + base + 8, :] = low
            lost = lost + low * low
            held = held + w[k] * w[k]
        more = jnp.sum(lost, axis=1, keepdims=True) > REMAINDER * jnp.sum(held, axis=1, keepdims=True)
        mark = load(2 * STEN)
        mark = jnp.where(mark > 0.0, mark + jnp.where(more, 64.0, 0.0), 0.0)
        return jnp.where(lane == row + base, mark, 0.0)

    marks = jnp.zeros((8, BLK), F32)
    for at in range(0, HOME if home else 0, 16):
        pair = [a_home[r, at : at + 16, :].astype(F32) for r in range(ROUTE)]
        for half in (0, 8):
            marks = marks + merge(at + half, lambda r: pair[r][half : half + 8])
    for i in range(len(offsets)):
        copies[i].wait()
        pair = [a_in[i, r].astype(F32) for r in range(ROUTE)]
        at = (HOME if home else 0) + OFFCAP * i
        for half in (0, 8):
            marks = marks + merge(at + half, lambda r: pair[r][half : half + 8])
    meta[...] = jnp.sum(marks, axis=0, keepdims=True).astype(jnp.int32)
    finish(launch([(meta, meta_s, meta_sem)]))

    def enlist(i, n):
        for j in range(8):
            slot = i * 8 + j
            mark = meta_s[0, slot]
            window = (mark & 63) - 1
            entry_slot[n] = slot
            entry_win[n] = window
            n = n + (mark > 0).astype(jnp.int32)
            entry_slot[n] = slot + count
            entry_win[n] = window
            n = n + (mark >= 64).astype(jnp.int32)
        return n

    n = lax.fori_loop(0, count // 8, enlist, jnp.int32(0))
    entry_count[0] = n
    for j in range(PACK):
        entry_slot[n + j] = 0
        entry_win[n + j] = NWIN

    iota = lax.broadcasted_iota(jnp.int32, (16, BLK), 0).astype(F32)

    def stored(group):
        at = lax.rem(group, 2)
        return pltpu.make_async_copy(ring.at[at], mats.at[pl.ds(group * PACK, PACK)], ring_sems.at[at])

    def build(group, carry):
        @pl.when(group >= 2)
        def _():
            stored(group - 2).wait()

        for j in range(PACK):
            entry = entry_slot[group * PACK + j]
            slot = lax.rem(entry, count)
            c = [jnp.broadcast_to(cells[k, pl.ds(slot, 1), :], (16, BLK)).astype(BF16) for k in range(STEN)]
            w = [jnp.broadcast_to(merged[k, pl.ds(entry, 1), :], (16, BLK)).astype(BF16) for k in range(STEN)]
            for i in range(WIN // 16):
                here = (iota + 16.0 * i).astype(BF16)
                m = jnp.zeros((16, BLK), BF16)
                for k in range(STEN):
                    m = jnp.where(c[k] == here, w[k], m)
                ring[lax.rem(group, 2), j, 16 * i : 16 * i + 16, :] = m
        stored(group).start()
        return carry

    groups = (n + PACK - 1) // PACK
    lax.fori_loop(0, groups, build, 0)

    @pl.when(groups >= 2)
    def _():
        stored(groups - 2).wait()

    @pl.when(groups >= 1)
    def _():
        stored(groups - 1).wait()


def spread_kernel(
    me, lev, geo_in, slot1, win1, count1, mats1, slot2, win2, count2, mats2,
    b_home, plus, minus, cross, mate, f_home, f_mate, f_plus, f_minus, f_cross, local, above,
    out, geo, values, firsts, total, ring, sems, ring_sems,
):
    core = lax.rem(me[0], 2)
    parts = (
        (plus, RELAY + ROUTE),
        (minus, RELAY + ROUTE),
        (cross, ROUTE),
        (mate, HALO + LOWS + 1 + ROUTE),
        (mate, OWN + HALO + ROUTE),
        (mate, OWN + RELAY + HALO + ROUTE),
    )
    pairs = [(b_home, values.at[pl.ds(0, HOME)])]
    pairs += [
        (p.at[pl.ds(at, OFFCAP)], values.at[pl.ds(HOME + OFFCAP * i, OFFCAP)]) for i, (p, at) in enumerate(parts)
    ]
    pairs += [(geo_in, geo)]
    copies = launch([(a, b, sems.at[i]) for i, (a, b) in enumerate(pairs)])
    loops = ((slot1, win1, count1, mats1, 0, EARLY), (slot2, win2, count2, mats2, EARLY, LATE))

    def fetched(mats, lane, group):
        at = lax.rem(group, RING)
        return pltpu.make_async_copy(mats.at[pl.ds(group * PACK, PACK)], ring.at[lane, at], ring_sems.at[lane, at])

    for lane, (_, _, count, mats, _, _) in enumerate(loops):
        groups = (count[0] + PACK - 1) // PACK
        for g in range(RING):

            @pl.when(g < groups)
            def _():
                fetched(mats, lane, g).start()

    total[...] = jnp.zeros_like(total)
    half = OFFCAP * 4
    pieces = (
        f_plus[:half], f_minus[:half], f_cross[...], f_mate[...], f_plus[half:], f_minus[half:],
    )
    firsts[: HOME * 4, :] = f_home[...].astype(F32)
    for i, piece in enumerate(pieces):
        firsts[HOME * 4 + half * i : HOME * 4 + half * (i + 1), :] = piece.astype(F32)
    firsts[SLOTS * 4 :, :] = jnp.zeros((8, BLK), F32)
    finish(copies)
    first_rows = lax.broadcasted_iota(jnp.int32, (8, BLK), 0) < 4

    for lane, (slots, wins, count, mats, base, size) in enumerate(loops):
        groups = (count[0] + PACK - 1) // PACK

        def step(group, carry):
            fetched(mats, lane, group).wait()
            products = []
            for j in range(PACK):
                slot = base + lax.rem(slots[group * PACK + j], size)
                tile = values[slot].astype(F32)
                head = jnp.where(first_rows, firsts[pl.ds(slot * 4, 8), :], tile[:8])
                left = jnp.concatenate([head, tile[8:]], axis=0).astype(BF16)
                mat = ring[lane, lax.rem(group, RING), j]
                products.append(lax.dot_general(left, mat, (((1,), (1,)), ((), ())), preferred_element_type=F32))

            for j in range(PACK):
                start = pl.multiple_of(wins[group * PACK + j] * WIN, WIN)
                total[:, pl.ds(start, WIN)] += products[j]

            @pl.when(group + RING < groups)
            def _():
                fetched(mats, lane, group + RING).start()

            return carry

        lax.fori_loop(0, groups, step, 0)

    sums = jnp.zeros((NBLK, BLK), F32)
    for peer in range(above.shape[0]):
        sums = sums + jnp.where(peer < lev[0], above[peer].astype(F32), 0.0)
    level = lax.broadcasted_iota(jnp.int32, (4, BLK), 0)
    factor = jnp.zeros((4, BLK), F32)
    for i in range(4):
        factor = jnp.where(level == i, geo[i], factor)
    for f in (0, 1, 3):
        out[f] = total[4 * f : 4 * f + 4, :CELLS]
    for b in range(NBLK):
        r = b // HALO
        term = factor * (local[4 * r : 4 * r + 4, lanes(b % HALO)] + sums[b : b + 1])
        out[2, :, lanes(b)] = total[8:12, lanes(b)] + term


def moved(parcel, by):
    peers = lax.axis_size("tile")
    return lax.ppermute(parcel, "tile", [(i, i + by) for i in range(peers) if 0 <= i + by < peers])


def swapped(parcel):
    return lax.ppermute(parcel, "tile", [(i, i ^ 1) for i in range(lax.axis_size("tile"))])


def crossed(parcel):
    peers = lax.axis_size("tile")
    pairs = [(i, i + (3 if i % 2 else -3)) for i in range(peers)]
    return lax.ppermute(parcel, "tile", [(i, j) for i, j in pairs if 0 <= j < peers])


def matrices(home, parts):
    count = (HOME if home else 0) + OFFCAP * len(parts)
    entries = 2 * count
    return call(
        lambda *refs: matrix_kernel(count, len(home), [at for _, at in parts], *refs),
        [
            ((entries, WIN, BLK), BF16, hbm(), pltpu.HBM),
            ((entries + 8,), jnp.int32, smem()),
            ((entries + 8,), jnp.int32, smem()),
            ((1,), jnp.int32, smem()),
        ],
        [vmem()] * len(home) + [free()] * len(parts),
        [
            pltpu.VMEM((len(parts), ROUTE, 16, BLK), BF16),
            pltpu.VMEM((STEN, count, BLK), F32),
            pltpu.VMEM((STEN, 2 * count, BLK), F32),
            pltpu.VMEM((2, PACK, WIN, BLK), BF16),
            pltpu.VMEM((1, BLK), jnp.int32),
            pltpu.SMEM((1, BLK), jnp.int32),
            pltpu.SemaphoreType.DMA((len(parts),)),
            pltpu.SemaphoreType.DMA((2,)),
            pltpu.SemaphoreType.DMA,
        ],
        4,
        16,
    )(*home, *[parcel for parcel, _ in parts])


def body(adj_in, helm_coef, geo_coef, dest_tile, src_window, src_cell, interp_w):
    me = lax.axis_index("tile").astype(jnp.int32)[None]
    lev = lax.axis_index("lev").astype(jnp.int32)[None]
    peers = lax.axis_size("lev")

    def parcel(entries):
        return ((entries, 16, BLK), BF16, vmem())

    def strip(blocks):
        return ((blocks * 4, BLK), BF16, vmem())

    slots, a_home, b_home, own, plus, minus, cross = call(
        pack_kernel,
        [
            ((NBLK,), jnp.int32, smem()),
            ((ROUTE, HOME, BLK), BF16, vmem()),
            parcel(HOME),
            parcel(OWN),
            parcel(RELAY + LOAD),
            parcel(RELAY + LOAD),
            parcel(LOAD),
        ],
        [smem()] + [hbm()] * 6,
        [
            pltpu.SMEM((NBLK,), jnp.int32),
            pltpu.SMEM((NBLK,), jnp.int32),
            pltpu.VMEM(adj_in.shape, BF16),
            pltpu.VMEM(helm_coef.shape, F32),
            pltpu.VMEM(src_cell.shape, jnp.int32),
            pltpu.VMEM(interp_w.shape, BF16),
            pltpu.SMEM((2 * REACH + 1,), jnp.int32),
            pltpu.VMEM((ROUTE * SLOTS, BLK), F32),
            pltpu.VMEM((SLOTS, 16, BLK), BF16),
            pltpu.SemaphoreType.DMA((6,)),
        ],
        1,
        24,
    )(me, *map(kept, (dest_tile[:, 0], src_window, adj_in, helm_coef, src_cell, interp_w)))
    plus = moved(plus, 2)
    minus = moved(minus, -2)
    cross = crossed(cross)

    relayed = call(
        relay_kernel,
        [((OWN + 2 * RELAY, 16, BLK), BF16, free())],
        [free()] * 3,
        [pltpu.SemaphoreType.DMA((3,))],
        1,
        16,
    )(own, plus, minus)[0]
    mate = swapped(relayed)

    early = matrices([a_home], [(plus, RELAY), (minus, RELAY), (cross, 0)])

    local, totals, f_home, f_mate, f_plus, f_minus, f_cross = call(
        solve_kernel,
        [
            ((8, NLON), F32, vmem()),
            ((peers, NBLK, BLK), BF16, vmem()),
            strip(HOME),
            strip(OFFCAP),
            strip(2 * OFFCAP),
            strip(2 * OFFCAP),
            strip(OFFCAP),
        ],
        [smem()] * 3 + [hbm()] + [free()] * 4,
        [
            pltpu.VMEM(helm_coef.shape, F32),
            pltpu.VMEM((6, HALO, 16, BLK), BF16),
            pltpu.VMEM((LOWS + 1, 16, BLK), BF16),
            pltpu.VMEM((6, 8, NLON), F32),
            pltpu.VMEM((6, 8, NLON), F32),
            pltpu.VMEM((2, 8, NLON), F32),
            pltpu.VMEM((1, BLK), jnp.int32),
            pltpu.SMEM((1, BLK), jnp.int32),
            pltpu.VMEM((SLOTS * 4, BLK), F32),
            pltpu.VMEM((SLOTS * 4, BLK), F32),
            pltpu.VMEM((NBLK, BLK), F32),
            pltpu.SemaphoreType.DMA((8,)),
            pltpu.SemaphoreType.DMA,
        ],
        2,
        24,
    )(me, slots, early[3], kept(helm_coef), own, plus, minus, mate)
    above = lax.all_to_all(totals, "lev", 0, 0)
    f_plus = moved(f_plus, 2)
    f_minus = moved(f_minus, -2)
    f_cross = crossed(f_cross)

    late = matrices(
        [],
        [(mate, HALO + LOWS + 1), (mate, OWN + HALO), (mate, OWN + RELAY + HALO)],
    )

    def lists(found):
        mats, entry_slot, entry_win, entry_count = found
        return entry_slot, entry_win, entry_count, kept(mats)

    listed = [smem()] * 3 + [hbm()]
    return call(
        spread_kernel,
        [((4, 4, CELLS), F32, vmem())],
        [smem()] * 2 + [hbm()] + listed * 2 + [free()] * 5 + [vmem()] * 7,
        [
            pltpu.SMEM((4,), F32),
            pltpu.VMEM((SLOTS, 16, BLK), BF16),
            pltpu.VMEM((SLOTS * 4 + 8, BLK), F32),
            pltpu.VMEM((16, CELLS + WIN), F32),
            pltpu.VMEM((2, RING, PACK, WIN, BLK), BF16),
            pltpu.SemaphoreType.DMA((GROUPS + 2,)),
            pltpu.SemaphoreType.DMA((2, RING)),
        ],
        4,
        24,
    )(
        me, lev, kept(geo_coef), *lists(early), *lists(late),
        b_home, plus, minus, cross, mate, f_home, f_mate, f_plus, f_minus, f_cross, local, above,
    )[0]


def solution(mesh):
    placed = (
        P(None, "lev", "tile"),
        P("lev", "tile"),
        P("lev"),
        P("tile", None),
        P("tile"),
        P(None, "tile"),
        P(None, "tile"),
    )
    return jax.shard_map(
        body, mesh=mesh, in_specs=placed, out_specs=P(None, "lev", "tile"), check_vma=False
    )
```

```python
import jax
import jax.numpy as jnp
from jax import lax
from jax.experimental import pallas as pl
from jax.experimental.pallas import tpu as pltpu
from jax.sharding import PartitionSpec as P

NLON = 4096
BLK = 128
WIN = 256
SWEEPS = 4
REACH = 3
HOME = 32
OFFCAP = 16

F32 = jnp.float32
BF16 = jnp.bfloat16
STEN = 12
NBLK = 64
CELLS = 8192
NWIN = CELLS // WIN
OFFSETS = (-3, -2, -1, 1, 2, 3)
GROUPS = len(OFFSETS)
SLOTS = HOME + OFFCAP * GROUPS
HALO = NLON // BLK
ROUTE = 2 * STEN + 1
LOAD = ROUTE + OFFCAP
RELAY = HALO + LOAD
LOWS = HALO // 2
OWN = HALO + LOWS + 1 + LOAD
MIDDLE = 2 * OFFCAP
LATE = 4 * OFFCAP
PACK = 4
RING = 8
REMAINDER = 1e-6


def vmem():
    return pl.BlockSpec(memory_space=pltpu.VMEM)


def smem():
    return pl.BlockSpec(memory_space=pltpu.SMEM)


def free():
    return pl.BlockSpec(memory_space=pl.ANY)


def hbm():
    return pl.BlockSpec(memory_space=pltpu.HBM)


def kept(array):
    return pltpu.with_memory_space_constraint(array, pltpu.HBM)


def lanes(i):
    return slice(i * BLK, (i + 1) * BLK)


def base_of(by):
    return 0 if by == 0 else HOME + OFFCAP * OFFSETS.index(by)


def either(core, first, second):
    return pl.multiple_of(jnp.where(core == 0, base_of(first), base_of(second)), OFFCAP)


def launch(copies):
    copies = [pltpu.make_async_copy(*copy) for copy in copies]
    for copy in copies:
        copy.start()
    return copies


def finish(copies):
    for copy in copies:
        copy.wait()


def call(kernel, outs, ins, scratch, cost, limit):
    return pl.pallas_call(
        kernel,
        out_shape=[(out[3] if out[3:] else jax.ShapeDtypeStruct)(out[0], out[1]) for out in outs],
        out_specs=[out[2] for out in outs],
        in_specs=ins,
        scratch_shapes=scratch,
        compiler_params=pltpu.CompilerParams(vmem_limit_bytes=limit << 20),
        cost_estimate=pl.CostEstimate(flops=cost * 1000000, bytes_accessed=cost * 3000000, transcendentals=0),
    )


def pack_kernel(
    me, dest_in, win_in, adj_in, helm_in, cell_in, weight_in,
    slots, a_home, b_home, own, plus, minus, cross,
    dest, win, adj, helm, cell, weight, count, a_all, b_all, sems,
):
    pairs = ((dest_in, dest), (win_in, win), (adj_in, adj), (helm_in, helm), (cell_in, cell), (weight_in, weight))
    copies = launch([(a, b, sems.at[i]) for i, (a, b) in enumerate(pairs)])
    core = lax.rem(me[0], 2)
    for by in range(-REACH, REACH + 1):
        count[by + REACH] = base_of(by)
    a_all[...] = jnp.zeros_like(a_all)
    b_all[...] = jnp.zeros_like(b_all)
    finish(copies)
    lane = lax.broadcasted_iota(jnp.int32, (16, BLK), 1)
    table = jnp.zeros((16, BLK), jnp.int32)
    for b in range(NBLK):
        route = dest[b] - me[0] + REACH
        slot = count[route]
        count[route] = slot + 1
        slots[b] = slot
        table = jnp.where(lane == b, slot, table)
        a_all[pl.ds(slot, STEN, stride=SLOTS), :] = weight[:, lanes(b)].astype(F32)
        a_all[pl.ds(STEN * SLOTS + slot, STEN, stride=SLOTS), :] = cell[:, lanes(b)].astype(F32)
        a_all[pl.ds(2 * STEN * SLOTS + slot, 1), :] = jnp.full((1, BLK), win[b] + 1, jnp.int32).astype(F32)
        b_all[slot] = jnp.concatenate([adj[f, :, lanes(b)].astype(F32) for f in range(4)], axis=0).astype(BF16)
    for r in range(ROUTE):
        a_home[r] = a_all[r * SLOTS : r * SLOTS + HOME, :].astype(BF16)
    b_home[...] = b_all[:HOME]
    loads = (
        (own, HALO + LOWS + 1, either(core, 1, -1)),
        (plus, HALO, either(core, 3, 1)),
        (plus, RELAY, either(core, 2, 2)),
        (minus, HALO, either(core, -1, -3)),
        (minus, RELAY, either(core, -2, -2)),
        (cross, 0, either(core, -3, 3)),
    )
    for parcel, at, base in loads:
        for r in range(ROUTE):
            parcel[at + r] = a_all[pl.ds(r * SLOTS + base, OFFCAP), :].astype(BF16)
        parcel[at + ROUTE : at + LOAD] = b_all[pl.ds(base, OFFCAP)]
    rest = []
    for i in range(HALO):
        coef = jnp.concatenate([helm[:, lanes(i)], helm[:, lanes(HALO + i)]], axis=0)
        rest.append(coef - coef.astype(BF16).astype(F32))
        first = [adj[0, :, lanes(i)].astype(F32), adj[0, :, lanes(HALO + i)].astype(F32)]
        piece = jnp.concatenate(first + [coef], axis=0).astype(BF16)
        for parcel in (own, plus, minus):
            parcel[i] = piece
    for i in range(LOWS):
        own[HALO + i] = jnp.concatenate(rest[2 * i : 2 * i + 2], axis=0).astype(BF16)
    own[HALO + LOWS] = table.astype(F32).astype(BF16)


def relay_kernel(_, own, plus, minus, out, sems):
    finish(
        launch(
            [
                (own, out.at[pl.ds(0, OWN)], sems.at[0]),
                (plus.at[pl.ds(0, RELAY)], out.at[pl.ds(OWN, RELAY)], sems.at[1]),
                (minus.at[pl.ds(0, RELAY)], out.at[pl.ds(OWN + RELAY, RELAY)], sems.at[2]),
            ]
        )
    )


def solve_kernel(
    me, slots, _, helm_in, own, plus, minus, mate,
    local, totals, f_home, f_mate, f_plus, f_minus, f_cross,
    helm, halo, lows, rhs, coef, result, table, table_s, mine_all, mate_all, t_all, sems, table_sem,
):
    core = lax.rem(me[0], 2)
    tables = launch([(mate.at[pl.ds(HALO, LOWS + 1)], lows, sems.at[7])])
    pairs = (
        (helm_in, helm),
        (plus.at[pl.ds(0, HALO)], halo.at[core]),
        (mate.at[pl.ds(OWN, HALO)], halo.at[1 - core]),
        (own.at[pl.ds(0, HALO)], halo.at[2 + core]),
        (mate.at[pl.ds(0, HALO)], halo.at[3 - core]),
        (minus.at[pl.ds(0, HALO)], halo.at[4 + core]),
        (mate.at[pl.ds(OWN + RELAY, HALO)], halo.at[5 - core]),
    )
    copies = launch([(a, b, sems.at[i]) for i, (a, b) in enumerate(pairs)])
    mine_all[...] = jnp.zeros_like(mine_all)
    mate_all[...] = jnp.zeros_like(mate_all)
    finish(tables)
    table[...] = lows[LOWS].astype(F32)[:1].astype(jnp.int32)
    tables = launch([(table, table_s, table_sem)])
    finish(copies)
    for band in range(6):
        for i in range(HALO):
            tile = halo[band, i].astype(F32)
            rhs[band, :, lanes(i)] = tile[:8]
            coef[band, :, lanes(i)] = tile[8:]
    for i in range(LOWS):
        tile = lows[i].astype(F32)
        coef[3 - core, :, lanes(2 * i)] += tile[:8]
        coef[3 - core, :, lanes(2 * i + 1)] += tile[8:]
    coef[2 + core] = jnp.concatenate([helm[:, :NLON], helm[:, NLON:]], axis=0)
    right = [rhs[band] for band in range(6)]
    factor = [coef[band] for band in range(6)]
    scale = [1.0 / (1.0 + 4.0 * c) for c in factor]
    solved = [r * s for r, s in zip(right, scale)]
    upper = lax.broadcasted_iota(jnp.int32, (8, NLON), 0) < 4
    for wanted in ((0, 1, 2, 3, 4, 5), (1, 2, 3, 4), (1, 2, 3, 4), (2, 3)):
        shifted = [c * s for c, s in zip(factor, solved)]
        turned = [pltpu.roll(p, 4, 0) for p in shifted]
        fresh = list(solved)
        for band in wanted:
            p = shifted[band]
            north = turned[max(band - 1, 0)]
            south = turned[min(band + 1, 5)]
            total = turned[band] + jnp.where(upper, north, south)
            total = total + pltpu.roll(p, 1, 1) + pltpu.roll(p, NLON - 1, 1)
            fresh[band] = (right[band] + total) * scale[band]
        solved = fresh
    result[0] = solved[2]
    result[1] = solved[3]
    mine = result[core]
    other = result[1 - core]
    finish(tables)
    for r in range(2):
        sums = mine[4 * r : 4 * r + 1]
        local[4 * r : 4 * r + 1, :] = sums
        for level in range(1, 4):
            sums = sums + mine[4 * r + level : 4 * r + level + 1]
            local[4 * r + level : 4 * r + level + 1, :] = sums
        for i in range(HALO):
            b = HALO * r + i
            t_all[b : b + 1, :] = sums[:, lanes(i)]
            mine_all[pl.ds(slots[b] * 4, 4), :] = mine[4 * r : 4 * r + 4, lanes(i)]
            mate_all[pl.ds(table_s[0, b] * 4, 4), :] = other[4 * r : 4 * r + 4, lanes(i)]
    totals_here = t_all[...].astype(BF16)
    for i in range(totals.shape[0]):
        totals[i] = totals_here

    def part(source, first, second):
        return source[pl.ds(either(core, first, second) * 4, OFFCAP * 4), :].astype(BF16)

    f_home[...] = mine_all[: HOME * 4].astype(BF16)
    f_mate[...] = part(mate_all, -1, 1)
    f_plus[: OFFCAP * 4] = part(mine_all, 2, 2)
    f_plus[OFFCAP * 4 :] = part(mate_all, 1, 3)
    f_minus[: OFFCAP * 4] = part(mine_all, -2, -2)
    f_minus[OFFCAP * 4 :] = part(mate_all, -3, -1)
    f_cross[...] = part(mine_all, -3, 3)


def matrix_kernel(count, home, offsets, *refs):
    a_home = refs[0] if home else None
    parcels, refs = refs[home : home + len(offsets)], refs[home + len(offsets) :]
    mats, entry_slot, entry_win, entry_count, a_in, cells, merged, ring, meta, meta_s, sems, ring_sems, meta_sem = refs
    copies = launch([(p.at[pl.ds(at, ROUTE)], a_in.at[i], sems.at[i]) for i, (p, at) in enumerate(zip(parcels, offsets))])

    lane = lax.broadcasted_iota(jnp.int32, (8, BLK), 1)
    row = lax.broadcasted_iota(jnp.int32, (8, BLK), 0)

    def merge(base, load):
        w = [load(k) for k in range(STEN)]
        c = [load(STEN + k) for k in range(STEN)]
        total = list(w)
        for k in range(STEN):
            for m in range(k):
                same = c[k] == c[m]
                total[k] = total[k] + jnp.where(same, w[m], 0.0)
                total[m] = total[m] + jnp.where(same, w[k], 0.0)
        lost = jnp.zeros((8, BLK), F32)
        held = jnp.zeros((8, BLK), F32)
        for k in range(STEN):
            high = total[k].astype(BF16).astype(F32)
            low = total[k] - high
            cells[k, base : base + 8, :] = c[k]
            merged[k, base : base + 8, :] = high
            merged[k, count + base : count + base + 8, :] = low
            lost = lost + low * low
            held = held + w[k] * w[k]
        more = jnp.sum(lost, axis=1, keepdims=True) > REMAINDER * jnp.sum(held, axis=1, keepdims=True)
        mark = load(2 * STEN)
        mark = jnp.where(mark > 0.0, mark + jnp.where(more, 64.0, 0.0), 0.0)
        return jnp.where(lane == row + base, mark, 0.0)

    marks = jnp.zeros((8, BLK), F32)
    for at in range(0, HOME if home else 0, 16):
        pair = [a_home[r, at : at + 16, :].astype(F32) for r in range(ROUTE)]
        for half in (0, 8):
            marks = marks + merge(at + half, lambda r: pair[r][half : half + 8])
    for i in range(len(offsets)):
        copies[i].wait()
        pair = [a_in[i, r].astype(F32) for r in range(ROUTE)]
        at = (HOME if home else 0) + OFFCAP * i
        for half in (0, 8):
            marks = marks + merge(at + half, lambda r: pair[r][half : half + 8])
    meta[...] = jnp.sum(marks, axis=0, keepdims=True).astype(jnp.int32)
    finish(launch([(meta, meta_s, meta_sem)]))

    def enlist(i, n):
        for j in range(8):
            slot = i * 8 + j
            mark = meta_s[0, slot]
            window = (mark & 63) - 1
            entry_slot[n] = slot
            entry_win[n] = window
            n = n + (mark > 0).astype(jnp.int32)
            entry_slot[n] = slot + count
            entry_win[n] = window
            n = n + (mark >= 64).astype(jnp.int32)
        return n

    n = lax.fori_loop(0, count // 8, enlist, jnp.int32(0))
    entry_count[0] = n
    for j in range(PACK):
        entry_slot[n + j] = 0
        entry_win[n + j] = NWIN

    iota = lax.broadcasted_iota(jnp.int32, (16, BLK), 0).astype(F32)

    def stored(group):
        at = lax.rem(group, RING)
        return pltpu.make_async_copy(ring.at[at], mats.at[pl.ds(group * PACK, PACK)], ring_sems.at[at])

    def build(group, carry):
        @pl.when(group >= RING)
        def _():
            stored(group - RING).wait()

        for j in range(PACK):
            entry = entry_slot[group * PACK + j]
            slot = lax.rem(entry, count)
            c = [jnp.broadcast_to(cells[k, pl.ds(slot, 1), :], (16, BLK)).astype(BF16) for k in range(STEN)]
            w = [jnp.broadcast_to(merged[k, pl.ds(entry, 1), :], (16, BLK)).astype(BF16) for k in range(STEN)]
            for i in range(WIN // 16):
                here = (iota + 16.0 * i).astype(BF16)
                m = jnp.zeros((16, BLK), BF16)
                for k in range(STEN):
                    m = jnp.where(c[k] == here, w[k], m)
                ring[lax.rem(group, RING), j, 16 * i : 16 * i + 16, :] = m
        stored(group).start()
        return carry

    groups = (n + PACK - 1) // PACK
    lax.fori_loop(0, groups, build, 0)
    for back in range(1, RING + 1):

        @pl.when(groups >= back)
        def _():
            stored(groups - back).wait()


def spread_kernel(
    me, lev, geo_in,
    slot1, win1, count1, mats1, slot2, win2, count2, mats2, slot3, win3, count3, mats3,
    b_home, plus, minus, cross, mate, f_home, f_mate, f_plus, f_minus, f_cross, local, above,
    out, geo, values, firsts, total, ring, sems, ring_sems,
):
    core = lax.rem(me[0], 2)
    parts = (
        (plus, RELAY + ROUTE),
        (minus, RELAY + ROUTE),
        (cross, ROUTE),
        (mate, HALO + LOWS + 1 + ROUTE),
        (mate, OWN + HALO + ROUTE),
        (mate, OWN + RELAY + HALO + ROUTE),
    )
    pairs = [(b_home, values.at[pl.ds(0, HOME)])]
    pairs += [
        (p.at[pl.ds(at, OFFCAP)], values.at[pl.ds(HOME + OFFCAP * i, OFFCAP)]) for i, (p, at) in enumerate(parts)
    ]
    pairs += [(geo_in, geo)]
    copies = launch([(a, b, sems.at[i]) for i, (a, b) in enumerate(pairs)])
    loops = (
        (slot1, win1, count1, mats1, 0, HOME),
        (slot2, win2, count2, mats2, HOME, MIDDLE),
        (slot3, win3, count3, mats3, HOME + MIDDLE, LATE),
    )

    def fetched(mats, lane, group):
        at = lax.rem(group, RING)
        return pltpu.make_async_copy(mats.at[pl.ds(group * PACK, PACK)], ring.at[lane, at], ring_sems.at[lane, at])

    for lane, (_, _, count, mats, _, _) in enumerate(loops):
        groups = (count[0] + PACK - 1) // PACK
        for g in range(RING):

            @pl.when(g < groups)
            def _():
                fetched(mats, lane, g).start()

    total[...] = jnp.zeros_like(total)
    half = OFFCAP * 4
    pieces = (
        f_plus[:half], f_minus[:half], f_cross[...], f_mate[...], f_plus[half:], f_minus[half:],
    )
    firsts[: HOME * 4, :] = f_home[...].astype(F32)
    for i, piece in enumerate(pieces):
        firsts[HOME * 4 + half * i : HOME * 4 + half * (i + 1), :] = piece.astype(F32)
    firsts[SLOTS * 4 :, :] = jnp.zeros((8, BLK), F32)
    finish(copies)
    first_rows = lax.broadcasted_iota(jnp.int32, (8, BLK), 0) < 4

    for lane, (slots, wins, count, mats, base, size) in enumerate(loops):
        groups = (count[0] + PACK - 1) // PACK

        def step(group, carry):
            fetched(mats, lane, group).wait()
            products = []
            for j in range(PACK):
                slot = base + lax.rem(slots[group * PACK + j], size)
                tile = values[slot].astype(F32)
                head = jnp.where(first_rows, firsts[pl.ds(slot * 4, 8), :], tile[:8])
                left = jnp.concatenate([head, tile[8:]], axis=0).astype(BF16)
                mat = ring[lane, lax.rem(group, RING), j]
                products.append(lax.dot_general(left, mat, (((1,), (1,)), ((), ())), preferred_element_type=F32))

            for j in range(PACK):
                start = pl.multiple_of(wins[group * PACK + j] * WIN, WIN)
                total[:, pl.ds(start, WIN)] += products[j]

            @pl.when(group + RING < groups)
            def _():
                fetched(mats, lane, group + RING).start()

            return carry

        lax.fori_loop(0, groups, step, 0)

    sums = jnp.zeros((NBLK, BLK), F32)
    for peer in range(above.shape[0]):
        sums = sums + jnp.where(peer < lev[0], above[peer].astype(F32), 0.0)
    level = lax.broadcasted_iota(jnp.int32, (4, BLK), 0)
    factor = jnp.zeros((4, BLK), F32)
    for i in range(4):
        factor = jnp.where(level == i, geo[i], factor)
    for f in (0, 1, 3):
        out[f] = total[4 * f : 4 * f + 4, :CELLS]
    for b in range(NBLK):
        r = b // HALO
        term = factor * (local[4 * r : 4 * r + 4, lanes(b % HALO)] + sums[b : b + 1])
        out[2, :, lanes(b)] = total[8:12, lanes(b)] + term


def moved(parcel, by):
    peers = lax.axis_size("tile")
    return lax.ppermute(parcel, "tile", [(i, i + by) for i in range(peers) if 0 <= i + by < peers])


def swapped(parcel):
    return lax.ppermute(parcel, "tile", [(i, i ^ 1) for i in range(lax.axis_size("tile"))])


def crossed(parcel):
    peers = lax.axis_size("tile")
    pairs = [(i, i + (3 if i % 2 else -3)) for i in range(peers)]
    return lax.ppermute(parcel, "tile", [(i, j) for i, j in pairs if 0 <= j < peers])


def matrices(home, parts, cost):
    count = (HOME if home else 0) + OFFCAP * len(parts)
    entries = 2 * count
    return call(
        lambda *refs: matrix_kernel(count, len(home), [at for _, at in parts], *refs),
        [
            ((entries, WIN, BLK), BF16, hbm(), pltpu.HBM),
            ((entries + 8,), jnp.int32, smem()),
            ((entries + 8,), jnp.int32, smem()),
            ((1,), jnp.int32, smem()),
        ],
        [vmem()] * len(home) + [free()] * len(parts),
        [
            pltpu.VMEM((max(len(parts), 1), ROUTE, 16, BLK), BF16),
            pltpu.VMEM((STEN, count, BLK), F32),
            pltpu.VMEM((STEN, 2 * count, BLK), F32),
            pltpu.VMEM((RING, PACK, WIN, BLK), BF16),
            pltpu.VMEM((1, BLK), jnp.int32),
            pltpu.SMEM((1, BLK), jnp.int32),
            pltpu.SemaphoreType.DMA((max(len(parts), 1),)),
            pltpu.SemaphoreType.DMA((RING,)),
            pltpu.SemaphoreType.DMA,
        ],
        cost,
        16,
    )(*home, *[parcel for parcel, _ in parts])


def body(adj_in, helm_coef, geo_coef, dest_tile, src_window, src_cell, interp_w):
    me = lax.axis_index("tile").astype(jnp.int32)[None]
    lev = lax.axis_index("lev").astype(jnp.int32)[None]
    peers = lax.axis_size("lev")

    def parcel(entries):
        return ((entries, 16, BLK), BF16, vmem())

    def strip(blocks):
        return ((blocks * 4, BLK), BF16, vmem())

    slots, a_home, b_home, own, plus, minus, cross = call(
        pack_kernel,
        [
            ((NBLK,), jnp.int32, smem()),
            ((ROUTE, HOME, BLK), BF16, vmem()),
            parcel(HOME),
            parcel(OWN),
            parcel(RELAY + LOAD),
            parcel(RELAY + LOAD),
            parcel(LOAD),
        ],
        [smem()] + [hbm()] * 6,
        [
            pltpu.SMEM((NBLK,), jnp.int32),
            pltpu.SMEM((NBLK,), jnp.int32),
            pltpu.VMEM(adj_in.shape, BF16),
            pltpu.VMEM(helm_coef.shape, F32),
            pltpu.VMEM(src_cell.shape, jnp.int32),
            pltpu.VMEM(interp_w.shape, BF16),
            pltpu.SMEM((2 * REACH + 1,), jnp.int32),
            pltpu.VMEM((ROUTE * SLOTS, BLK), F32),
            pltpu.VMEM((SLOTS, 16, BLK), BF16),
            pltpu.SemaphoreType.DMA((6,)),
        ],
        1,
        24,
    )(me, *map(kept, (dest_tile[:, 0], src_window, adj_in, helm_coef, src_cell, interp_w)))
    plus = moved(plus, 2)
    minus = moved(minus, -2)
    cross = crossed(cross)
    first = matrices([a_home], [], 40)

    relayed = call(
        relay_kernel,
        [((OWN + 2 * RELAY, 16, BLK), BF16, free())],
        [smem()] + [free()] * 3,
        [pltpu.SemaphoreType.DMA((3,))],
        1,
        16,
    )(first[3], own, plus, minus)[0]
    mate = swapped(relayed)

    middle = matrices([], [(plus, RELAY), (minus, RELAY)], 10)

    local, totals, f_home, f_mate, f_plus, f_minus, f_cross = call(
        solve_kernel,
        [
            ((8, NLON), F32, vmem()),
            ((peers, NBLK, BLK), BF16, vmem()),
            strip(HOME),
            strip(OFFCAP),
            strip(2 * OFFCAP),
            strip(2 * OFFCAP),
            strip(OFFCAP),
        ],
        [smem()] * 3 + [hbm()] + [free()] * 4,
        [
            pltpu.VMEM(helm_coef.shape, F32),
            pltpu.VMEM((6, HALO, 16, BLK), BF16),
            pltpu.VMEM((LOWS + 1, 16, BLK), BF16),
            pltpu.VMEM((6, 8, NLON), F32),
            pltpu.VMEM((6, 8, NLON), F32),
            pltpu.VMEM((2, 8, NLON), F32),
            pltpu.VMEM((1, BLK), jnp.int32),
            pltpu.SMEM((1, BLK), jnp.int32),
            pltpu.VMEM((SLOTS * 4, BLK), F32),
            pltpu.VMEM((SLOTS * 4, BLK), F32),
            pltpu.VMEM((NBLK, BLK), F32),
            pltpu.SemaphoreType.DMA((8,)),
            pltpu.SemaphoreType.DMA,
        ],
        2,
        24,
    )(me, slots, middle[3], kept(helm_coef), own, plus, minus, mate)
    above = lax.all_to_all(totals, "lev", 0, 0)
    f_plus = moved(f_plus, 2)
    f_minus = moved(f_minus, -2)
    f_cross = crossed(f_cross)

    late = matrices(
        [],
        [(cross, 0), (mate, HALO + LOWS + 1), (mate, OWN + HALO), (mate, OWN + RELAY + HALO)],
        4,
    )

    def lists(found):
        mats, entry_slot, entry_win, entry_count = found
        return entry_slot, entry_win, entry_count, kept(mats)

    listed = [smem()] * 3 + [hbm()]
    return call(
        spread_kernel,
        [((4, 4, CELLS), F32, vmem())],
        [smem()] * 2 + [hbm()] + listed * 3 + [free()] * 5 + [vmem()] * 7,
        [
            pltpu.SMEM((4,), F32),
            pltpu.VMEM((SLOTS, 16, BLK), BF16),
            pltpu.VMEM((SLOTS * 4 + 8, BLK), F32),
            pltpu.VMEM((16, CELLS + WIN), F32),
            pltpu.VMEM((3, RING, PACK, WIN, BLK), BF16),
            pltpu.SemaphoreType.DMA((GROUPS + 2,)),
            pltpu.SemaphoreType.DMA((3, RING)),
        ],
        4,
        24,
    )(
        me, lev, kept(geo_coef), *lists(first), *lists(middle), *lists(late),
        b_home, plus, minus, cross, mate, f_home, f_mate, f_plus, f_minus, f_cross, local, above,
    )[0]


def solution(mesh):
    placed = (
        P(None, "lev", "tile"),
        P("lev", "tile"),
        P("lev"),
        P("tile", None),
        P("tile"),
        P(None, "tile"),
        P(None, "tile"),
    )
    return jax.shard_map(
        body, mesh=mesh, in_specs=placed, out_specs=P(None, "lev", "tile"), check_vma=False
    )
```

```python
import jax
import jax.numpy as jnp
from jax import lax
from jax.experimental import pallas as pl
from jax.experimental.pallas import tpu as pltpu
from jax.sharding import PartitionSpec as P

NLON = 4096
BLK = 128
WIN = 256
SWEEPS = 4
REACH = 3
HOME = 32
OFFCAP = 16

F32 = jnp.float32
BF16 = jnp.bfloat16
STEN = 12
NBLK = 64
CELLS = 8192
NWIN = CELLS // WIN
OFFSETS = (-3, -2, -1, 1, 2, 3)
GROUPS = len(OFFSETS)
SLOTS = HOME + OFFCAP * GROUPS
HALO = NLON // BLK
ROUTE = 2 * STEN + 1
LOAD = ROUTE + OFFCAP
RELAY = HALO + LOAD
LOWS = HALO // 2
OWN = HALO + LOWS + 1 + LOAD
MIDDLE = 2 * OFFCAP
LATE = 3 * OFFCAP
CROSS = LOAD + 4
PACK = 4
RING = 8
REMAINDER = 1e-6


def vmem():
    return pl.BlockSpec(memory_space=pltpu.VMEM)


def smem():
    return pl.BlockSpec(memory_space=pltpu.SMEM)


def free():
    return pl.BlockSpec(memory_space=pl.ANY)


def hbm():
    return pl.BlockSpec(memory_space=pltpu.HBM)


def kept(array):
    return pltpu.with_memory_space_constraint(array, pltpu.HBM)


def lanes(i):
    return slice(i * BLK, (i + 1) * BLK)


def base_of(by):
    return 0 if by == 0 else HOME + OFFCAP * OFFSETS.index(by)


def either(core, first, second):
    return pl.multiple_of(jnp.where(core == 0, base_of(first), base_of(second)), OFFCAP)


def launch(copies):
    copies = [pltpu.make_async_copy(*copy) for copy in copies]
    for copy in copies:
        copy.start()
    return copies


def finish(copies):
    for copy in copies:
        copy.wait()


def call(kernel, outs, ins, scratch, cost, limit):
    return pl.pallas_call(
        kernel,
        out_shape=[(out[3] if out[3:] else jax.ShapeDtypeStruct)(out[0], out[1]) for out in outs],
        out_specs=[out[2] for out in outs],
        in_specs=ins,
        scratch_shapes=scratch,
        compiler_params=pltpu.CompilerParams(vmem_limit_bytes=limit << 20),
        cost_estimate=pl.CostEstimate(flops=cost * 1000000, bytes_accessed=cost * 3000000, transcendentals=0),
    )


def pack_kernel(
    me, dest_in, win_in, adj_in, helm_in, cell_in, weight_in,
    slots, a_home, b_home, own, plus, minus, cross,
    dest, win, adj, helm, cell, weight, count, a_all, b_all, sems,
):
    pairs = ((dest_in, dest), (win_in, win), (adj_in, adj), (helm_in, helm), (cell_in, cell), (weight_in, weight))
    copies = launch([(a, b, sems.at[i]) for i, (a, b) in enumerate(pairs)])
    core = lax.rem(me[0], 2)
    for by in range(-REACH, REACH + 1):
        count[by + REACH] = base_of(by)
    a_all[...] = jnp.zeros_like(a_all)
    b_all[...] = jnp.zeros_like(b_all)
    finish(copies)
    lane = lax.broadcasted_iota(jnp.int32, (16, BLK), 1)
    table = jnp.zeros((16, BLK), jnp.int32)
    for b in range(NBLK):
        route = dest[b] - me[0] + REACH
        slot = count[route]
        count[route] = slot + 1
        slots[b] = slot
        table = jnp.where(lane == b, slot, table)
        a_all[pl.ds(slot, STEN, stride=SLOTS), :] = weight[:, lanes(b)].astype(F32)
        a_all[pl.ds(STEN * SLOTS + slot, STEN, stride=SLOTS), :] = cell[:, lanes(b)].astype(F32)
        a_all[pl.ds(2 * STEN * SLOTS + slot, 1), :] = jnp.full((1, BLK), win[b] + 1, jnp.int32).astype(F32)
        b_all[slot] = jnp.concatenate([adj[f, :, lanes(b)].astype(F32) for f in range(4)], axis=0).astype(BF16)
    for r in range(ROUTE):
        a_home[r] = a_all[r * SLOTS : r * SLOTS + HOME, :].astype(BF16)
    b_home[...] = b_all[:HOME]
    loads = (
        (own, HALO + LOWS + 1, either(core, 1, -1)),
        (plus, HALO, either(core, 3, 1)),
        (plus, RELAY, either(core, 2, 2)),
        (minus, HALO, either(core, -1, -3)),
        (minus, RELAY, either(core, -2, -2)),
        (cross, 0, either(core, -3, 3)),
    )
    for parcel, at, base in loads:
        for r in range(ROUTE):
            parcel[at + r] = a_all[pl.ds(r * SLOTS + base, OFFCAP), :].astype(BF16)
        parcel[at + ROUTE : at + LOAD] = b_all[pl.ds(base, OFFCAP)]
    rest = []
    for i in range(HALO):
        coef = jnp.concatenate([helm[:, lanes(i)], helm[:, lanes(HALO + i)]], axis=0)
        rest.append(coef - coef.astype(BF16).astype(F32))
        first = [adj[0, :, lanes(i)].astype(F32), adj[0, :, lanes(HALO + i)].astype(F32)]
        piece = jnp.concatenate(first + [coef], axis=0).astype(BF16)
        for parcel in (own, plus, minus):
            parcel[i] = piece
    for i in range(LOWS):
        own[HALO + i] = jnp.concatenate(rest[2 * i : 2 * i + 2], axis=0).astype(BF16)
    own[HALO + LOWS] = table.astype(F32).astype(BF16)


def relay_kernel(_, own, plus, minus, out, sems):
    finish(
        launch(
            [
                (own, out.at[pl.ds(0, OWN)], sems.at[0]),
                (plus.at[pl.ds(0, RELAY)], out.at[pl.ds(OWN, RELAY)], sems.at[1]),
                (minus.at[pl.ds(0, RELAY)], out.at[pl.ds(OWN + RELAY, RELAY)], sems.at[2]),
            ]
        )
    )


def solve_kernel(
    me, slots, _, helm_in, own, plus, minus, mate, cross_in,
    local, totals, f_home, f_mate, f_plus, f_minus, cross,
    helm, halo, lows, rhs, coef, result, table, table_s, mine_all, mate_all, t_all, sems, table_sem,
):
    core = lax.rem(me[0], 2)
    tables = launch([(mate.at[pl.ds(HALO, LOWS + 1)], lows, sems.at[7])])
    passed = launch([(cross_in, cross.at[pl.ds(0, LOAD)], sems.at[8])])
    pairs = (
        (helm_in, helm),
        (plus.at[pl.ds(0, HALO)], halo.at[core]),
        (mate.at[pl.ds(OWN, HALO)], halo.at[1 - core]),
        (own.at[pl.ds(0, HALO)], halo.at[2 + core]),
        (mate.at[pl.ds(0, HALO)], halo.at[3 - core]),
        (minus.at[pl.ds(0, HALO)], halo.at[4 + core]),
        (mate.at[pl.ds(OWN + RELAY, HALO)], halo.at[5 - core]),
    )
    copies = launch([(a, b, sems.at[i]) for i, (a, b) in enumerate(pairs)])
    mine_all[...] = jnp.zeros_like(mine_all)
    mate_all[...] = jnp.zeros_like(mate_all)
    finish(tables)
    table[...] = lows[LOWS].astype(F32)[:1].astype(jnp.int32)
    tables = launch([(table, table_s, table_sem)])
    finish(copies)
    for band in range(6):
        for i in range(HALO):
            tile = halo[band, i].astype(F32)
            rhs[band, :, lanes(i)] = tile[:8]
            coef[band, :, lanes(i)] = tile[8:]
    for i in range(LOWS):
        tile = lows[i].astype(F32)
        coef[3 - core, :, lanes(2 * i)] += tile[:8]
        coef[3 - core, :, lanes(2 * i + 1)] += tile[8:]
    coef[2 + core] = jnp.concatenate([helm[:, :NLON], helm[:, NLON:]], axis=0)
    right = [rhs[band] for band in range(6)]
    factor = [coef[band] for band in range(6)]
    scale = [1.0 / (1.0 + 4.0 * c) for c in factor]
    solved = [r * s for r, s in zip(right, scale)]
    upper = lax.broadcasted_iota(jnp.int32, (8, NLON), 0) < 4
    for wanted in ((0, 1, 2, 3, 4, 5), (1, 2, 3, 4), (1, 2, 3, 4), (2, 3)):
        shifted = [c * s for c, s in zip(factor, solved)]
        turned = [pltpu.roll(p, 4, 0) for p in shifted]
        fresh = list(solved)
        for band in wanted:
            p = shifted[band]
            north = turned[max(band - 1, 0)]
            south = turned[min(band + 1, 5)]
            total = turned[band] + jnp.where(upper, north, south)
            total = total + pltpu.roll(p, 1, 1) + pltpu.roll(p, NLON - 1, 1)
            fresh[band] = (right[band] + total) * scale[band]
        solved = fresh
    result[0] = solved[2]
    result[1] = solved[3]
    mine = result[core]
    other = result[1 - core]
    finish(tables)
    for r in range(2):
        sums = mine[4 * r : 4 * r + 1]
        local[4 * r : 4 * r + 1, :] = sums
        for level in range(1, 4):
            sums = sums + mine[4 * r + level : 4 * r + level + 1]
            local[4 * r + level : 4 * r + level + 1, :] = sums
        for i in range(HALO):
            b = HALO * r + i
            t_all[b : b + 1, :] = sums[:, lanes(i)]
            mine_all[pl.ds(slots[b] * 4, 4), :] = mine[4 * r : 4 * r + 4, lanes(i)]
            mate_all[pl.ds(table_s[0, b] * 4, 4), :] = other[4 * r : 4 * r + 4, lanes(i)]
    totals_here = t_all[...].astype(BF16)
    for i in range(totals.shape[0]):
        totals[i] = totals_here

    def part(source, first, second):
        return source[pl.ds(either(core, first, second) * 4, OFFCAP * 4), :].astype(BF16)

    f_home[...] = mine_all[: HOME * 4].astype(BF16)
    f_mate[...] = part(mate_all, -1, 1)
    f_plus[: OFFCAP * 4] = part(mine_all, 2, 2)
    f_plus[OFFCAP * 4 :] = part(mate_all, 1, 3)
    f_minus[: OFFCAP * 4] = part(mine_all, -2, -2)
    f_minus[OFFCAP * 4 :] = part(mate_all, -3, -1)
    piece = part(mine_all, -3, 3)
    for i in range(4):
        cross[LOAD + i] = piece[16 * i : 16 * i + 16]
    finish(passed)


def merge(load, cells, merged, count, base):
    w = [load(k) for k in range(STEN)]
    c = [load(STEN + k) for k in range(STEN)]
    total = list(w)
    for k in range(STEN):
        for m in range(k):
            same = c[k] == c[m]
            total[k] = total[k] + jnp.where(same, w[m], 0.0)
            total[m] = total[m] + jnp.where(same, w[k], 0.0)
    lost = jnp.zeros((8, BLK), F32)
    held = jnp.zeros((8, BLK), F32)
    for k in range(STEN):
        high = total[k].astype(BF16).astype(F32)
        low = total[k] - high
        cells[k, base : base + 8, :] = c[k]
        merged[k, base : base + 8, :] = high
        merged[k, count + base : count + base + 8, :] = low
        lost = lost + low * low
        held = held + w[k] * w[k]
    more = jnp.sum(lost, axis=1, keepdims=True) > REMAINDER * jnp.sum(held, axis=1, keepdims=True)
    mark = load(2 * STEN)
    mark = jnp.where(mark > 0.0, mark + jnp.where(more, 64.0, 0.0), 0.0)
    lane = lax.broadcasted_iota(jnp.int32, (8, BLK), 1)
    row = lax.broadcasted_iota(jnp.int32, (8, BLK), 0)
    return jnp.where(lane == row + base, mark, 0.0)


def merge_all(groups, cells, merged, count, meta):
    marks = jnp.zeros((8, BLK), F32)
    for i, group in enumerate(groups):
        rows = group()
        for half in (0, 8):
            marks = marks + merge(lambda r: rows[r][half : half + 8], cells, merged, count, 16 * i + half)
    meta[...] = jnp.sum(marks, axis=0, keepdims=True).astype(jnp.int32)


def enlist(meta_s, count, entry_slot, entry_win):
    def eight(i, n):
        for j in range(8):
            slot = i * 8 + j
            mark = meta_s[0, slot]
            window = (mark & 63) - 1
            entry_slot[n] = slot
            entry_win[n] = window
            n = n + (mark > 0).astype(jnp.int32)
            entry_slot[n] = slot + count
            entry_win[n] = window
            n = n + (mark >= 64).astype(jnp.int32)
        return n

    n = lax.fori_loop(0, count // 8, eight, jnp.int32(0))
    for j in range(PACK):
        entry_slot[n + j] = 0
        entry_win[n + j] = NWIN
    return n


def build(group, cells, merged, count, entry_slot, target):
    iota = lax.broadcasted_iota(jnp.int32, (16, BLK), 0).astype(F32)
    for j in range(PACK):
        entry = entry_slot[group * PACK + j]
        slot = lax.rem(entry, count)
        c = [jnp.broadcast_to(cells[k, pl.ds(slot, 1), :], (16, BLK)).astype(BF16) for k in range(STEN)]
        w = [jnp.broadcast_to(merged[k, pl.ds(entry, 1), :], (16, BLK)).astype(BF16) for k in range(STEN)]
        for i in range(WIN // 16):
            here = (iota + 16.0 * i).astype(BF16)
            m = jnp.zeros((16, BLK), BF16)
            for k in range(STEN):
                m = jnp.where(c[k] == here, w[k], m)
            target[j, 16 * i : 16 * i + 16, :] = m


def multiply(group, slots, base, size, values, firsts, source):
    first_rows = lax.broadcasted_iota(jnp.int32, (8, BLK), 0) < 4
    products = []
    for j in range(PACK):
        slot = base + lax.rem(slots[group * PACK + j], size)
        tile = values[slot].astype(F32)
        head = jnp.where(first_rows, firsts[pl.ds(slot * 4, 8), :], tile[:8])
        left = jnp.concatenate([head, tile[8:]], axis=0).astype(BF16)
        products.append(lax.dot_general(left, source[j], (((1,), (1,)), ((), ())), preferred_element_type=F32))
    return products


def add_up(group, wins, total, products):
    for j in range(PACK):
        start = pl.multiple_of(wins[group * PACK + j] * WIN, WIN)
        total[:, pl.ds(start, WIN)] += products[j]


def groups_of(n):
    return (n + PACK - 1) // PACK


def ringed(ring, sems, mats, out):
    def copy(group):
        at = lax.rem(group, RING)
        far, near = mats.at[pl.ds(group * PACK, PACK)], ring.at[at]
        return pltpu.make_async_copy(*((near, far) if out else (far, near)), sems.at[at])

    return copy


def drain(stored, groups):
    for back in range(1, RING + 1):

        @pl.when(groups >= back)
        def _():
            stored(groups - back).wait()


def prefetch(fetched, groups):
    for g in range(RING):

        @pl.when(g < groups)
        def _():
            fetched(g).start()


def arrival(copy, tiles):
    def rows():
        copy.wait()
        return [tiles[r].astype(F32) for r in range(ROUTE)]

    return rows


def matrix_kernel(count, home, offsets, *refs):
    a_home = refs[0] if home else None
    parcels, refs = refs[home : home + len(offsets)], refs[home + len(offsets) :]
    mats, entry_slot, entry_win, entry_count, a_in, cells, merged, ring, meta, meta_s, sems, ring_sems, meta_sem = refs
    copies = launch([(p.at[pl.ds(at, ROUTE)], a_in.at[i], sems.at[i]) for i, (p, at) in enumerate(zip(parcels, offsets))])

    def own_rows(at):
        return lambda: [a_home[r, at : at + 16, :].astype(F32) for r in range(ROUTE)]

    parts = [own_rows(at) for at in range(0, HOME if home else 0, 16)]
    parts += [arrival(copy, a_in.at[i]) for i, copy in enumerate(copies)]
    merge_all(parts, cells, merged, count, meta)
    finish(launch([(meta, meta_s, meta_sem)]))
    n = enlist(meta_s, count, entry_slot, entry_win)
    entry_count[0] = n
    stored = ringed(ring, ring_sems, mats, True)

    def step(group, carry):
        @pl.when(group >= RING)
        def _():
            stored(group - RING).wait()

        build(group, cells, merged, count, entry_slot, ring.at[lax.rem(group, RING)])
        stored(group).start()
        return carry

    lax.fori_loop(0, groups_of(n), step, 0)
    drain(stored, groups_of(n))


def late_kernel(
    mate, slot1, win1, count1, mats1, b_home, f_home,
    mats, entry_slot, entry_win, entry_count, total,
    a_in, cells, merged, meta, meta_s, firsts, out_ring, in_ring, sems, out_sems, in_sems, meta_sem,
):
    offsets = (HALO + LOWS + 1, OWN + HALO, OWN + RELAY + HALO)
    copies = launch([(mate.at[pl.ds(at, ROUTE)], a_in.at[i], sems.at[i]) for i, at in enumerate(offsets)])
    stored = ringed(out_ring, out_sems, mats, True)
    fetched = ringed(in_ring, in_sems, mats1, False)
    home_groups = groups_of(count1[0])
    prefetch(fetched, home_groups)
    total[...] = jnp.zeros_like(total)
    firsts[: HOME * 4, :] = f_home[...].astype(F32)
    firsts[HOME * 4 :, :] = jnp.zeros((8, BLK), F32)
    merge_all([arrival(copy, a_in.at[i]) for i, copy in enumerate(copies)], cells, merged, LATE, meta)
    finish(launch([(meta, meta_s, meta_sem)]))
    n = enlist(meta_s, LATE, entry_slot, entry_win)
    entry_count[0] = n
    late_groups = groups_of(n)

    def step(building, multiplying):
        def run(group, carry):
            at = lax.rem(group, RING)
            if building:

                @pl.when(group >= RING)
                def _():
                    stored(group - RING).wait()

            if multiplying:
                fetched(group).wait()
                products = multiply(group, slot1, 0, HOME, b_home, firsts, in_ring.at[at])
            if building:
                build(group, cells, merged, LATE, entry_slot, out_ring.at[at])
            if multiplying:
                add_up(group, win1, total, products)

                @pl.when(group + RING < home_groups)
                def _():
                    fetched(group + RING).start()

            if building:
                stored(group).start()
            return carry

        return run

    both = jnp.minimum(home_groups, late_groups)
    lax.fori_loop(0, both, step(True, True), 0)
    lax.fori_loop(both, late_groups, step(True, False), 0)
    lax.fori_loop(both, home_groups, step(False, True), 0)
    drain(stored, late_groups)


def spread_kernel(
    lev, geo_in, slot2, win2, count2, mats2, slot3, win3, count3, mats3,
    plus, minus, cross, mate, f_mate, f_plus, f_minus, begun, local, above,
    out, geo, values, firsts, total, ring, a_in, cells, merged, meta, meta_s, entry_slot, entry_win, fresh,
    sems, ring_sems, meta_sem,
):
    routes = launch([(cross.at[pl.ds(0, ROUTE)], a_in, sems.at[GROUPS + 1])])
    parts = (
        (plus, RELAY + ROUTE),
        (minus, RELAY + ROUTE),
        (mate, HALO + LOWS + 1 + ROUTE),
        (mate, OWN + HALO + ROUTE),
        (mate, OWN + RELAY + HALO + ROUTE),
        (cross, ROUTE),
    )
    pairs = [(p.at[pl.ds(at, OFFCAP)], values.at[pl.ds(OFFCAP * i, OFFCAP)]) for i, (p, at) in enumerate(parts)]
    pairs += [(geo_in, geo)]
    copies = launch([(a, b, sems.at[i]) for i, (a, b) in enumerate(pairs)])
    loops = ((slot2, win2, count2, mats2, 0, MIDDLE), (slot3, win3, count3, mats3, MIDDLE, LATE))
    fetches = [ringed(ring.at[i], ring_sems.at[i], loop[3], False) for i, loop in enumerate(loops)]
    for fetched, loop in zip(fetches, loops):
        prefetch(fetched, groups_of(loop[2][0]))
    merge_all([arrival(routes[0], a_in)], cells, merged, OFFCAP, meta)
    metas = launch([(meta, meta_s, meta_sem)])

    total[...] = begun[...]
    half = OFFCAP * 4
    for i, piece in enumerate((f_plus[:half], f_minus[:half], f_mate[...], f_plus[half:], f_minus[half:])):
        firsts[half * i : half * (i + 1), :] = piece.astype(F32)
    for i in range(4):
        at = half * (GROUPS - 1) + 16 * i
        firsts[at : at + 16, :] = cross[LOAD + i].astype(F32)
    firsts[half * GROUPS :, :] = jnp.zeros((8, BLK), F32)
    finish(copies)

    for i, (fetched, (slots, wins, count, _, base, size)) in enumerate(zip(fetches, loops)):
        groups = groups_of(count[0])

        def step(group, carry):
            fetched(group).wait()
            products = multiply(group, slots, base, size, values, firsts, ring.at[i, lax.rem(group, RING)])
            add_up(group, wins, total, products)

            @pl.when(group + RING < groups)
            def _():
                fetched(group + RING).start()

            return carry

        lax.fori_loop(0, groups, step, 0)

    finish(metas)
    n = enlist(meta_s, OFFCAP, entry_slot, entry_win)

    def last(group, carry):
        build(group, cells, merged, OFFCAP, entry_slot, fresh)
        add_up(group, entry_win, total, multiply(group, entry_slot, MIDDLE + LATE, OFFCAP, values, firsts, fresh))
        return carry

    lax.fori_loop(0, groups_of(n), last, 0)

    sums = jnp.zeros((NBLK, BLK), F32)
    for peer in range(above.shape[0]):
        sums = sums + jnp.where(peer < lev[0], above[peer].astype(F32), 0.0)
    level = lax.broadcasted_iota(jnp.int32, (4, BLK), 0)
    factor = jnp.zeros((4, BLK), F32)
    for i in range(4):
        factor = jnp.where(level == i, geo[i], factor)
    for f in (0, 1, 3):
        out[f] = total[4 * f : 4 * f + 4, :CELLS]
    for b in range(NBLK):
        r = b // HALO
        term = factor * (local[4 * r : 4 * r + 4, lanes(b % HALO)] + sums[b : b + 1])
        out[2, :, lanes(b)] = total[8:12, lanes(b)] + term


def moved(parcel, by):
    peers = lax.axis_size("tile")
    return lax.ppermute(parcel, "tile", [(i, i + by) for i in range(peers) if 0 <= i + by < peers])


def swapped(parcel):
    return lax.ppermute(parcel, "tile", [(i, i ^ 1) for i in range(lax.axis_size("tile"))])


def crossed(parcel):
    peers = lax.axis_size("tile")
    pairs = [(i, i + (3 if i % 2 else -3)) for i in range(peers)]
    return lax.ppermute(parcel, "tile", [(i, j) for i, j in pairs if 0 <= j < peers])


def matrices(home, parts, cost):
    count = (HOME if home else 0) + OFFCAP * len(parts)
    entries = 2 * count
    return call(
        lambda *refs: matrix_kernel(count, len(home), [at for _, at in parts], *refs),
        [
            ((entries, WIN, BLK), BF16, hbm(), pltpu.HBM),
            ((entries + 8,), jnp.int32, smem()),
            ((entries + 8,), jnp.int32, smem()),
            ((1,), jnp.int32, smem()),
        ],
        [vmem()] * len(home) + [free()] * len(parts),
        [
            pltpu.VMEM((max(len(parts), 1), ROUTE, 16, BLK), BF16),
            pltpu.VMEM((STEN, count, BLK), F32),
            pltpu.VMEM((STEN, 2 * count, BLK), F32),
            pltpu.VMEM((RING, PACK, WIN, BLK), BF16),
            pltpu.VMEM((1, BLK), jnp.int32),
            pltpu.SMEM((1, BLK), jnp.int32),
            pltpu.SemaphoreType.DMA((max(len(parts), 1),)),
            pltpu.SemaphoreType.DMA((RING,)),
            pltpu.SemaphoreType.DMA,
        ],
        cost,
        16,
    )(*home, *[parcel for parcel, _ in parts])


def body(adj_in, helm_coef, geo_coef, dest_tile, src_window, src_cell, interp_w):
    me = lax.axis_index("tile").astype(jnp.int32)[None]
    lev = lax.axis_index("lev").astype(jnp.int32)[None]
    peers = lax.axis_size("lev")

    def parcel(entries):
        return ((entries, 16, BLK), BF16, vmem())

    def strip(blocks):
        return ((blocks * 4, BLK), BF16, vmem())

    slots, a_home, b_home, own, plus, minus, cross = call(
        pack_kernel,
        [
            ((NBLK,), jnp.int32, smem()),
            ((ROUTE, HOME, BLK), BF16, vmem()),
            parcel(HOME),
            parcel(OWN),
            parcel(RELAY + LOAD),
            parcel(RELAY + LOAD),
            parcel(LOAD),
        ],
        [smem()] + [hbm()] * 6,
        [
            pltpu.SMEM((NBLK,), jnp.int32),
            pltpu.SMEM((NBLK,), jnp.int32),
            pltpu.VMEM(adj_in.shape, BF16),
            pltpu.VMEM(helm_coef.shape, F32),
            pltpu.VMEM(src_cell.shape, jnp.int32),
            pltpu.VMEM(interp_w.shape, BF16),
            pltpu.SMEM((2 * REACH + 1,), jnp.int32),
            pltpu.VMEM((ROUTE * SLOTS, BLK), F32),
            pltpu.VMEM((SLOTS, 16, BLK), BF16),
            pltpu.SemaphoreType.DMA((6,)),
        ],
        1,
        24,
    )(me, *map(kept, (dest_tile[:, 0], src_window, adj_in, helm_coef, src_cell, interp_w)))
    plus = moved(plus, 2)
    minus = moved(minus, -2)
    first = matrices([a_home], [], 40)

    relayed = call(
        relay_kernel,
        [((OWN + 2 * RELAY, 16, BLK), BF16, free())],
        [smem()] + [free()] * 3,
        [pltpu.SemaphoreType.DMA((3,))],
        1,
        16,
    )(first[3], own, plus, minus)[0]
    mate = swapped(relayed)

    middle = matrices([], [(plus, RELAY), (minus, RELAY)], 10)

    local, totals, f_home, f_mate, f_plus, f_minus, cross = call(
        solve_kernel,
        [
            ((8, NLON), F32, vmem()),
            ((peers, NBLK, BLK), BF16, vmem()),
            strip(HOME),
            strip(OFFCAP),
            strip(2 * OFFCAP),
            strip(2 * OFFCAP),
            parcel(CROSS),
        ],
        [smem()] * 3 + [hbm()] + [free()] * 5,
        [
            pltpu.VMEM(helm_coef.shape, F32),
            pltpu.VMEM((6, HALO, 16, BLK), BF16),
            pltpu.VMEM((LOWS + 1, 16, BLK), BF16),
            pltpu.VMEM((6, 8, NLON), F32),
            pltpu.VMEM((6, 8, NLON), F32),
            pltpu.VMEM((2, 8, NLON), F32),
            pltpu.VMEM((1, BLK), jnp.int32),
            pltpu.SMEM((1, BLK), jnp.int32),
            pltpu.VMEM((SLOTS * 4, BLK), F32),
            pltpu.VMEM((SLOTS * 4, BLK), F32),
            pltpu.VMEM((NBLK, BLK), F32),
            pltpu.SemaphoreType.DMA((9,)),
            pltpu.SemaphoreType.DMA,
        ],
        2,
        24,
    )(me, slots, middle[3], kept(helm_coef), own, plus, minus, mate, cross)
    above = lax.all_to_all(totals, "lev", 0, 0)
    f_plus = moved(f_plus, 2)
    f_minus = moved(f_minus, -2)
    cross = crossed(cross)

    def lists(found):
        mats, entry_slot, entry_win, entry_count = found
        return entry_slot, entry_win, entry_count, kept(mats)

    listed = [smem()] * 3 + [hbm()]
    *late, begun = call(
        late_kernel,
        [
            ((2 * LATE, WIN, BLK), BF16, hbm(), pltpu.HBM),
            ((2 * LATE + 8,), jnp.int32, smem()),
            ((2 * LATE + 8,), jnp.int32, smem()),
            ((1,), jnp.int32, smem()),
            ((16, CELLS + WIN), F32, vmem()),
        ],
        [free()] + listed + [vmem()] * 2,
        [
            pltpu.VMEM((3, ROUTE, 16, BLK), BF16),
            pltpu.VMEM((STEN, LATE, BLK), F32),
            pltpu.VMEM((STEN, 2 * LATE, BLK), F32),
            pltpu.VMEM((1, BLK), jnp.int32),
            pltpu.SMEM((1, BLK), jnp.int32),
            pltpu.VMEM((HOME * 4 + 8, BLK), F32),
            pltpu.VMEM((RING, PACK, WIN, BLK), BF16),
            pltpu.VMEM((RING, PACK, WIN, BLK), BF16),
            pltpu.SemaphoreType.DMA((3,)),
            pltpu.SemaphoreType.DMA((RING,)),
            pltpu.SemaphoreType.DMA((RING,)),
            pltpu.SemaphoreType.DMA,
        ],
        4,
        24,
    )(mate, *lists(first), b_home, f_home)

    return call(
        spread_kernel,
        [((4, 4, CELLS), F32, vmem())],
        [smem(), hbm()] + listed * 2 + [free()] * 2 + [vmem(), free()] + [vmem()] * 6,
        [
            pltpu.SMEM((4,), F32),
            pltpu.VMEM((SLOTS - HOME, 16, BLK), BF16),
            pltpu.VMEM(((SLOTS - HOME) * 4 + 8, BLK), F32),
            pltpu.VMEM((16, CELLS + WIN), F32),
            pltpu.VMEM((2, RING, PACK, WIN, BLK), BF16),
            pltpu.VMEM((ROUTE, 16, BLK), BF16),
            pltpu.VMEM((STEN, OFFCAP, BLK), F32),
            pltpu.VMEM((STEN, 2 * OFFCAP, BLK), F32),
            pltpu.VMEM((1, BLK), jnp.int32),
            pltpu.SMEM((1, BLK), jnp.int32),
            pltpu.SMEM((2 * OFFCAP + 8,), jnp.int32),
            pltpu.SMEM((2 * OFFCAP + 8,), jnp.int32),
            pltpu.VMEM((PACK, WIN, BLK), BF16),
            pltpu.SemaphoreType.DMA((GROUPS + 2,)),
            pltpu.SemaphoreType.DMA((2, RING)),
            pltpu.SemaphoreType.DMA,
        ],
        4,
        24,
    )(
        lev, kept(geo_coef), *lists(middle), *lists(late),
        plus, minus, cross, mate, f_mate, f_plus, f_minus, begun, local, above,
    )[0]


def solution(mesh):
    placed = (
        P(None, "lev", "tile"),
        P("lev", "tile"),
        P("lev"),
        P("tile", None),
        P("tile"),
        P(None, "tile"),
        P(None, "tile"),
    )
    return jax.shard_map(
        body, mesh=mesh, in_specs=placed, out_specs=P(None, "lev", "tile"), check_vma=False
    )
```

```python
import jax
import jax.numpy as jnp
from jax import lax
from jax.experimental import pallas as pl
from jax.experimental.pallas import tpu as pltpu
from jax.sharding import PartitionSpec as P

NLON = 4096
BLK = 128
WIN = 256
SWEEPS = 4
REACH = 3
HOME = 32
OFFCAP = 16

F32 = jnp.float32
BF16 = jnp.bfloat16
STEN = 12
NBLK = 64
CELLS = 8192
NWIN = CELLS // WIN
OFFSETS = (-3, -2, -1, 1, 2, 3)
SLOTS = HOME + OFFCAP * len(OFFSETS)
HALO = NLON // BLK
ROUTE = 2 * STEN + 1
LOAD = ROUTE + OFFCAP
LOWS = HALO // 2
MATE = HALO + LOWS + 1
MATE_PLUS = MATE + LOAD
MATE_MINUS = MATE_PLUS + LOAD
RELAY_PLUS = MATE_MINUS + LOAD
RELAY_MINUS = RELAY_PLUS + HALO
OWN = RELAY_MINUS + HALO
NEAR = HOME + OFFCAP
FAR = 5 * OFFCAP
CROSS = LOAD + 4
PAIR = 2 * LOAD + 8
PACK = 4
REMAINDER = 1e-6


def vmem():
    return pl.BlockSpec(memory_space=pltpu.VMEM)


def smem():
    return pl.BlockSpec(memory_space=pltpu.SMEM)


def free():
    return pl.BlockSpec(memory_space=pl.ANY)


def hbm():
    return pl.BlockSpec(memory_space=pltpu.HBM)


def kept(array):
    return pltpu.with_memory_space_constraint(array, pltpu.HBM)


def lanes(i):
    return slice(i * BLK, (i + 1) * BLK)


def base_of(by):
    return 0 if by == 0 else HOME + OFFCAP * OFFSETS.index(by)


def either(core, first, second):
    return pl.multiple_of(jnp.where(core == 0, base_of(first), base_of(second)), OFFCAP)


def launch(copies):
    copies = [pltpu.make_async_copy(*copy) for copy in copies]
    for copy in copies:
        copy.start()
    return copies


def finish(copies):
    for copy in copies:
        copy.wait()


def call(kernel, outs, ins, scratch, cost, limit, aliases=None):
    return pl.pallas_call(
        kernel,
        out_shape=[(out[3] if out[3:] else jax.ShapeDtypeStruct)(out[0], out[1]) for out in outs],
        out_specs=[out[2] for out in outs],
        in_specs=ins,
        scratch_shapes=scratch,
        input_output_aliases=aliases or {},
        compiler_params=pltpu.CompilerParams(vmem_limit_bytes=limit << 20),
        cost_estimate=pl.CostEstimate(flops=cost * 1000000, bytes_accessed=cost * 3000000, transcendentals=0),
    )


def halo_pieces(first, helm):
    for i in range(HALO):
        coef = jnp.concatenate([helm[:, lanes(i)], helm[:, lanes(HALO + i)]], axis=0)
        side = [first[:, lanes(i)].astype(F32), first[:, lanes(HALO + i)].astype(F32)]
        yield i, coef, jnp.concatenate(side + [coef], axis=0).astype(BF16)


def halo_kernel(adj_in, helm_in, out, first, helm, sems):
    finish(launch([(adj_in.at[0], first, sems.at[0]), (helm_in, helm, sems.at[1])]))
    for i, _, piece in halo_pieces(first, helm):
        out[i] = piece


def pack_kernel(
    me, dest_in, win_in, adj_in, helm_in, cell_in, weight_in,
    slots, a_home, b_home, own, plus, minus, cross,
    dest, win, adj, helm, cell, weight, count, a_all, b_all, sems,
):
    pairs = ((dest_in, dest), (win_in, win), (adj_in, adj), (helm_in, helm), (cell_in, cell), (weight_in, weight))
    copies = launch([(a, b, sems.at[i]) for i, (a, b) in enumerate(pairs)])
    core = lax.rem(me[0], 2)
    for by in range(-REACH, REACH + 1):
        count[by + REACH] = base_of(by)
    a_all[...] = jnp.zeros_like(a_all)
    b_all[...] = jnp.zeros_like(b_all)
    finish(copies)
    lane = lax.broadcasted_iota(jnp.int32, (16, BLK), 1)
    table = jnp.zeros((16, BLK), jnp.int32)
    for b in range(NBLK):
        route = dest[b] - me[0] + REACH
        slot = count[route]
        count[route] = slot + 1
        slots[b] = slot
        table = jnp.where(lane == b, slot, table)
        a_all[pl.ds(slot, STEN, stride=SLOTS), :] = weight[:, lanes(b)].astype(F32)
        a_all[pl.ds(STEN * SLOTS + slot, STEN, stride=SLOTS), :] = cell[:, lanes(b)].astype(F32)
        a_all[pl.ds(2 * STEN * SLOTS + slot, 1), :] = jnp.full((1, BLK), win[b] + 1, jnp.int32).astype(F32)
        b_all[slot] = jnp.concatenate([adj[f, :, lanes(b)].astype(F32) for f in range(4)], axis=0).astype(BF16)
    for r in range(ROUTE):
        a_home[r] = a_all[r * SLOTS : r * SLOTS + HOME, :].astype(BF16)
    b_home[...] = b_all[:HOME]
    loads = (
        (own, MATE, either(core, 1, -1)),
        (own, MATE_PLUS, either(core, 3, 1)),
        (own, MATE_MINUS, either(core, -1, -3)),
        (plus, 0, either(core, 2, 2)),
        (minus, 0, either(core, -2, -2)),
        (cross, 0, either(core, -3, 3)),
    )
    for parcel, at, base in loads:
        for r in range(ROUTE):
            parcel[at + r] = a_all[pl.ds(r * SLOTS + base, OFFCAP), :].astype(BF16)
        parcel[at + ROUTE : at + LOAD] = b_all[pl.ds(base, OFFCAP)]
    rest = []
    for i, coef, piece in halo_pieces(adj.at[0], helm):
        rest.append(coef - coef.astype(BF16).astype(F32))
        own[i] = piece
    for i in range(LOWS):
        own[HALO + i] = jnp.concatenate(rest[2 * i : 2 * i + 2], axis=0).astype(BF16)
    own[HALO + LOWS] = table.astype(F32).astype(BF16)
    own[RELAY_PLUS:] = jnp.zeros((2 * HALO, 16, BLK), BF16)


def relay_kernel(_, plus, minus, out, sems):
    finish(
        launch(
            [
                (plus, out.at[pl.ds(RELAY_PLUS, HALO)], sems.at[0]),
                (minus, out.at[pl.ds(RELAY_MINUS, HALO)], sems.at[1]),
            ]
        )
    )


def solve_kernel(
    me, slots, helm_in, own, plus, minus, mate, plus_in, minus_in, cross_in,
    local, totals, f_home, f_mate, f_plus, f_minus, cross,
    helm, halo, lows, rhs, coef, result, table, table_s, mine_all, mate_all, t_all, sems, table_sem,
):
    core = lax.rem(me[0], 2)
    tables = launch([(mate.at[pl.ds(HALO, LOWS + 1)], lows, sems.at[7])])
    forward = (
        (plus_in, f_plus.at[pl.ds(0, LOAD)]),
        (mate.at[pl.ds(MATE_PLUS, LOAD)], f_plus.at[pl.ds(LOAD, LOAD)]),
        (minus_in, f_minus.at[pl.ds(0, LOAD)]),
        (mate.at[pl.ds(MATE_MINUS, LOAD)], f_minus.at[pl.ds(LOAD, LOAD)]),
        (cross_in, cross.at[pl.ds(0, LOAD)]),
    )
    pairs = (
        (helm_in, helm),
        (plus, halo.at[core]),
        (mate.at[pl.ds(RELAY_PLUS, HALO)], halo.at[1 - core]),
        (own, halo.at[2 + core]),
        (mate.at[pl.ds(0, HALO)], halo.at[3 - core]),
        (minus, halo.at[4 + core]),
        (mate.at[pl.ds(RELAY_MINUS, HALO)], halo.at[5 - core]),
    )
    copies = launch([(a, b, sems.at[i]) for i, (a, b) in enumerate(pairs)])
    passed = launch([(a, b, sems.at[8 + i]) for i, (a, b) in enumerate(forward)])
    mine_all[...] = jnp.zeros_like(mine_all)
    mate_all[...] = jnp.zeros_like(mate_all)
    finish(tables)
    table[...] = lows[LOWS].astype(F32)[:1].astype(jnp.int32)
    tables = launch([(table, table_s, table_sem)])
    finish(copies)
    for band in range(6):
        for i in range(HALO):
            tile = halo[band, i].astype(F32)
            rhs[band, :, lanes(i)] = tile[:8]
            coef[band, :, lanes(i)] = tile[8:]
    for i in range(LOWS):
        tile = lows[i].astype(F32)
        coef[3 - core, :, lanes(2 * i)] += tile[:8]
        coef[3 - core, :, lanes(2 * i + 1)] += tile[8:]
    coef[2 + core] = jnp.concatenate([helm[:, :NLON], helm[:, NLON:]], axis=0)
    right = [rhs[band] for band in range(6)]
    factor = [coef[band] for band in range(6)]
    scale = [1.0 / (1.0 + 4.0 * c) for c in factor]
    solved = [r * s for r, s in zip(right, scale)]
    upper = lax.broadcasted_iota(jnp.int32, (8, NLON), 0) < 4
    for wanted in ((0, 1, 2, 3, 4, 5), (1, 2, 3, 4), (1, 2, 3, 4), (2, 3)):
        shifted = [c * s for c, s in zip(factor, solved)]
        turned = [pltpu.roll(p, 4, 0) for p in shifted]
        fresh = list(solved)
        for band in wanted:
            p = shifted[band]
            north = turned[max(band - 1, 0)]
            south = turned[min(band + 1, 5)]
            total = turned[band] + jnp.where(upper, north, south)
            total = total + pltpu.roll(p, 1, 1) + pltpu.roll(p, NLON - 1, 1)
            fresh[band] = (right[band] + total) * scale[band]
        solved = fresh
    result[0] = solved[2]
    result[1] = solved[3]
    mine = result[core]
    other = result[1 - core]
    finish(tables)
    for r in range(2):
        sums = mine[4 * r : 4 * r + 1]
        local[4 * r : 4 * r + 1, :] = sums
        for level in range(1, 4):
            sums = sums + mine[4 * r + level : 4 * r + level + 1]
            local[4 * r + level : 4 * r + level + 1, :] = sums
        for i in range(HALO):
            b = HALO * r + i
            t_all[b : b + 1, :] = sums[:, lanes(i)]
            mine_all[pl.ds(slots[b] * 4, 4), :] = mine[4 * r : 4 * r + 4, lanes(i)]
            mate_all[pl.ds(table_s[0, b] * 4, 4), :] = other[4 * r : 4 * r + 4, lanes(i)]
    totals_here = t_all[...].astype(BF16)
    for i in range(totals.shape[0]):
        totals[i] = totals_here

    def part(source, first, second):
        return source[pl.ds(either(core, first, second) * 4, OFFCAP * 4), :].astype(BF16)

    f_home[...] = mine_all[: HOME * 4].astype(BF16)
    f_mate[...] = part(mate_all, -1, 1)
    sent = (
        (f_plus, 2 * LOAD, part(mine_all, 2, 2)),
        (f_plus, 2 * LOAD + 4, part(mate_all, 1, 3)),
        (f_minus, 2 * LOAD, part(mine_all, -2, -2)),
        (f_minus, 2 * LOAD + 4, part(mate_all, -3, -1)),
        (cross, LOAD, part(mine_all, -3, 3)),
    )
    for parcel, at, piece in sent:
        for i in range(4):
            parcel[at + i] = piece[16 * i : 16 * i + 16]
    finish(passed)


def merge(load, cells, merged, count, base):
    w = [load(k) for k in range(STEN)]
    c = [load(STEN + k) for k in range(STEN)]
    total = list(w)
    for k in range(STEN):
        for m in range(k):
            same = c[k] == c[m]
            total[k] = total[k] + jnp.where(same, w[m], 0.0)
            total[m] = total[m] + jnp.where(same, w[k], 0.0)
    lost = jnp.zeros((8, BLK), F32)
    held = jnp.zeros((8, BLK), F32)
    for k in range(STEN):
        high = total[k].astype(BF16).astype(F32)
        low = total[k] - high
        cells[k, base : base + 8, :] = c[k]
        merged[k, base : base + 8, :] = high
        merged[k, count + base : count + base + 8, :] = low
        lost = lost + low * low
        held = held + w[k] * w[k]
    more = jnp.sum(lost, axis=1, keepdims=True) > REMAINDER * jnp.sum(held, axis=1, keepdims=True)
    mark = load(2 * STEN)
    mark = jnp.where(mark > 0.0, mark + jnp.where(more, 64.0, 0.0), 0.0)
    lane = lax.broadcasted_iota(jnp.int32, (8, BLK), 1)
    row = lax.broadcasted_iota(jnp.int32, (8, BLK), 0)
    return jnp.where(lane == row + base, mark, 0.0)


def merge_all(groups, cells, merged, count, meta):
    marks = jnp.zeros((8, BLK), F32)
    for i, group in enumerate(groups):
        rows = group()
        for half in (0, 8):
            marks = marks + merge(lambda r: rows[r][half : half + 8], cells, merged, count, 16 * i + half)
    meta[...] = jnp.sum(marks, axis=0, keepdims=True).astype(jnp.int32)


def enlist(meta_s, count, entry_slot, entry_win):
    def eight(i, n):
        for j in range(8):
            slot = i * 8 + j
            mark = meta_s[0, slot]
            window = (mark & 63) - 1
            entry_slot[n + 1] = slot
            entry_win[n + 1] = window
            n = n + (mark > 0).astype(jnp.int32)
            entry_slot[n + 1] = slot + count
            entry_win[n + 1] = window
            n = n + (mark >= 64).astype(jnp.int32)
        return n

    n = lax.fori_loop(0, count // 8, eight, jnp.int32(0))
    for at in [0] + [n + 1 + j for j in range(PACK)]:
        entry_slot[at] = 0
        entry_win[at] = NWIN
    return n


def spread(parts, count, cells, merged, meta, meta_s, entry_slot, entry_win, values, firsts, mats, total, meta_sem, ready):
    merge_all(parts, cells, merged, count, meta)
    finish(launch([(meta, meta_s, meta_sem)]))
    n = enlist(meta_s, count, entry_slot, entry_win)
    ready()
    iota = lax.broadcasted_iota(jnp.int32, (16, BLK), 0).astype(F32)
    first_rows = lax.broadcasted_iota(jnp.int32, (8, BLK), 0) < 4
    mats[PACK - 1] = jnp.zeros((WIN, BLK), BF16)

    def multiply(at, mat):
        slot = lax.rem(entry_slot[at], count)
        tile = values[slot].astype(F32)
        head = jnp.where(first_rows, firsts[pl.ds(slot * 4, 8), :], tile[:8])
        left = jnp.concatenate([head, tile[8:]], axis=0).astype(BF16)
        return lax.dot_general(left, mat[...], (((1,), (1,)), ((), ())), preferred_element_type=F32)

    def build(at, mat):
        entry = entry_slot[at]
        slot = lax.rem(entry, count)
        c = [jnp.broadcast_to(cells[k, pl.ds(slot, 1), :], (16, BLK)).astype(BF16) for k in range(STEN)]
        w = [jnp.broadcast_to(merged[k, pl.ds(entry, 1), :], (16, BLK)).astype(BF16) for k in range(STEN)]
        for i in range(WIN // 16):
            here = (iota + 16.0 * i).astype(BF16)
            m = jnp.zeros((16, BLK), BF16)
            for k in range(STEN):
                m = jnp.where(c[k] == here, w[k], m)
            mat[16 * i : 16 * i + 16, :] = m

    def add(at, product):
        start = pl.multiple_of(entry_win[at] * WIN, WIN)
        total[:, pl.ds(start, WIN)] += product

    def step(group, carry):
        for j in range(PACK):
            at = group * PACK + j
            product = multiply(at, mats.at[(j - 1) % PACK])
            build(at + 1, mats.at[j])
            add(at, product)
        return carry

    groups = (n + PACK - 1) // PACK
    lax.fori_loop(0, groups, step, 0)
    add(groups * PACK, multiply(groups * PACK, mats.at[PACK - 1]))


def spread_scratch(count):
    return [
        pltpu.VMEM((STEN, count, BLK), F32),
        pltpu.VMEM((STEN, 2 * count, BLK), F32),
        pltpu.VMEM((1, BLK), jnp.int32),
        pltpu.SMEM((1, BLK), jnp.int32),
        pltpu.SMEM((2 * count + 8,), jnp.int32),
        pltpu.SMEM((2 * count + 8,), jnp.int32),
        pltpu.VMEM((count, 16, BLK), BF16),
        pltpu.VMEM((count * 4 + 8, BLK), F32),
        pltpu.VMEM((PACK, WIN, BLK), BF16),
    ]


def arrival(copy, tiles):
    def rows():
        copy.wait()
        return [tiles[r].astype(F32) for r in range(ROUTE)]

    return rows


def near_kernel(
    mate, a_home, b_home, f_home, f_mate, total,
    a_in, cells, merged, meta, meta_s, entry_slot, entry_win, values, firsts, mats, sems, meta_sem,
):
    routes = launch([(mate.at[pl.ds(MATE, ROUTE)], a_in, sems.at[0])])
    copies = launch([(mate.at[pl.ds(MATE + ROUTE, OFFCAP)], values.at[pl.ds(HOME, OFFCAP)], sems.at[1])])
    total[...] = jnp.zeros_like(total)
    values[:HOME] = b_home[...]
    firsts[: HOME * 4, :] = f_home[...].astype(F32)
    firsts[HOME * 4 : NEAR * 4, :] = f_mate[...].astype(F32)
    firsts[NEAR * 4 :, :] = jnp.zeros((8, BLK), F32)

    def own_rows(at):
        return lambda: [a_home[r, at : at + 16, :].astype(F32) for r in range(ROUTE)]

    parts = [own_rows(at) for at in range(0, HOME, 16)] + [arrival(routes[0], a_in)]
    spread(
        parts, NEAR, cells, merged, meta, meta_s, entry_slot, entry_win, values, firsts, mats, total, meta_sem,
        lambda: finish(copies),
    )


def far_kernel(
    lev, geo_in, plus, minus, cross, begun, local, above,
    out, geo, total, a_in, cells, merged, meta, meta_s, entry_slot, entry_win, values, firsts, mats, sems, meta_sem,
):
    parts = (
        (plus, 0, 2 * LOAD),
        (plus, LOAD, 2 * LOAD + 4),
        (minus, 0, 2 * LOAD),
        (minus, LOAD, 2 * LOAD + 4),
        (cross, 0, LOAD),
    )
    count = len(parts)
    routes = launch([(p.at[pl.ds(at, ROUTE)], a_in.at[i], sems.at[i]) for i, (p, at, _) in enumerate(parts)])
    pairs = [
        (p.at[pl.ds(at + ROUTE, OFFCAP)], values.at[pl.ds(OFFCAP * i, OFFCAP)]) for i, (p, at, _) in enumerate(parts)
    ]
    pairs += [(geo_in, geo)]
    copies = launch([(a, b, sems.at[count + i]) for i, (a, b) in enumerate(pairs)])
    total[...] = begun[...]
    for i, (p, _, at) in enumerate(parts):
        for j in range(4):
            row = OFFCAP * 4 * i + 16 * j
            firsts[row : row + 16, :] = p[at + j].astype(F32)
    firsts[FAR * 4 :, :] = jnp.zeros((8, BLK), F32)
    spread(
        [arrival(copy, a_in.at[i]) for i, copy in enumerate(routes)],
        FAR, cells, merged, meta, meta_s, entry_slot, entry_win, values, firsts, mats, total, meta_sem,
        lambda: finish(copies),
    )

    sums = jnp.zeros((NBLK, BLK), F32)
    for peer in range(above.shape[0]):
        sums = sums + jnp.where(peer < lev[0], above[peer].astype(F32), 0.0)
    level = lax.broadcasted_iota(jnp.int32, (4, BLK), 0)
    factor = jnp.zeros((4, BLK), F32)
    for i in range(4):
        factor = jnp.where(level == i, geo[i], factor)
    for f in (0, 1, 3):
        out[f] = total[4 * f : 4 * f + 4, :CELLS]
    for b in range(NBLK):
        r = b // HALO
        term = factor * (local[4 * r : 4 * r + 4, lanes(b % HALO)] + sums[b : b + 1])
        out[2, :, lanes(b)] = total[8:12, lanes(b)] + term


def moved(parcel, by):
    peers = lax.axis_size("tile")
    return lax.ppermute(parcel, "tile", [(i, i + by) for i in range(peers) if 0 <= i + by < peers])


def swapped(parcel):
    return lax.ppermute(parcel, "tile", [(i, i ^ 1) for i in range(lax.axis_size("tile"))])


def crossed(parcel):
    peers = lax.axis_size("tile")
    pairs = [(i, i + (3 if i % 2 else -3)) for i in range(peers)]
    return lax.ppermute(parcel, "tile", [(i, j) for i, j in pairs if 0 <= j < peers])


def body(adj_in, helm_coef, geo_coef, dest_tile, src_window, src_cell, interp_w):
    me = lax.axis_index("tile").astype(jnp.int32)[None]
    lev = lax.axis_index("lev").astype(jnp.int32)[None]
    peers = lax.axis_size("lev")

    def parcel(entries):
        return ((entries, 16, BLK), BF16, vmem())

    def strip(blocks):
        return ((blocks * 4, BLK), BF16, vmem())

    halo = call(
        halo_kernel,
        [parcel(HALO)],
        [hbm()] * 2,
        [pltpu.VMEM(adj_in.shape[1:], BF16), pltpu.VMEM(helm_coef.shape, F32), pltpu.SemaphoreType.DMA((2,))],
        1,
        16,
    )(kept(adj_in), kept(helm_coef))[0]
    plus = moved(halo, 2)
    minus = moved(halo, -2)

    slots, a_home, b_home, own, same_plus, same_minus, cross = call(
        pack_kernel,
        [
            ((NBLK,), jnp.int32, smem()),
            ((ROUTE, HOME, BLK), BF16, vmem()),
            parcel(HOME),
            parcel(OWN),
            parcel(LOAD),
            parcel(LOAD),
            parcel(LOAD),
        ],
        [smem()] + [hbm()] * 6,
        [
            pltpu.SMEM((NBLK,), jnp.int32),
            pltpu.SMEM((NBLK,), jnp.int32),
            pltpu.VMEM(adj_in.shape, BF16),
            pltpu.VMEM(helm_coef.shape, F32),
            pltpu.VMEM(src_cell.shape, jnp.int32),
            pltpu.VMEM(interp_w.shape, BF16),
            pltpu.SMEM((2 * REACH + 1,), jnp.int32),
            pltpu.VMEM((ROUTE * SLOTS, BLK), F32),
            pltpu.VMEM((SLOTS, 16, BLK), BF16),
            pltpu.SemaphoreType.DMA((6,)),
        ],
        20,
        24,
    )(me, *map(kept, (dest_tile[:, 0], src_window, adj_in, helm_coef, src_cell, interp_w)))

    relayed = call(
        relay_kernel,
        [((OWN, 16, BLK), BF16, free())],
        [free()] * 3,
        [pltpu.SemaphoreType.DMA((2,))],
        1,
        16,
        {0: 0},
    )(own, plus, minus)[0]
    mate = swapped(relayed)

    local, totals, f_home, f_mate, f_plus, f_minus, cross = call(
        solve_kernel,
        [
            ((8, NLON), F32, vmem()),
            ((peers, NBLK, BLK), BF16, vmem()),
            strip(HOME),
            strip(OFFCAP),
            parcel(PAIR),
            parcel(PAIR),
            parcel(CROSS),
        ],
        [smem()] * 2 + [hbm()] + [free()] * 7,
        [
            pltpu.VMEM(helm_coef.shape, F32),
            pltpu.VMEM((6, HALO, 16, BLK), BF16),
            pltpu.VMEM((LOWS + 1, 16, BLK), BF16),
            pltpu.VMEM((6, 8, NLON), F32),
            pltpu.VMEM((6, 8, NLON), F32),
            pltpu.VMEM((2, 8, NLON), F32),
            pltpu.VMEM((1, BLK), jnp.int32),
            pltpu.SMEM((1, BLK), jnp.int32),
            pltpu.VMEM((SLOTS * 4, BLK), F32),
            pltpu.VMEM((SLOTS * 4, BLK), F32),
            pltpu.VMEM((NBLK, BLK), F32),
            pltpu.SemaphoreType.DMA((13,)),
            pltpu.SemaphoreType.DMA,
        ],
        2,
        24,
    )(me, slots, kept(helm_coef), halo, plus, minus, mate, same_plus, same_minus, cross)
    f_plus = moved(f_plus, 2)
    f_minus = moved(f_minus, -2)
    cross = crossed(cross)
    above = lax.all_to_all(totals, "lev", 0, 0)

    begun = call(
        near_kernel,
        [((16, CELLS + WIN), F32, vmem())],
        [free()] + [vmem()] * 4,
        [pltpu.VMEM((ROUTE, 16, BLK), BF16)]
        + spread_scratch(NEAR)
        + [pltpu.SemaphoreType.DMA((2,)), pltpu.SemaphoreType.DMA],
        8,
        16,
    )(mate, a_home, b_home, f_home, f_mate)[0]

    return call(
        far_kernel,
        [((4, 4, CELLS), F32, vmem())],
        [smem(), hbm()] + [vmem()] * 6,
        [
            pltpu.SMEM((4,), F32),
            pltpu.VMEM((16, CELLS + WIN), F32),
            pltpu.VMEM((5, ROUTE, 16, BLK), BF16),
        ]
        + spread_scratch(FAR)
        + [pltpu.SemaphoreType.DMA((11,)), pltpu.SemaphoreType.DMA],
        4,
        16,
    )(lev, kept(geo_coef), f_plus, f_minus, cross, begun, local, above)[0]


def solution(mesh):
    placed = (
        P(None, "lev", "tile"),
        P("lev", "tile"),
        P("lev"),
        P("tile", None),
        P("tile"),
        P(None, "tile"),
        P(None, "tile"),
    )
    return jax.shard_map(
        body, mesh=mesh, in_specs=placed, out_specs=P(None, "lev", "tile"), check_vma=False
    )
```

```python
import jax
import jax.numpy as jnp
from jax import lax
from jax.experimental import pallas as pl
from jax.experimental.pallas import tpu as pltpu
from jax.sharding import PartitionSpec as P

NLON = 4096
BLK = 128
WIN = 256
SWEEPS = 4
REACH = 3
HOME = 32
OFFCAP = 16

F32 = jnp.float32
BF16 = jnp.bfloat16
STEN = 12
NBLK = 64
CELLS = 8192
NWIN = CELLS // WIN
OFFSETS = (-3, -2, -1, 1, 2, 3)
SLOTS = HOME + OFFCAP * len(OFFSETS)
HALO = NLON // BLK
ROUTE = 2 * STEN + 1
LOAD = ROUTE + OFFCAP
LOWS = HALO // 2
MATE = HALO + LOWS + 1
MATE_PLUS = MATE + LOAD
MATE_MINUS = MATE_PLUS + LOAD
RELAY_PLUS = MATE_MINUS + LOAD
RELAY_MINUS = RELAY_PLUS + HALO
OWN = RELAY_MINUS + HALO
NEAR = HOME + OFFCAP
FAR = 5 * OFFCAP
CROSS = LOAD + 4
PAIR = 2 * LOAD + 8
PACK = 8
REMAINDER = 1e-6


def vmem():
    return pl.BlockSpec(memory_space=pltpu.VMEM)


def smem():
    return pl.BlockSpec(memory_space=pltpu.SMEM)


def free():
    return pl.BlockSpec(memory_space=pl.ANY)


def hbm():
    return pl.BlockSpec(memory_space=pltpu.HBM)


def kept(array):
    return pltpu.with_memory_space_constraint(array, pltpu.HBM)


def lanes(i):
    return slice(i * BLK, (i + 1) * BLK)


def base_of(by):
    return 0 if by == 0 else HOME + OFFCAP * OFFSETS.index(by)


def either(core, first, second):
    return pl.multiple_of(jnp.where(core == 0, base_of(first), base_of(second)), OFFCAP)


def launch(copies):
    copies = [pltpu.make_async_copy(*copy) for copy in copies]
    for copy in copies:
        copy.start()
    return copies


def finish(copies):
    for copy in copies:
        copy.wait()


def call(kernel, outs, ins, scratch, cost, limit, aliases=None):
    return pl.pallas_call(
        kernel,
        out_shape=[(out[3] if out[3:] else jax.ShapeDtypeStruct)(out[0], out[1]) for out in outs],
        out_specs=[out[2] for out in outs],
        in_specs=ins,
        scratch_shapes=scratch,
        input_output_aliases=aliases or {},
        compiler_params=pltpu.CompilerParams(vmem_limit_bytes=limit << 20),
        cost_estimate=pl.CostEstimate(flops=cost * 1000000, bytes_accessed=cost * 3000000, transcendentals=0),
    )


def halo_pieces(first, helm):
    for i in range(HALO):
        coef = jnp.concatenate([helm[:, lanes(i)], helm[:, lanes(HALO + i)]], axis=0)
        side = [first[:, lanes(i)].astype(F32), first[:, lanes(HALO + i)].astype(F32)]
        yield i, coef, jnp.concatenate(side + [coef], axis=0).astype(BF16)


def halo_kernel(adj_in, helm_in, out, first, helm, sems):
    finish(launch([(adj_in.at[0], first, sems.at[0]), (helm_in, helm, sems.at[1])]))
    for i, _, piece in halo_pieces(first, helm):
        out[i] = piece


def pack_kernel(
    me, dest_in, win_in, adj_in, helm_in, cell_in, weight_in,
    slots, a_home, b_home, own, plus, minus, cross,
    dest, win, adj, helm, cell, weight, count, a_all, b_all, sems,
):
    pairs = ((dest_in, dest), (win_in, win), (adj_in, adj), (helm_in, helm), (cell_in, cell), (weight_in, weight))
    copies = launch([(a, b, sems.at[i]) for i, (a, b) in enumerate(pairs)])
    core = lax.rem(me[0], 2)
    for by in range(-REACH, REACH + 1):
        count[by + REACH] = base_of(by)
    a_all[...] = jnp.zeros_like(a_all)
    b_all[...] = jnp.zeros_like(b_all)
    finish(copies)
    lane = lax.broadcasted_iota(jnp.int32, (16, BLK), 1)
    table = jnp.zeros((16, BLK), jnp.int32)
    for b in range(NBLK):
        route = dest[b] - me[0] + REACH
        slot = count[route]
        count[route] = slot + 1
        slots[b] = slot
        table = jnp.where(lane == b, slot, table)
        a_all[pl.ds(slot, STEN, stride=SLOTS), :] = weight[:, lanes(b)].astype(F32)
        a_all[pl.ds(STEN * SLOTS + slot, STEN, stride=SLOTS), :] = cell[:, lanes(b)].astype(F32)
        a_all[pl.ds(2 * STEN * SLOTS + slot, 1), :] = jnp.full((1, BLK), win[b] + 1, jnp.int32).astype(F32)
        b_all[slot] = jnp.concatenate([adj[f, :, lanes(b)].astype(F32) for f in range(4)], axis=0).astype(BF16)
    for r in range(ROUTE):
        a_home[r] = a_all[r * SLOTS : r * SLOTS + HOME, :].astype(BF16)
    b_home[...] = b_all[:HOME]
    loads = (
        (own, MATE, either(core, 1, -1)),
        (own, MATE_PLUS, either(core, 3, 1)),
        (own, MATE_MINUS, either(core, -1, -3)),
        (plus, 0, either(core, 2, 2)),
        (minus, 0, either(core, -2, -2)),
        (cross, 0, either(core, -3, 3)),
    )
    for parcel, at, base in loads:
        for r in range(ROUTE):
            parcel[at + r] = a_all[pl.ds(r * SLOTS + base, OFFCAP), :].astype(BF16)
        parcel[at + ROUTE : at + LOAD] = b_all[pl.ds(base, OFFCAP)]
    rest = []
    for i, coef, piece in halo_pieces(adj.at[0], helm):
        rest.append(coef - coef.astype(BF16).astype(F32))
        own[i] = piece
    for i in range(LOWS):
        own[HALO + i] = jnp.concatenate(rest[2 * i : 2 * i + 2], axis=0).astype(BF16)
    own[HALO + LOWS] = table.astype(F32).astype(BF16)
    own[RELAY_PLUS:] = jnp.zeros((2 * HALO, 16, BLK), BF16)


def relay_kernel(_, plus, minus, out, sems):
    finish(
        launch(
            [
                (plus, out.at[pl.ds(RELAY_PLUS, HALO)], sems.at[0]),
                (minus, out.at[pl.ds(RELAY_MINUS, HALO)], sems.at[1]),
            ]
        )
    )


def solve_kernel(
    me, slots, helm_in, own, plus, minus, mate, plus_in, minus_in, cross_in,
    local, totals, f_home, f_mate, f_plus, f_minus, cross,
    helm, halo, lows, rhs, coef, result, table, table_s, mine_all, mate_all, t_all, sems, table_sem,
):
    core = lax.rem(me[0], 2)
    tables = launch([(mate.at[pl.ds(HALO, LOWS + 1)], lows, sems.at[7])])
    forward = (
        (plus_in, f_plus.at[pl.ds(0, LOAD)]),
        (mate.at[pl.ds(MATE_PLUS, LOAD)], f_plus.at[pl.ds(LOAD, LOAD)]),
        (minus_in, f_minus.at[pl.ds(0, LOAD)]),
        (mate.at[pl.ds(MATE_MINUS, LOAD)], f_minus.at[pl.ds(LOAD, LOAD)]),
        (cross_in, cross.at[pl.ds(0, LOAD)]),
    )
    pairs = (
        (helm_in, helm),
        (plus, halo.at[core]),
        (mate.at[pl.ds(RELAY_PLUS, HALO)], halo.at[1 - core]),
        (own, halo.at[2 + core]),
        (mate.at[pl.ds(0, HALO)], halo.at[3 - core]),
        (minus, halo.at[4 + core]),
        (mate.at[pl.ds(RELAY_MINUS, HALO)], halo.at[5 - core]),
    )
    copies = launch([(a, b, sems.at[i]) for i, (a, b) in enumerate(pairs)])
    passed = launch([(a, b, sems.at[8 + i]) for i, (a, b) in enumerate(forward)])
    mine_all[...] = jnp.zeros_like(mine_all)
    mate_all[...] = jnp.zeros_like(mate_all)
    finish(tables)
    table[...] = lows[LOWS].astype(F32)[:1].astype(jnp.int32)
    tables = launch([(table, table_s, table_sem)])
    finish(copies)
    for band in range(6):
        for i in range(HALO):
            tile = halo[band, i].astype(F32)
            rhs[band, :, lanes(i)] = tile[:8]
            coef[band, :, lanes(i)] = tile[8:]
    for i in range(LOWS):
        tile = lows[i].astype(F32)
        coef[3 - core, :, lanes(2 * i)] += tile[:8]
        coef[3 - core, :, lanes(2 * i + 1)] += tile[8:]
    coef[2 + core] = jnp.concatenate([helm[:, :NLON], helm[:, NLON:]], axis=0)
    right = [rhs[band] for band in range(6)]
    factor = [coef[band] for band in range(6)]
    scale = [1.0 / (1.0 + 4.0 * c) for c in factor]
    solved = [r * s for r, s in zip(right, scale)]
    upper = lax.broadcasted_iota(jnp.int32, (8, NLON), 0) < 4
    for wanted in ((0, 1, 2, 3, 4, 5), (1, 2, 3, 4), (1, 2, 3, 4), (2, 3)):
        shifted = [c * s for c, s in zip(factor, solved)]
        turned = [pltpu.roll(p, 4, 0) for p in shifted]
        fresh = list(solved)
        for band in wanted:
            p = shifted[band]
            north = turned[max(band - 1, 0)]
            south = turned[min(band + 1, 5)]
            total = turned[band] + jnp.where(upper, north, south)
            total = total + pltpu.roll(p, 1, 1) + pltpu.roll(p, NLON - 1, 1)
            fresh[band] = (right[band] + total) * scale[band]
        solved = fresh
    result[0] = solved[2]
    result[1] = solved[3]
    mine = result[core]
    other = result[1 - core]
    finish(tables)
    for r in range(2):
        sums = mine[4 * r : 4 * r + 1]
        local[4 * r : 4 * r + 1, :] = sums
        for level in range(1, 4):
            sums = sums + mine[4 * r + level : 4 * r + level + 1]
            local[4 * r + level : 4 * r + level + 1, :] = sums
        for i in range(HALO):
            b = HALO * r + i
            t_all[b : b + 1, :] = sums[:, lanes(i)]
            mine_all[pl.ds(slots[b] * 4, 4), :] = mine[4 * r : 4 * r + 4, lanes(i)]
            mate_all[pl.ds(table_s[0, b] * 4, 4), :] = other[4 * r : 4 * r + 4, lanes(i)]
    totals_here = t_all[...].astype(BF16)
    for i in range(totals.shape[0]):
        totals[i] = totals_here

    def part(source, first, second):
        return source[pl.ds(either(core, first, second) * 4, OFFCAP * 4), :].astype(BF16)

    f_home[...] = mine_all[: HOME * 4].astype(BF16)
    f_mate[...] = part(mate_all, -1, 1)
    sent = (
        (f_plus, 2 * LOAD, part(mine_all, 2, 2)),
        (f_plus, 2 * LOAD + 4, part(mate_all, 1, 3)),
        (f_minus, 2 * LOAD, part(mine_all, -2, -2)),
        (f_minus, 2 * LOAD + 4, part(mate_all, -3, -1)),
        (cross, LOAD, part(mine_all, -3, 3)),
    )
    for parcel, at, piece in sent:
        for i in range(4):
            parcel[at + i] = piece[16 * i : 16 * i + 16]
    finish(passed)


def merge(load, cells, merged, count, base):
    w = [load(k) for k in range(STEN)]
    c = [load(STEN + k) for k in range(STEN)]
    total = list(w)
    for k in range(STEN):
        for m in range(k):
            same = c[k] == c[m]
            total[k] = total[k] + jnp.where(same, w[m], 0.0)
            total[m] = total[m] + jnp.where(same, w[k], 0.0)
    lost = jnp.zeros((8, BLK), F32)
    held = jnp.zeros((8, BLK), F32)
    for k in range(STEN):
        high = total[k].astype(BF16).astype(F32)
        low = total[k] - high
        cells[k, base : base + 8, :] = c[k]
        merged[k, base : base + 8, :] = high
        merged[k, count + base : count + base + 8, :] = low
        lost = lost + low * low
        held = held + w[k] * w[k]
    more = jnp.sum(lost, axis=1, keepdims=True) > REMAINDER * jnp.sum(held, axis=1, keepdims=True)
    mark = load(2 * STEN)
    mark = jnp.where(mark > 0.0, mark + jnp.where(more, 64.0, 0.0), 0.0)
    lane = lax.broadcasted_iota(jnp.int32, (8, BLK), 1)
    row = lax.broadcasted_iota(jnp.int32, (8, BLK), 0)
    return jnp.where(lane == row + base, mark, 0.0)


def merge_all(groups, cells, merged, count, meta):
    marks = jnp.zeros((8, BLK), F32)
    for i, group in enumerate(groups):
        rows = group()
        for half in (0, 8):
            marks = marks + merge(lambda r: rows[r][half : half + 8], cells, merged, count, 16 * i + half)
    meta[...] = jnp.sum(marks, axis=0, keepdims=True).astype(jnp.int32)


def enlist(meta_s, count, entry_slot, entry_win):
    def eight(i, n):
        for j in range(8):
            slot = i * 8 + j
            mark = meta_s[0, slot]
            window = (mark & 63) - 1
            entry_slot[n] = slot
            entry_win[n] = window
            n = n + (mark > 0).astype(jnp.int32)
            entry_slot[n] = slot + count
            entry_win[n] = window
            n = n + (mark >= 64).astype(jnp.int32)
        return n

    n = lax.fori_loop(0, count // 8, eight, jnp.int32(0))
    for j in range(PACK):
        entry_slot[n + j] = 0
        entry_win[n + j] = NWIN
    return n


def spread(parts, count, cells, merged, meta, meta_s, entry_slot, entry_win, values, firsts, total, meta_sem, ready):
    merge_all(parts, cells, merged, count, meta)
    finish(launch([(meta, meta_s, meta_sem)]))
    n = enlist(meta_s, count, entry_slot, entry_win)
    ready()
    iota = lax.broadcasted_iota(jnp.int32, (16, BLK), 0).astype(F32)
    first_rows = lax.broadcasted_iota(jnp.int32, (8, BLK), 0) < 4

    def multiply(at, mat):
        slot = lax.rem(entry_slot[at], count)
        tile = values[slot].astype(F32)
        head = jnp.where(first_rows, firsts[pl.ds(slot * 4, 8), :], tile[:8])
        left = jnp.concatenate([head, tile[8:]], axis=0).astype(BF16)
        return lax.dot_general(left, mat, (((1,), (1,)), ((), ())), preferred_element_type=F32)

    def build(at):
        entry = entry_slot[at]
        slot = lax.rem(entry, count)
        c = [jnp.broadcast_to(cells[k, pl.ds(slot, 1), :], (16, BLK)).astype(BF16) for k in range(STEN)]
        w = [jnp.broadcast_to(merged[k, pl.ds(entry, 1), :], (16, BLK)).astype(BF16) for k in range(STEN)]
        tiles = []
        for i in range(WIN // 16):
            here = (iota + 16.0 * i).astype(BF16)
            m = jnp.zeros((16, BLK), BF16)
            for k in range(STEN):
                m = jnp.where(c[k] == here, w[k], m)
            tiles.append(m)
        return jnp.concatenate(tiles, axis=0)

    def add(at, product):
        start = pl.multiple_of(entry_win[at] * WIN, WIN)
        total[:, pl.ds(start, WIN)] += product

    def step(group, carry):
        products = []
        for j in range(PACK):
            at = group * PACK + j
            products.append((at, multiply(at, build(at))))
        for at, product in products:
            add(at, product)
        return carry

    lax.fori_loop(0, (n + PACK - 1) // PACK, step, 0)


def spread_scratch(count):
    return [
        pltpu.VMEM((STEN, count, BLK), F32),
        pltpu.VMEM((STEN, 2 * count, BLK), F32),
        pltpu.VMEM((1, BLK), jnp.int32),
        pltpu.SMEM((1, BLK), jnp.int32),
        pltpu.SMEM((2 * count + PACK,), jnp.int32),
        pltpu.SMEM((2 * count + PACK,), jnp.int32),
        pltpu.VMEM((count, 16, BLK), BF16),
        pltpu.VMEM((count * 4 + 8, BLK), F32),
    ]


def arrival(copy, tiles):
    def rows():
        copy.wait()
        return [tiles[r].astype(F32) for r in range(ROUTE)]

    return rows


def near_kernel(
    mate, a_home, b_home, f_home, f_mate, total,
    a_in, cells, merged, meta, meta_s, entry_slot, entry_win, values, firsts, sems, meta_sem,
):
    routes = launch([(mate.at[pl.ds(MATE, ROUTE)], a_in, sems.at[0])])
    copies = launch([(mate.at[pl.ds(MATE + ROUTE, OFFCAP)], values.at[pl.ds(HOME, OFFCAP)], sems.at[1])])
    total[...] = jnp.zeros_like(total)
    values[:HOME] = b_home[...]
    firsts[: HOME * 4, :] = f_home[...].astype(F32)
    firsts[HOME * 4 : NEAR * 4, :] = f_mate[...].astype(F32)
    firsts[NEAR * 4 :, :] = jnp.zeros((8, BLK), F32)

    def own_rows(at):
        return lambda: [a_home[r, at : at + 16, :].astype(F32) for r in range(ROUTE)]

    parts = [own_rows(at) for at in range(0, HOME, 16)] + [arrival(routes[0], a_in)]
    spread(
        parts, NEAR, cells, merged, meta, meta_s, entry_slot, entry_win, values, firsts, total, meta_sem,
        lambda: finish(copies),
    )


def far_kernel(
    lev, geo_in, plus, minus, cross, begun, local, above,
    out, geo, total, a_in, cells, merged, meta, meta_s, entry_slot, entry_win, values, firsts, sems, meta_sem,
):
    parts = (
        (plus, 0, 2 * LOAD),
        (plus, LOAD, 2 * LOAD + 4),
        (minus, 0, 2 * LOAD),
        (minus, LOAD, 2 * LOAD + 4),
        (cross, 0, LOAD),
    )
    count = len(parts)
    routes = launch([(p.at[pl.ds(at, ROUTE)], a_in.at[i], sems.at[i]) for i, (p, at, _) in enumerate(parts)])
    pairs = [
        (p.at[pl.ds(at + ROUTE, OFFCAP)], values.at[pl.ds(OFFCAP * i, OFFCAP)]) for i, (p, at, _) in enumerate(parts)
    ]
    pairs += [(geo_in, geo)]
    copies = launch([(a, b, sems.at[count + i]) for i, (a, b) in enumerate(pairs)])
    total[...] = begun[...]
    for i, (p, _, at) in enumerate(parts):
        for j in range(4):
            row = OFFCAP * 4 * i + 16 * j
            firsts[row : row + 16, :] = p[at + j].astype(F32)
    firsts[FAR * 4 :, :] = jnp.zeros((8, BLK), F32)
    spread(
        [arrival(copy, a_in.at[i]) for i, copy in enumerate(routes)],
        FAR, cells, merged, meta, meta_s, entry_slot, entry_win, values, firsts, total, meta_sem,
        lambda: finish(copies),
    )

    sums = jnp.zeros((NBLK, BLK), F32)
    for peer in range(above.shape[0]):
        sums = sums + jnp.where(peer < lev[0], above[peer].astype(F32), 0.0)
    level = lax.broadcasted_iota(jnp.int32, (4, BLK), 0)
    factor = jnp.zeros((4, BLK), F32)
    for i in range(4):
        factor = jnp.where(level == i, geo[i], factor)
    for f in (0, 1, 3):
        out[f] = total[4 * f : 4 * f + 4, :CELLS]
    for b in range(NBLK):
        r = b // HALO
        term = factor * (local[4 * r : 4 * r + 4, lanes(b % HALO)] + sums[b : b + 1])
        out[2, :, lanes(b)] = total[8:12, lanes(b)] + term


def moved(parcel, by):
    peers = lax.axis_size("tile")
    return lax.ppermute(parcel, "tile", [(i, i + by) for i in range(peers) if 0 <= i + by < peers])


def swapped(parcel):
    return lax.ppermute(parcel, "tile", [(i, i ^ 1) for i in range(lax.axis_size("tile"))])


def crossed(parcel):
    peers = lax.axis_size("tile")
    pairs = [(i, i + (3 if i % 2 else -3)) for i in range(peers)]
    return lax.ppermute(parcel, "tile", [(i, j) for i, j in pairs if 0 <= j < peers])


def body(adj_in, helm_coef, geo_coef, dest_tile, src_window, src_cell, interp_w):
    me = lax.axis_index("tile").astype(jnp.int32)[None]
    lev = lax.axis_index("lev").astype(jnp.int32)[None]
    peers = lax.axis_size("lev")

    def parcel(entries):
        return ((entries, 16, BLK), BF16, vmem())

    def strip(blocks):
        return ((blocks * 4, BLK), BF16, vmem())

    halo = call(
        halo_kernel,
        [parcel(HALO)],
        [hbm()] * 2,
        [pltpu.VMEM(adj_in.shape[1:], BF16), pltpu.VMEM(helm_coef.shape, F32), pltpu.SemaphoreType.DMA((2,))],
        1,
        16,
    )(kept(adj_in), kept(helm_coef))[0]
    plus = moved(halo, 2)
    minus = moved(halo, -2)

    slots, a_home, b_home, own, same_plus, same_minus, cross = call(
        pack_kernel,
        [
            ((NBLK,), jnp.int32, smem()),
            ((ROUTE, HOME, BLK), BF16, vmem()),
            parcel(HOME),
            parcel(OWN),
            parcel(LOAD),
            parcel(LOAD),
            parcel(LOAD),
        ],
        [smem()] + [hbm()] * 6,
        [
            pltpu.SMEM((NBLK,), jnp.int32),
            pltpu.SMEM((NBLK,), jnp.int32),
            pltpu.VMEM(adj_in.shape, BF16),
            pltpu.VMEM(helm_coef.shape, F32),
            pltpu.VMEM(src_cell.shape, jnp.int32),
            pltpu.VMEM(interp_w.shape, BF16),
            pltpu.SMEM((2 * REACH + 1,), jnp.int32),
            pltpu.VMEM((ROUTE * SLOTS, BLK), F32),
            pltpu.VMEM((SLOTS, 16, BLK), BF16),
            pltpu.SemaphoreType.DMA((6,)),
        ],
        20,
        24,
    )(me, *map(kept, (dest_tile[:, 0], src_window, adj_in, helm_coef, src_cell, interp_w)))

    relayed = call(
        relay_kernel,
        [((OWN, 16, BLK), BF16, free())],
        [free()] * 3,
        [pltpu.SemaphoreType.DMA((2,))],
        1,
        16,
        {0: 0},
    )(own, plus, minus)[0]
    mate = swapped(relayed)

    local, totals, f_home, f_mate, f_plus, f_minus, cross = call(
        solve_kernel,
        [
            ((8, NLON), F32, vmem()),
            ((peers, NBLK, BLK), BF16, vmem()),
            strip(HOME),
            strip(OFFCAP),
            parcel(PAIR),
            parcel(PAIR),
            parcel(CROSS),
        ],
        [smem()] * 2 + [hbm()] + [free()] * 7,
        [
            pltpu.VMEM(helm_coef.shape, F32),
            pltpu.VMEM((6, HALO, 16, BLK), BF16),
            pltpu.VMEM((LOWS + 1, 16, BLK), BF16),
            pltpu.VMEM((6, 8, NLON), F32),
            pltpu.VMEM((6, 8, NLON), F32),
            pltpu.VMEM((2, 8, NLON), F32),
            pltpu.VMEM((1, BLK), jnp.int32),
            pltpu.SMEM((1, BLK), jnp.int32),
            pltpu.VMEM((SLOTS * 4, BLK), F32),
            pltpu.VMEM((SLOTS * 4, BLK), F32),
            pltpu.VMEM((NBLK, BLK), F32),
            pltpu.SemaphoreType.DMA((13,)),
            pltpu.SemaphoreType.DMA,
        ],
        2,
        24,
    )(me, slots, kept(helm_coef), halo, plus, minus, mate, same_plus, same_minus, cross)
    f_plus = moved(f_plus, 2)
    f_minus = moved(f_minus, -2)
    cross = crossed(cross)
    above = lax.all_to_all(totals, "lev", 0, 0)

    begun = call(
        near_kernel,
        [((16, CELLS + WIN), F32, vmem())],
        [free()] + [vmem()] * 4,
        [pltpu.VMEM((ROUTE, 16, BLK), BF16)]
        + spread_scratch(NEAR)
        + [pltpu.SemaphoreType.DMA((2,)), pltpu.SemaphoreType.DMA],
        8,
        16,
    )(mate, a_home, b_home, f_home, f_mate)[0]

    return call(
        far_kernel,
        [((4, 4, CELLS), F32, vmem())],
        [smem(), hbm()] + [vmem()] * 6,
        [
            pltpu.SMEM((4,), F32),
            pltpu.VMEM((16, CELLS + WIN), F32),
            pltpu.VMEM((5, ROUTE, 16, BLK), BF16),
        ]
        + spread_scratch(FAR)
        + [pltpu.SemaphoreType.DMA((11,)), pltpu.SemaphoreType.DMA],
        4,
        16,
    )(lev, kept(geo_coef), f_plus, f_minus, cross, begun, local, above)[0]


def solution(mesh):
    placed = (
        P(None, "lev", "tile"),
        P("lev", "tile"),
        P("lev"),
        P("tile", None),
        P("tile"),
        P(None, "tile"),
        P(None, "tile"),
    )
    return jax.shard_map(
        body, mesh=mesh, in_specs=placed, out_specs=P(None, "lev", "tile"), check_vma=False
    )
```

```python
import jax
import jax.numpy as jnp
from jax import lax
from jax.experimental import pallas as pl
from jax.experimental.pallas import tpu as pltpu
from jax.sharding import PartitionSpec as P

NLON = 4096
BLK = 128
WIN = 256
SWEEPS = 4
REACH = 3
HOME = 32
OFFCAP = 16

F32 = jnp.float32
BF16 = jnp.bfloat16
STEN = 12
NBLK = 64
CELLS = 8192
NWIN = CELLS // WIN
OFFSETS = (-3, -2, -1, 1, 2, 3)
SLOTS = HOME + OFFCAP * len(OFFSETS)
HALO = NLON // BLK
ROUTE = 2 * STEN + 1
LOAD = ROUTE + OFFCAP
LOWS = HALO // 2
MATE = HALO + LOWS + 1
MATE_PLUS = MATE + LOAD
MATE_MINUS = MATE_PLUS + LOAD
RELAY_PLUS = MATE_MINUS + LOAD
RELAY_MINUS = RELAY_PLUS + HALO
OWN = RELAY_MINUS + HALO
NEAR = HOME + OFFCAP
FAR = 4 * OFFCAP
CROSS = LOAD + 4
PAIR = 2 * LOAD + 8
PACK = 8
REMAINDER = 1e-6


def vmem():
    return pl.BlockSpec(memory_space=pltpu.VMEM)


def smem():
    return pl.BlockSpec(memory_space=pltpu.SMEM)


def free():
    return pl.BlockSpec(memory_space=pl.ANY)


def hbm():
    return pl.BlockSpec(memory_space=pltpu.HBM)


def kept(array):
    return pltpu.with_memory_space_constraint(array, pltpu.HBM)


def lanes(i):
    return slice(i * BLK, (i + 1) * BLK)


def base_of(by):
    return 0 if by == 0 else HOME + OFFCAP * OFFSETS.index(by)


def either(core, first, second):
    return pl.multiple_of(jnp.where(core == 0, base_of(first), base_of(second)), OFFCAP)


def launch(copies):
    copies = [pltpu.make_async_copy(*copy) for copy in copies]
    for copy in copies:
        copy.start()
    return copies


def finish(copies):
    for copy in copies:
        copy.wait()


def call(kernel, outs, ins, scratch, cost, limit, aliases=None):
    return pl.pallas_call(
        kernel,
        out_shape=[(out[3] if out[3:] else jax.ShapeDtypeStruct)(out[0], out[1]) for out in outs],
        out_specs=[out[2] for out in outs],
        in_specs=ins,
        scratch_shapes=scratch,
        input_output_aliases=aliases or {},
        compiler_params=pltpu.CompilerParams(vmem_limit_bytes=limit << 20),
        cost_estimate=pl.CostEstimate(flops=cost * 1000000, bytes_accessed=cost * 3000000, transcendentals=0),
    )


def halo_pieces(first, helm):
    for i in range(HALO):
        coef = jnp.concatenate([helm[:, lanes(i)], helm[:, lanes(HALO + i)]], axis=0)
        side = [first[:, lanes(i)].astype(F32), first[:, lanes(HALO + i)].astype(F32)]
        yield i, coef, jnp.concatenate(side + [coef], axis=0).astype(BF16)


def halo_kernel(adj_in, helm_in, out, first, helm, sems):
    finish(launch([(adj_in.at[0], first, sems.at[0]), (helm_in, helm, sems.at[1])]))
    for i, _, piece in halo_pieces(first, helm):
        out[i] = piece


def pack_kernel(
    me, dest_in, win_in, adj_in, helm_in, cell_in, weight_in,
    slots, a_home, b_home, own, plus, minus, cross,
    dest, win, adj, helm, cell, weight, count, a_all, b_all, sems,
):
    pairs = ((dest_in, dest), (win_in, win), (adj_in, adj), (helm_in, helm), (cell_in, cell), (weight_in, weight))
    copies = launch([(a, b, sems.at[i]) for i, (a, b) in enumerate(pairs)])
    core = lax.rem(me[0], 2)
    for by in range(-REACH, REACH + 1):
        count[by + REACH] = base_of(by)
    a_all[...] = jnp.zeros_like(a_all)
    b_all[...] = jnp.zeros_like(b_all)
    finish(copies)
    lane = lax.broadcasted_iota(jnp.int32, (16, BLK), 1)
    table = jnp.zeros((16, BLK), jnp.int32)
    for b in range(NBLK):
        route = dest[b] - me[0] + REACH
        slot = count[route]
        count[route] = slot + 1
        slots[b] = slot
        table = jnp.where(lane == b, slot, table)
        a_all[pl.ds(slot, STEN, stride=SLOTS), :] = weight[:, lanes(b)].astype(F32)
        a_all[pl.ds(STEN * SLOTS + slot, STEN, stride=SLOTS), :] = cell[:, lanes(b)].astype(F32)
        a_all[pl.ds(2 * STEN * SLOTS + slot, 1), :] = jnp.full((1, BLK), win[b] + 1, jnp.int32).astype(F32)
        b_all[slot] = jnp.concatenate([adj[f, :, lanes(b)].astype(F32) for f in range(4)], axis=0).astype(BF16)
    for r in range(ROUTE):
        a_home[r] = a_all[r * SLOTS : r * SLOTS + HOME, :].astype(BF16)
    b_home[...] = b_all[:HOME]
    loads = (
        (own, MATE, either(core, 1, -1)),
        (own, MATE_PLUS, either(core, 3, 1)),
        (own, MATE_MINUS, either(core, -1, -3)),
        (plus, 0, either(core, 2, 2)),
        (minus, 0, either(core, -2, -2)),
        (cross, 0, either(core, -3, 3)),
    )
    for parcel, at, base in loads:
        for r in range(ROUTE):
            parcel[at + r] = a_all[pl.ds(r * SLOTS + base, OFFCAP), :].astype(BF16)
        parcel[at + ROUTE : at + LOAD] = b_all[pl.ds(base, OFFCAP)]
    rest = []
    for i, coef, piece in halo_pieces(adj.at[0], helm):
        rest.append(coef - coef.astype(BF16).astype(F32))
        own[i] = piece
    for i in range(LOWS):
        own[HALO + i] = jnp.concatenate(rest[2 * i : 2 * i + 2], axis=0).astype(BF16)
    own[HALO + LOWS] = table.astype(F32).astype(BF16)
    own[RELAY_PLUS:] = jnp.zeros((2 * HALO, 16, BLK), BF16)


def relay_kernel(_, plus, minus, out, sems):
    finish(
        launch(
            [
                (plus, out.at[pl.ds(RELAY_PLUS, HALO)], sems.at[0]),
                (minus, out.at[pl.ds(RELAY_MINUS, HALO)], sems.at[1]),
            ]
        )
    )


def solve_kernel(
    me, slots, helm_in, own, plus, minus, mate, plus_in, minus_in, cross_in,
    local, totals, f_home, f_mate, f_plus, f_minus, cross,
    helm, halo, lows, rhs, coef, result, table, table_s, mine_all, mate_all, t_all, sems, table_sem,
):
    core = lax.rem(me[0], 2)
    tables = launch([(mate.at[pl.ds(HALO, LOWS + 1)], lows, sems.at[7])])
    forward = (
        (plus_in, f_plus.at[pl.ds(0, LOAD)]),
        (mate.at[pl.ds(MATE_PLUS, LOAD)], f_plus.at[pl.ds(LOAD, LOAD)]),
        (minus_in, f_minus.at[pl.ds(0, LOAD)]),
        (mate.at[pl.ds(MATE_MINUS, LOAD)], f_minus.at[pl.ds(LOAD, LOAD)]),
        (cross_in, cross.at[pl.ds(0, LOAD)]),
    )
    pairs = (
        (helm_in, helm),
        (plus, halo.at[core]),
        (mate.at[pl.ds(RELAY_PLUS, HALO)], halo.at[1 - core]),
        (own, halo.at[2 + core]),
        (mate.at[pl.ds(0, HALO)], halo.at[3 - core]),
        (minus, halo.at[4 + core]),
        (mate.at[pl.ds(RELAY_MINUS, HALO)], halo.at[5 - core]),
    )
    copies = launch([(a, b, sems.at[i]) for i, (a, b) in enumerate(pairs)])
    passed = launch([(a, b, sems.at[8 + i]) for i, (a, b) in enumerate(forward)])
    mine_all[...] = jnp.zeros_like(mine_all)
    mate_all[...] = jnp.zeros_like(mate_all)
    finish(tables)
    table[...] = lows[LOWS].astype(F32)[:1].astype(jnp.int32)
    tables = launch([(table, table_s, table_sem)])
    finish(copies)
    for band in range(6):
        for i in range(HALO):
            tile = halo[band, i].astype(F32)
            rhs[band, :, lanes(i)] = tile[:8]
            coef[band, :, lanes(i)] = tile[8:]
    for i in range(LOWS):
        tile = lows[i].astype(F32)
        coef[3 - core, :, lanes(2 * i)] += tile[:8]
        coef[3 - core, :, lanes(2 * i + 1)] += tile[8:]
    coef[2 + core] = jnp.concatenate([helm[:, :NLON], helm[:, NLON:]], axis=0)
    right = [rhs[band] for band in range(6)]
    factor = [coef[band] for band in range(6)]
    scale = [1.0 / (1.0 + 4.0 * c) for c in factor]
    solved = [r * s for r, s in zip(right, scale)]
    upper = lax.broadcasted_iota(jnp.int32, (8, NLON), 0) < 4
    for wanted in ((0, 1, 2, 3, 4, 5), (1, 2, 3, 4), (1, 2, 3, 4), (2, 3)):
        shifted = [c * s for c, s in zip(factor, solved)]
        turned = [pltpu.roll(p, 4, 0) for p in shifted]
        fresh = list(solved)
        for band in wanted:
            p = shifted[band]
            north = turned[max(band - 1, 0)]
            south = turned[min(band + 1, 5)]
            total = turned[band] + jnp.where(upper, north, south)
            total = total + pltpu.roll(p, 1, 1) + pltpu.roll(p, NLON - 1, 1)
            fresh[band] = (right[band] + total) * scale[band]
        solved = fresh
    result[0] = solved[2]
    result[1] = solved[3]
    mine = result[core]
    other = result[1 - core]
    finish(tables)
    for r in range(2):
        sums = mine[4 * r : 4 * r + 1]
        local[4 * r : 4 * r + 1, :] = sums
        for level in range(1, 4):
            sums = sums + mine[4 * r + level : 4 * r + level + 1]
            local[4 * r + level : 4 * r + level + 1, :] = sums
        for i in range(HALO):
            b = HALO * r + i
            t_all[b : b + 1, :] = sums[:, lanes(i)]
            mine_all[pl.ds(slots[b] * 4, 4), :] = mine[4 * r : 4 * r + 4, lanes(i)]
            mate_all[pl.ds(table_s[0, b] * 4, 4), :] = other[4 * r : 4 * r + 4, lanes(i)]
    totals_here = t_all[...].astype(BF16)
    for i in range(totals.shape[0]):
        totals[i] = totals_here

    def part(source, first, second):
        return source[pl.ds(either(core, first, second) * 4, OFFCAP * 4), :].astype(BF16)

    f_home[...] = mine_all[: HOME * 4].astype(BF16)
    f_mate[...] = part(mate_all, -1, 1)
    sent = (
        (f_plus, 2 * LOAD, part(mine_all, 2, 2)),
        (f_plus, 2 * LOAD + 4, part(mate_all, 1, 3)),
        (f_minus, 2 * LOAD, part(mine_all, -2, -2)),
        (f_minus, 2 * LOAD + 4, part(mate_all, -3, -1)),
        (cross, LOAD, part(mine_all, -3, 3)),
    )
    for parcel, at, piece in sent:
        for i in range(4):
            parcel[at + i] = piece[16 * i : 16 * i + 16]
    finish(passed)


def merge(load, cells, merged, count, base):
    w = [load(k) for k in range(STEN)]
    c = [load(STEN + k) for k in range(STEN)]
    total = list(w)
    for k in range(STEN):
        for m in range(k):
            same = c[k] == c[m]
            total[k] = total[k] + jnp.where(same, w[m], 0.0)
            total[m] = total[m] + jnp.where(same, w[k], 0.0)
    lost = jnp.zeros((8, BLK), F32)
    held = jnp.zeros((8, BLK), F32)
    for k in range(STEN):
        high = total[k].astype(BF16).astype(F32)
        low = total[k] - high
        cells[k, base : base + 8, :] = c[k]
        merged[k, base : base + 8, :] = high
        merged[k, count + base : count + base + 8, :] = low
        lost = lost + low * low
        held = held + w[k] * w[k]
    more = jnp.sum(lost, axis=1, keepdims=True) > REMAINDER * jnp.sum(held, axis=1, keepdims=True)
    mark = load(2 * STEN)
    mark = jnp.where(mark > 0.0, mark + jnp.where(more, 64.0, 0.0), 0.0)
    lane = lax.broadcasted_iota(jnp.int32, (8, BLK), 1)
    row = lax.broadcasted_iota(jnp.int32, (8, BLK), 0)
    return jnp.where(lane == row + base, mark, 0.0)


def merge_all(groups, cells, merged, count, meta):
    marks = jnp.zeros((8, BLK), F32)
    for i, group in enumerate(groups):
        rows = group()
        for half in (0, 8):
            marks = marks + merge(lambda r: rows[r][half : half + 8], cells, merged, count, 16 * i + half)
    meta[...] = jnp.sum(marks, axis=0, keepdims=True).astype(jnp.int32)


def enlist(meta_s, count, entry_slot, entry_win):
    def eight(i, n):
        for j in range(8):
            slot = i * 8 + j
            mark = meta_s[0, slot]
            window = (mark & 63) - 1
            entry_slot[n] = slot
            entry_win[n] = window
            n = n + (mark > 0).astype(jnp.int32)
            entry_slot[n] = slot + count
            entry_win[n] = window
            n = n + (mark >= 64).astype(jnp.int32)
        return n

    n = lax.fori_loop(0, count // 8, eight, jnp.int32(0))
    for j in range(PACK):
        entry_slot[n + j] = 0
        entry_win[n + j] = NWIN
    return n


def spread(parts, count, cells, merged, meta, meta_s, entry_slot, entry_win, values, firsts, total, meta_sem, ready):
    merge_all(parts, cells, merged, count, meta)
    finish(launch([(meta, meta_s, meta_sem)]))
    n = enlist(meta_s, count, entry_slot, entry_win)
    ready()
    iota = lax.broadcasted_iota(jnp.int32, (16, BLK), 0).astype(F32)
    first_rows = lax.broadcasted_iota(jnp.int32, (8, BLK), 0) < 4

    def multiply(at, mat):
        slot = lax.rem(entry_slot[at], count)
        tile = values[slot].astype(F32)
        head = jnp.where(first_rows, firsts[pl.ds(slot * 4, 8), :], tile[:8])
        left = jnp.concatenate([head, tile[8:]], axis=0).astype(BF16)
        return lax.dot_general(left, mat, (((1,), (1,)), ((), ())), preferred_element_type=F32)

    def build(at):
        entry = entry_slot[at]
        slot = lax.rem(entry, count)
        c = [jnp.broadcast_to(cells[k, pl.ds(slot, 1), :], (16, BLK)).astype(BF16) for k in range(STEN)]
        w = [jnp.broadcast_to(merged[k, pl.ds(entry, 1), :], (16, BLK)).astype(BF16) for k in range(STEN)]
        tiles = []
        for i in range(WIN // 16):
            here = (iota + 16.0 * i).astype(BF16)
            m = jnp.zeros((16, BLK), BF16)
            for k in range(STEN):
                m = jnp.where(c[k] == here, w[k], m)
            tiles.append(m)
        return jnp.concatenate(tiles, axis=0)

    def add(at, product):
        start = pl.multiple_of(entry_win[at] * WIN, WIN)
        total[:, pl.ds(start, WIN)] += product

    def step(group, carry):
        products = []
        for j in range(PACK):
            at = group * PACK + j
            products.append((at, multiply(at, build(at))))
        for at, product in products:
            add(at, product)
        return carry

    lax.fori_loop(0, (n + PACK - 1) // PACK, step, 0)


def spread_scratch(count):
    return [
        pltpu.VMEM((STEN, count, BLK), F32),
        pltpu.VMEM((STEN, 2 * count, BLK), F32),
        pltpu.VMEM((1, BLK), jnp.int32),
        pltpu.SMEM((1, BLK), jnp.int32),
        pltpu.SMEM((2 * count + PACK,), jnp.int32),
        pltpu.SMEM((2 * count + PACK,), jnp.int32),
        pltpu.VMEM((count, 16, BLK), BF16),
        pltpu.VMEM((count * 4 + 8, BLK), F32),
    ]


def arrival(copy, tiles):
    def rows():
        copy.wait()
        return [tiles[r].astype(F32) for r in range(ROUTE)]

    return rows


def near_kernel(
    mate, a_home, b_home, f_home, f_mate, total,
    a_in, cells, merged, meta, meta_s, entry_slot, entry_win, values, firsts, sems, meta_sem,
):
    routes = launch([(mate.at[pl.ds(MATE, ROUTE)], a_in, sems.at[0])])
    copies = launch([(mate.at[pl.ds(MATE + ROUTE, OFFCAP)], values.at[pl.ds(HOME, OFFCAP)], sems.at[1])])
    total[...] = jnp.zeros_like(total)
    values[:HOME] = b_home[...]
    firsts[: HOME * 4, :] = f_home[...].astype(F32)
    firsts[HOME * 4 : NEAR * 4, :] = f_mate[...].astype(F32)
    firsts[NEAR * 4 :, :] = jnp.zeros((8, BLK), F32)

    def own_rows(at):
        return lambda: [a_home[r, at : at + 16, :].astype(F32) for r in range(ROUTE)]

    parts = [own_rows(at) for at in range(0, HOME, 16)] + [arrival(routes[0], a_in)]
    spread(
        parts, NEAR, cells, merged, meta, meta_s, entry_slot, entry_win, values, firsts, total, meta_sem,
        lambda: finish(copies),
    )


def spread_parcels(parts, begun, total, a_in, scratch, sems, meta_sem):
    cells, merged, meta, meta_s, entry_slot, entry_win, values, firsts = scratch
    count = len(parts)
    routes = launch([(p.at[pl.ds(at, ROUTE)], a_in.at[i], sems.at[i]) for i, (p, at, _) in enumerate(parts)])
    pairs = [
        (p.at[pl.ds(at + ROUTE, OFFCAP)], values.at[pl.ds(OFFCAP * i, OFFCAP)]) for i, (p, at, _) in enumerate(parts)
    ]
    copies = launch([(a, b, sems.at[count + i]) for i, (a, b) in enumerate(pairs)])
    total[...] = begun[...]
    for i, (p, _, at) in enumerate(parts):
        for j in range(4):
            row = OFFCAP * 4 * i + 16 * j
            firsts[row : row + 16, :] = p[at + j].astype(F32)
    firsts[OFFCAP * 4 * count :, :] = jnp.zeros((8, BLK), F32)
    spread(
        [arrival(copy, a_in.at[i]) for i, copy in enumerate(routes)],
        OFFCAP * count, cells, merged, meta, meta_s, entry_slot, entry_win, values, firsts, total, meta_sem,
        lambda: finish(copies),
    )


def far_kernel(plus, minus, begun, total, a_in, *rest):
    parts = (
        (plus, 0, 2 * LOAD),
        (plus, LOAD, 2 * LOAD + 4),
        (minus, 0, 2 * LOAD),
        (minus, LOAD, 2 * LOAD + 4),
    )
    spread_parcels(parts, begun, total, a_in, rest[:-2], *rest[-2:])


def last_kernel(lev, geo_in, cross, begun, local, above, out, geo, geo_sem, total, a_in, *rest):
    geos = launch([(geo_in, geo, geo_sem)])
    spread_parcels([(cross, 0, LOAD)], begun, total, a_in, rest[:-2], *rest[-2:])
    finish(geos)

    sums = jnp.zeros((NBLK, BLK), F32)
    for peer in range(above.shape[0]):
        sums = sums + jnp.where(peer < lev[0], above[peer].astype(F32), 0.0)
    level = lax.broadcasted_iota(jnp.int32, (4, BLK), 0)
    factor = jnp.zeros((4, BLK), F32)
    for i in range(4):
        factor = jnp.where(level == i, geo[i], factor)
    for f in (0, 1, 3):
        out[f] = total[4 * f : 4 * f + 4, :CELLS]
    for b in range(NBLK):
        r = b // HALO
        term = factor * (local[4 * r : 4 * r + 4, lanes(b % HALO)] + sums[b : b + 1])
        out[2, :, lanes(b)] = total[8:12, lanes(b)] + term


def moved(parcel, by):
    peers = lax.axis_size("tile")
    return lax.ppermute(parcel, "tile", [(i, i + by) for i in range(peers) if 0 <= i + by < peers])


def swapped(parcel):
    return lax.ppermute(parcel, "tile", [(i, i ^ 1) for i in range(lax.axis_size("tile"))])


def crossed(parcel):
    peers = lax.axis_size("tile")
    pairs = [(i, i + (3 if i % 2 else -3)) for i in range(peers)]
    return lax.ppermute(parcel, "tile", [(i, j) for i, j in pairs if 0 <= j < peers])


def body(adj_in, helm_coef, geo_coef, dest_tile, src_window, src_cell, interp_w):
    me = lax.axis_index("tile").astype(jnp.int32)[None]
    lev = lax.axis_index("lev").astype(jnp.int32)[None]
    peers = lax.axis_size("lev")

    def parcel(entries):
        return ((entries, 16, BLK), BF16, vmem())

    def strip(blocks):
        return ((blocks * 4, BLK), BF16, vmem())

    halo = call(
        halo_kernel,
        [parcel(HALO)],
        [hbm()] * 2,
        [pltpu.VMEM(adj_in.shape[1:], BF16), pltpu.VMEM(helm_coef.shape, F32), pltpu.SemaphoreType.DMA((2,))],
        1,
        16,
    )(kept(adj_in), kept(helm_coef))[0]
    plus = moved(halo, 2)
    minus = moved(halo, -2)

    slots, a_home, b_home, own, same_plus, same_minus, cross = call(
        pack_kernel,
        [
            ((NBLK,), jnp.int32, smem()),
            ((ROUTE, HOME, BLK), BF16, vmem()),
            parcel(HOME),
            parcel(OWN),
            parcel(LOAD),
            parcel(LOAD),
            parcel(LOAD),
        ],
        [smem()] + [hbm()] * 6,
        [
            pltpu.SMEM((NBLK,), jnp.int32),
            pltpu.SMEM((NBLK,), jnp.int32),
            pltpu.VMEM(adj_in.shape, BF16),
            pltpu.VMEM(helm_coef.shape, F32),
            pltpu.VMEM(src_cell.shape, jnp.int32),
            pltpu.VMEM(interp_w.shape, BF16),
            pltpu.SMEM((2 * REACH + 1,), jnp.int32),
            pltpu.VMEM((ROUTE * SLOTS, BLK), F32),
            pltpu.VMEM((SLOTS, 16, BLK), BF16),
            pltpu.SemaphoreType.DMA((6,)),
        ],
        20,
        24,
    )(me, *map(kept, (dest_tile[:, 0], src_window, adj_in, helm_coef, src_cell, interp_w)))

    relayed = call(
        relay_kernel,
        [((OWN, 16, BLK), BF16, free())],
        [free()] * 3,
        [pltpu.SemaphoreType.DMA((2,))],
        1,
        16,
        {0: 0},
    )(own, plus, minus)[0]
    mate = swapped(relayed)

    local, totals, f_home, f_mate, f_plus, f_minus, cross = call(
        solve_kernel,
        [
            ((8, NLON), F32, vmem()),
            ((peers, NBLK, BLK), BF16, vmem()),
            strip(HOME),
            strip(OFFCAP),
            parcel(PAIR),
            parcel(PAIR),
            parcel(CROSS),
        ],
        [smem()] * 2 + [hbm()] + [free()] * 7,
        [
            pltpu.VMEM(helm_coef.shape, F32),
            pltpu.VMEM((6, HALO, 16, BLK), BF16),
            pltpu.VMEM((LOWS + 1, 16, BLK), BF16),
            pltpu.VMEM((6, 8, NLON), F32),
            pltpu.VMEM((6, 8, NLON), F32),
            pltpu.VMEM((2, 8, NLON), F32),
            pltpu.VMEM((1, BLK), jnp.int32),
            pltpu.SMEM((1, BLK), jnp.int32),
            pltpu.VMEM((SLOTS * 4, BLK), F32),
            pltpu.VMEM((SLOTS * 4, BLK), F32),
            pltpu.VMEM((NBLK, BLK), F32),
            pltpu.SemaphoreType.DMA((13,)),
            pltpu.SemaphoreType.DMA,
        ],
        2,
        24,
    )(me, slots, kept(helm_coef), halo, plus, minus, mate, same_plus, same_minus, cross)
    f_plus = moved(f_plus, 2)
    f_minus = moved(f_minus, -2)
    cross = crossed(cross)
    above = lax.all_to_all(totals, "lev", 0, 0)

    begun = call(
        near_kernel,
        [((16, CELLS + WIN), F32, vmem())],
        [free()] + [vmem()] * 4,
        [pltpu.VMEM((ROUTE, 16, BLK), BF16)]
        + spread_scratch(NEAR)
        + [pltpu.SemaphoreType.DMA((2,)), pltpu.SemaphoreType.DMA],
        8,
        16,
    )(mate, a_home, b_home, f_home, f_mate)[0]

    begun = call(
        far_kernel,
        [((16, CELLS + WIN), F32, vmem())],
        [vmem()] * 3,
        [pltpu.VMEM((4, ROUTE, 16, BLK), BF16)]
        + spread_scratch(FAR)
        + [pltpu.SemaphoreType.DMA((8,)), pltpu.SemaphoreType.DMA],
        8,
        16,
    )(f_plus, f_minus, begun)[0]

    return call(
        last_kernel,
        [((4, 4, CELLS), F32, vmem())],
        [smem(), hbm()] + [vmem()] * 4,
        [
            pltpu.SMEM((4,), F32),
            pltpu.SemaphoreType.DMA,
            pltpu.VMEM((16, CELLS + WIN), F32),
            pltpu.VMEM((1, ROUTE, 16, BLK), BF16),
        ]
        + spread_scratch(OFFCAP)
        + [pltpu.SemaphoreType.DMA((2,)), pltpu.SemaphoreType.DMA],
        4,
        16,
    )(lev, kept(geo_coef), cross, begun, local, above)[0]


def solution(mesh):
    placed = (
        P(None, "lev", "tile"),
        P("lev", "tile"),
        P("lev"),
        P("tile", None),
        P("tile"),
        P(None, "tile"),
        P(None, "tile"),
    )
    return jax.shard_map(
        body, mesh=mesh, in_specs=placed, out_specs=P(None, "lev", "tile"), check_vma=False
    )
```
